128 devices in a mesh: row: 16 (over x, y), col: 8 (over z, core).
Axes of the slice: x: 4, y: 4, z: 4, core: 2. Of those that a mesh axis runs over, the one named last changes fastest.
Arguments:
- object_slab: float32 [4, 4096, 4096], P(None, 'row', 'col'), may hold values from -6 to 6
- probe_wave: float32 [2, 256, 256], replicated, may hold values from -6 to 6
- scan_offsets: int32 [1024, 2], P(('row', 'col')), may hold values from 0 to 3840, as said below
- live_counts: int32 [128], P(('row', 'col')), may hold values from 1 to 8, as said below
- amplitudes: float32 [1024, 256, 256], P(('row', 'col')), may hold values from 0 to 3
Outputs:
- object_grad: float32 [4, 4096, 4096], P(None, 'row', 'col')
- probe_grad: float32 [2, 256, 256], replicated
The draws below stay inside these ranges and needn't reach their ends.
Inputs may be any that keep to these rules, and one draw needn't show every extreme that they name: `scan_offsets`: each slot's window lies inside the object, and its corner lies in the object tile of the device that holds the slot. Slot 0 of the first device has corner (0, 0), slot 0 of the last device has corner (3840, 3840). `live_counts`: every device has at least one live slot and some device has all 8 slots live.
All inputs are finite; a program needn't handle non-finite values.
Results may differ from the reference program's by a relative error of at most 0.0003.
Values sent between devices are 32-bit elements; how exact they have to be, the bound alone decides.
No kernel may reach another device: no remote copies, remote signals or barrier semaphores. Data moves between devices by JAX's collectives and lax.ppermute only.
A program may use at most 128 MiB of HBM per device.

```python
import math
import jax
import jax.numpy as jnp
from jax import lax

W = 256
TR = 256
TC = 512
POS_CAP = 8
NR = 4096
NC = 4096
POSITIONS = 1024
N_ROW = 16
N_COL = 8


def draw_scan_offsets(key, part):
    key = jax.random.fold_in(key, 11)
    key_rows, key_cols = jax.random.split(key)
    device = jnp.arange(POSITIONS) // POS_CAP
    tile_row = device // N_COL
    tile_col = device % N_COL
    row_span = jnp.where(tile_row == N_ROW - 1, TR - W + 1, TR)
    col_span = jnp.where(tile_col == N_COL - 1, TC - W + 1, TC)
    local_rows = jax.random.randint(key_rows, (POSITIONS,), 0, row_span)
    local_cols = jax.random.randint(key_cols, (POSITIONS,), 0, col_span)
    slot_index = jnp.arange(POSITIONS)
    local_rows = jnp.where(slot_index == 0, 0, local_rows)
    local_cols = jnp.where(slot_index == 0, 0, local_cols)
    last_first = (N_ROW * N_COL - 1) * POS_CAP
    local_rows = jnp.where(slot_index == last_first, TR - W, local_rows)
    local_cols = jnp.where(slot_index == last_first, TC - W, local_cols)
    rows_global = tile_row * TR + local_rows
    cols_global = tile_col * TC + local_cols
    return jnp.stack([rows_global, cols_global], axis=1).astype(jnp.int32)


def draw_live_counts(key, part):
    key = jax.random.fold_in(key, 12)
    key_base, key_band = jax.random.split(key)
    device = jnp.arange(N_ROW * N_COL)
    tile_col = device % N_COL
    base_counts = jax.random.randint(key_base, (N_ROW * N_COL,), 1, POS_CAP // 2 + 1)
    band_start = jax.random.randint(key_band, (), 0, N_COL)
    in_band = (tile_col - band_start) % N_COL < max(N_COL // 4, 1)
    return jnp.where(in_band, POS_CAP, base_counts).astype(jnp.int32)


def shard_levels(rng, extent, cuts, least, high):
    def one(dim, blocks):
        draws = jax.random.uniform(jax.random.fold_in(jax.random.fold_in(rng, 6), dim), (blocks,), jnp.float32, least / len(cuts), high / len(cuts))
        return jnp.repeat(jnp.exp(draws), extent[dim] // blocks).reshape((-1,) + (1,) * (len(extent) - dim - 1))

    level = one(*cuts[0])
    for cut in cuts[1:]:
        level = level * one(*cut)
    return level


def bell_draw(key, extent, scale, reach, shards=(), kind=jnp.bfloat16):
    level = shard_levels(key, extent, shards, -0.22, 0.18) if shards else 1.0
    entries = jax.random.normal(key, extent, jnp.float32) * scale * level
    return jnp.minimum(jnp.maximum(entries, -reach), reach).astype(kind)


def setup_inputs(seed: int = 0) -> dict:
    keys = jax.random.split(jax.random.key(seed), 6)
    object_slab = bell_draw(keys[0], (4, NR, NC), 0.7, 6.0, ((1, 16), (2, 8)), jnp.float32)
    probe_wave = bell_draw(keys[1], (2, W, W), 1.0, 6.0, (), jnp.float32)
    scan_offsets = draw_scan_offsets(jax.random.fold_in(keys[5], 71), 0)
    live_counts = draw_live_counts(jax.random.fold_in(keys[5], 71), 0)
    amplitudes = jnp.clip(3.0 * jax.random.uniform(keys[4], (POSITIONS, W, W), jnp.float32) ** shard_levels(keys[4], (POSITIONS, W, W), ((0, 128),), -0.2, 0.2), 0.0, 3.0)
    return dict(object_slab=object_slab, probe_wave=probe_wave, scan_offsets=scan_offsets, live_counts=live_counts, amplitudes=amplitudes)


def fresnel_phase(width):
    index_range = jnp.arange(width)
    freqs = jnp.where(index_range < width // 2, index_range, index_range - width).astype(jnp.float32) / width
    square_sum = freqs[:, None] ** 2 + freqs[None, :] ** 2
    return -math.pi * (width / 4.0) * square_sum

def position_grads(window, measured, probe_wave, transfer):
    object_one = window[0] + 1j * window[1]
    object_two = window[2] + 1j * window[3]
    probe_field = probe_wave[0] + 1j * probe_wave[1]
    psi_one = probe_field * object_one
    propagated = jnp.fft.ifft2(transfer * jnp.fft.fft2(psi_one, norm='ortho'), norm='ortho')
    psi_two = propagated * object_two
    far_field = jnp.fft.fft2(psi_two, norm='ortho')
    intensity = jnp.real(far_field) ** 2 + jnp.imag(far_field) ** 2
    factor = 1.0 - measured / jnp.sqrt(intensity + 1.0)
    residue_wave = factor * far_field
    back_far = jnp.fft.ifft2(residue_wave, norm='ortho')
    grad_two = jnp.conj(propagated) * back_far
    back_prop = jnp.conj(object_two) * back_far
    back_one = jnp.fft.ifft2(jnp.conj(transfer) * jnp.fft.fft2(back_prop, norm='ortho'), norm='ortho')
    grad_one = jnp.conj(probe_field) * back_one
    grad_probe = jnp.conj(object_one) * back_one
    object_part = jnp.stack([jnp.real(grad_one), jnp.imag(grad_one), jnp.real(grad_two), jnp.imag(grad_two)])
    probe_part = jnp.stack([jnp.real(grad_probe), jnp.imag(grad_probe)])
    return (object_part, probe_part)

def reference(object_slab, probe_wave, scan_offsets, live_counts, amplitudes):
    phases = fresnel_phase(W)
    transfer = jnp.cos(phases) + 1j * jnp.sin(phases)
    zero_index = jnp.zeros((), jnp.int32)

    def visit(carry, index):
        grad_full, probe_acc = carry
        live = index % POS_CAP < live_counts[index // POS_CAP]
        weight = live.astype(object_slab.dtype)
        row_at = scan_offsets[index, 0].astype(jnp.int32)
        col_at = scan_offsets[index, 1].astype(jnp.int32)
        window = lax.dynamic_slice(object_slab, (zero_index, row_at, col_at), (4, W, W))
        object_part, probe_part = position_grads(window, amplitudes[index], probe_wave, transfer)
        current = lax.dynamic_slice(grad_full, (zero_index, row_at, col_at), (4, W, W))
        grad_full = lax.dynamic_update_slice(grad_full, current + weight * object_part.astype(object_slab.dtype), (zero_index, row_at, col_at))
        probe_acc = probe_acc + weight * probe_part.astype(object_slab.dtype)
        return ((grad_full, probe_acc), None)
    init = (jnp.zeros_like(object_slab), jnp.zeros_like(probe_wave))
    (grad_full, probe_acc), _ = lax.scan(visit, init, jnp.arange(POSITIONS, dtype=jnp.int32))
    return (grad_full, probe_acc)
```

```python
import math
import numpy as np
import ml_dtypes
import jax
import jax.numpy as jnp
from jax import lax
from jax.experimental import pallas as pl
from jax.experimental.pallas import tpu as pltpu
from jax.sharding import PartitionSpec as P

W = 256
F32 = jnp.float32
BF16 = jnp.bfloat16


def split_host(table):
    high = table.astype(np.float32).astype(ml_dtypes.bfloat16)
    low = (table - high.astype(np.float64)).astype(np.float32).astype(ml_dtypes.bfloat16)
    return high, low


def tables(width):
    index = np.arange(width)
    angles = 2.0 * np.pi / width * (index[:, None] * index[None, :] % width)
    dft = (np.cos(angles) - 1j * np.sin(angles)) / math.sqrt(width)
    freqs = np.where(index < width // 2, index, index - width) / width
    fresnel = np.exp(-1j * np.pi * (width / 4.0) * freqs**2)
    hop = np.conj(dft) @ (fresnel[:, None] * dft)
    out = []
    for table in (dft, hop):
        for part in (table.real, table.imag, -table.imag):
            out.extend(split_host(part))
    return np.stack(out)


def split(x):
    high = x.astype(BF16)
    return high, (x - high.astype(F32)).astype(BF16)


def kernel(meta, own, right, down0, down1, corner, amp, probe, tab,
           gown, gright, gdown0, gdown1, gcorner, gprobe,
           ext, gext, probe2, win, hs, zs, prop, xs, sems):
    width = W
    copies = [
        pltpu.make_async_copy(own, ext.at[0, :, :, pl.ds(0, 512)], sems.at[0]),
        pltpu.make_async_copy(right, ext.at[0, :, :, pl.ds(512, 256)], sems.at[1]),
        pltpu.make_async_copy(down0, ext.at[1, :, :, pl.ds(0, 256)], sems.at[2]),
        pltpu.make_async_copy(down1, ext.at[1, :, :, pl.ds(256, 256)], sems.at[3]),
        pltpu.make_async_copy(corner, ext.at[1, :, :, pl.ds(512, 256)], sems.at[4]),
    ]
    for copy in copies:
        copy.start()
    gext[...] = jnp.zeros_like(gext)
    gprobe[...] = jnp.zeros_like(gprobe)
    for copy in copies:
        copy.wait()
    live = meta[0]

    def block(table, part, level):
        return tab[table * 6 + part * 2 + level]

    def right_mul(x_ref, table, sign, out_ref):
        rh, rl = x_ref[0, :, :width], x_ref[1, :, :width]
        ih, il = x_ref[0, :, width:], x_ref[1, :, width:]
        lhs = jnp.concatenate([rh, ih, rl, il, rh, ih], axis=1)
        im, nim = (1, 2) if sign > 0 else (2, 1)
        def col(a, b):
            return jnp.concatenate([block(table, a, 0), block(table, b, 0), block(table, a, 0), block(table, b, 0), block(table, a, 1), block(table, b, 1)], axis=0)
        out_ref[:, :width] = jnp.dot(lhs, col(0, nim), preferred_element_type=F32)
        out_ref[:, width:] = jnp.dot(lhs, col(im, 0), preferred_element_type=F32)

    def left_mul(x_ref, table, sign, out_ref):
        rh, rl = x_ref[0, :, :width], x_ref[1, :, :width]
        ih, il = x_ref[0, :, width:], x_ref[1, :, width:]
        rhs = jnp.concatenate([rh, ih, rl, il, rh, ih], axis=0)
        im, nim = (1, 2) if sign > 0 else (2, 1)
        def row(a, b):
            return jnp.concatenate([block(table, a, 0), block(table, b, 0), block(table, a, 0), block(table, b, 0), block(table, a, 1), block(table, b, 1)], axis=1)
        out_ref[:, :width] = jnp.dot(row(0, nim), rhs, preferred_element_type=F32)
        out_ref[:, width:] = jnp.dot(row(im, 0), rhs, preferred_element_type=F32)

    R = 32
    n_chunks = width // R

    def chunks(body):
        def step(i, _):
            body(pl.multiple_of(i * R, R))
            return 0
        lax.fori_loop(0, n_chunks, step, 0)

    def put_split(at, re, im):
        h, l = split(re)
        xs[0, pl.ds(at, R), :width] = h
        xs[1, pl.ds(at, R), :width] = l
        h, l = split(im)
        xs[0, pl.ds(at, R), width:] = h
        xs[1, pl.ds(at, R), width:] = l

    def resplit():
        def body(at):
            put_split(at, hs[pl.ds(at, R), :width], hs[pl.ds(at, R), width:])
        chunks(body)

    def visit(s, _):
        r = meta[1 + s]
        c = meta[9 + s]
        cb = c // width
        cc = c - cb * width
        c0 = pl.multiple_of(cb * width, width)
        c1 = pl.multiple_of(cb * width + width, width)
        probe2[0] = pltpu.roll(pltpu.roll(probe[0], cc, 1), r, 0)
        probe2[1] = pltpu.roll(pltpu.roll(probe[1], cc, 1), r, 0)
        cmask = lax.broadcasted_iota(jnp.int32, (R, width), 1) >= cc

        def load(at):
            rmask = lax.broadcasted_iota(jnp.int32, (R, width), 0) + at >= r
            planes = []
            for p in range(4):
                top = jnp.where(cmask, ext[0, p, pl.ds(at, R), pl.ds(c0, width)], ext[0, p, pl.ds(at, R), pl.ds(c1, width)])
                bot = jnp.where(cmask, ext[1, p, pl.ds(at, R), pl.ds(c0, width)], ext[1, p, pl.ds(at, R), pl.ds(c1, width)])
                planes.append(jnp.where(rmask, top, bot))
            for p in range(4):
                win[p, pl.ds(at, R), :] = planes[p]
            pr, pi = probe2[0, pl.ds(at, R), :], probe2[1, pl.ds(at, R), :]
            put_split(at, pr * planes[0] - pi * planes[1], pr * planes[1] + pi * planes[0])
        chunks(load)
        right_mul(xs, 1, 1, hs)
        resplit()
        left_mul(xs, 1, 1, prop)
        def times_two(at):
            pr, pi = prop[pl.ds(at, R), :width], prop[pl.ds(at, R), width:]
            o, q = win[2, pl.ds(at, R), :], win[3, pl.ds(at, R), :]
            put_split(at, pr * o - pi * q, pr * q + pi * o)
        chunks(times_two)
        left_mul(xs, 0, 1, hs)
        resplit()
        right_mul(xs, 0, 1, zs)
        def chi(at):
            fr, fi = zs[pl.ds(at, R), :width], zs[pl.ds(at, R), width:]
            a = amp[s, pl.ds(at, R), :]
            factor = 1.0 - a * lax.rsqrt(fr * fr + fi * fi + 1.0)
            put_split(at, factor * fr, factor * fi)
        chunks(chi)
        right_mul(xs, 0, -1, hs)
        resplit()
        left_mul(xs, 0, -1, zs)
        def back(at):
            gr, gi = zs[pl.ds(at, R), :width], zs[pl.ds(at, R), width:]
            o, q = win[2, pl.ds(at, R), :], win[3, pl.ds(at, R), :]
            put_split(at, o * gr + q * gi, o * gi - q * gr)
            pr, pi = prop[pl.ds(at, R), :width], prop[pl.ds(at, R), width:]
            win[2, pl.ds(at, R), :] = pr * gr + pi * gi
            win[3, pl.ds(at, R), :] = pr * gi - pi * gr
        chunks(back)
        left_mul(xs, 1, -1, hs)
        resplit()
        right_mul(xs, 1, -1, zs)
        def finish(at):
            gr, gi = zs[pl.ds(at, R), :width], zs[pl.ds(at, R), width:]
            o, q = win[0, pl.ds(at, R), :], win[1, pl.ds(at, R), :]
            pr, pi = probe2[0, pl.ds(at, R), :], probe2[1, pl.ds(at, R), :]
            probe2[0, pl.ds(at, R), :] = o * gr + q * gi
            probe2[1, pl.ds(at, R), :] = o * gi - q * gr
            rmask = lax.broadcasted_iota(jnp.int32, (R, width), 0) + at >= r
            parts = [pr * gr + pi * gi, pr * gi - pi * gr, win[2, pl.ds(at, R), :], win[3, pl.ds(at, R), :]]
            zero = jnp.zeros((R, width), F32)
            for p in range(4):
                top = jnp.where(rmask, parts[p], zero)
                bot = jnp.where(rmask, zero, parts[p])
                for row, v in ((0, top), (1, bot)):
                    gext[row, p, pl.ds(at, R), pl.ds(c0, width)] += jnp.where(cmask, v, zero)
                    gext[row, p, pl.ds(at, R), pl.ds(c1, width)] += jnp.where(cmask, zero, v)
        chunks(finish)
        for p in range(2):
            gprobe[p] += pltpu.roll(pltpu.roll(probe2[p], width - cc, 1), width - r, 0)
        return 0

    lax.fori_loop(0, live, visit, 0)
    outs = [
        pltpu.make_async_copy(gext.at[0, :, :, pl.ds(0, 512)], gown, sems.at[0]),
        pltpu.make_async_copy(gext.at[0, :, :, pl.ds(512, 256)], gright, sems.at[1]),
        pltpu.make_async_copy(gext.at[1, :, :, pl.ds(0, 256)], gdown0, sems.at[2]),
        pltpu.make_async_copy(gext.at[1, :, :, pl.ds(256, 256)], gdown1, sems.at[3]),
        pltpu.make_async_copy(gext.at[1, :, :, pl.ds(512, 256)], gcorner, sems.at[4]),
    ]
    for copy in outs:
        copy.start()
    for copy in outs:
        copy.wait()


def slots_call(meta, own, right, down0, down1, corner, amp, probe, tab):
    any_spec = pl.BlockSpec(memory_space=pl.ANY)
    vmem = pl.BlockSpec(memory_space=pltpu.VMEM)
    shape = lambda *s: jax.ShapeDtypeStruct(s, F32)
    return pl.pallas_call(
        kernel,
        in_specs=[pl.BlockSpec(memory_space=pltpu.SMEM)] + [any_spec] * 5 + [vmem] * 3,
        out_specs=[any_spec] * 5 + [vmem],
        out_shape=[shape(4, 256, 512)] + [shape(4, 256, 256)] * 4 + [shape(2, 256, 256)],
        scratch_shapes=[
            pltpu.VMEM((2, 4, 256, 768), F32),
            pltpu.VMEM((2, 4, 256, 768), F32),
            pltpu.VMEM((2, 256, 256), F32),
            pltpu.VMEM((4, 256, 256), F32),
            pltpu.VMEM((256, 512), F32),
            pltpu.VMEM((256, 512), F32),
            pltpu.VMEM((256, 512), F32),
            pltpu.VMEM((2, 256, 512), BF16),
            pltpu.SemaphoreType.DMA((5,)),
        ],
        compiler_params=pltpu.CompilerParams(vmem_limit_bytes=50 * 2**20),
        cost_estimate=pl.CostEstimate(flops=8 * 100 * 2**25, bytes_accessed=20 * 2**20, transcendentals=0),
    )(meta, own, right, down0, down1, corner, amp, probe, tab)


def shift(value, axis, steps):
    count = lax.axis_size(axis)
    first, last = (max(0, -steps), min(count, count - steps))
    return lax.ppermute(value, axis, [(source, source + steps) for source in range(first, last)])


def sum_all(value, axes):
    count = lax.axis_size(axes)
    shares = value.reshape(count, -1, value.shape[-1])
    mine = lax.all_to_all(shares, axes, 0, 0, tiled=True).sum(axis=0)
    spread = jnp.broadcast_to(mine[None], shares.shape)
    return lax.all_to_all(spread, axes, 0, 0, tiled=True).reshape(value.shape)


def body(object_slab, probe_wave, scan_offsets, live_counts, amplitudes):
    rows_tile, cols_tile = object_slab.shape[1:]
    local_rows = scan_offsets[:, 0] - lax.axis_index("row") * rows_tile
    local_cols = scan_offsets[:, 1] - lax.axis_index("col") * cols_tile
    meta = jnp.concatenate([live_counts, local_rows, local_cols])
    first_half = object_slab[:, :, :W]
    down0 = shift(first_half, "row", -1)
    right = shift(first_half, "col", -1)
    down1 = shift(object_slab[:, :, W:], "row", -1)
    corner = shift(down0, "col", -1)
    tab = jnp.asarray(tables(W))
    gown, gright, gdown0, gdown1, gcorner, gprobe = slots_call(
        meta, object_slab, right, down0, down1, corner, amplitudes, probe_wave, tab
    )
    corner_back = shift(gcorner, "col", 1)
    down1_back = shift(gdown1, "row", 1)
    right_back = shift(gright, "col", 1)
    down0_back = shift(gdown0 + corner_back, "row", 1)
    probe_grad = sum_all(gprobe, ("row", "col"))
    object_grad = gown + jnp.concatenate([right_back + down0_back, down1_back], axis=2)
    return object_grad, probe_grad


def solution(mesh):
    return jax.shard_map(
        body,
        mesh=mesh,
        in_specs=(
            P(None, "row", "col"),
            P(),
            P(("row", "col"), None),
            P(("row", "col")),
            P(("row", "col"), None, None),
        ),
        out_specs=(P(None, "row", "col"), P()),
        check_vma=False,
    )
```

```python
import math

import jax
import jax.numpy as jnp
import ml_dtypes
import numpy as np
from jax import lax
from jax.experimental import pallas as pl
from jax.experimental.pallas import tpu as pltpu
from jax.sharding import PartitionSpec as P

W = 256
HALF_W = 128
TC = 512
EXT = TC + W
SLOTS = 8
GROUP = 4
CHUNK = 32
F32 = jnp.float32
BF16 = jnp.bfloat16

RE, IM, NEG_IM = 0, 1, 2


def split_host(table):
    high = table.astype(np.float32).astype(ml_dtypes.bfloat16)
    low = (table - high.astype(np.float64)).astype(np.float32).astype(ml_dtypes.bfloat16)
    return [high, low]


def hop_tables():
    index = np.arange(W)
    dft = np.exp(-2j * np.pi / W * (index[:, None] * index[None, :] % W)) / math.sqrt(W)
    freqs = np.where(index < W // 2, index, index - W) / W
    fresnel = np.exp(-1j * np.pi * (W / 4.0) * freqs**2)
    hop = np.conj(dft) @ (fresnel[:, None] * dft)
    hop = hop * np.exp(1j * np.pi * index / W)
    out = []
    for table in (hop, hop.T):
        for part in (table.real, table.imag, -table.imag):
            out.extend(split_host(part))
    return np.stack(out)


def dft_tables():
    index = np.arange(W)
    angles = 2.0 * np.pi / W * (index[:, None] + 0.5) * (index[None, :HALF_W] + 0.5)
    table = np.concatenate([np.cos(angles), np.sin(angles)], axis=1) / math.sqrt(W)
    return np.stack(split_host(table) + split_host(table.T))


def fold_tables():
    source = np.concatenate([np.arange(HALF_W), np.arange(W - 1, HALF_W - 1, -1)])
    table = np.zeros((W, W), np.float32)
    table[source, np.arange(W)] = 1.0
    return np.stack([table, table.T]).astype(ml_dtypes.bfloat16)


def split(x):
    high = x.astype(BF16)
    return high, (x - high.astype(F32)).astype(BF16)


def lanes(*parts):
    return jnp.concatenate(parts, axis=1)


def rows(*parts):
    return jnp.concatenate(parts, axis=0)


def dot(a, b):
    return jnp.dot(a, b, preferred_element_type=F32)


def half_right(field, tab, at):
    high, low = tab[2 * at], tab[2 * at + 1]
    rh, rl = split(field[0])
    ih, il = split(field[1])
    out = dot(rows(lanes(rh, rl, rh), lanes(ih, il, ih)), rows(high, high, low))
    return out[:W], out[W:]


def half_left(field, tab, at):
    high, low = tab[2 * at], tab[2 * at + 1]
    rh, rl = split(field[0])
    ih, il = split(field[1])
    out = dot(lanes(high, high, low), lanes(rows(rh, rl, rh), rows(ih, il, ih)))
    return out[:, :W], out[:, W:]


def hop_parts(tab, at, conj):
    im, neg = (IM, NEG_IM) if not conj else (NEG_IM, IM)

    def three(a, b):
        a, b = 2 * (3 * at + a), 2 * (3 * at + b)
        return [tab[a], tab[b], tab[a], tab[b], tab[a + 1], tab[b + 1]]

    return three(RE, neg), three(im, RE)


def hop_right(field, tab, at, conj):
    rh, rl = split(field[0])
    ih, il = split(field[1])
    to_re, to_im = hop_parts(tab, at, conj)
    out = dot(lanes(rh, ih, rl, il, rh, ih), lanes(rows(*to_re), rows(*to_im)))
    return out[:, :W], out[:, W:]


def hop_left(field, tab, at, conj):
    rh, rl = split(field[0])
    ih, il = split(field[1])
    to_re, to_im = hop_parts(tab, at, conj)
    out = dot(rows(lanes(*to_re), lanes(*to_im)), rows(rh, ih, rl, il, rh, ih))
    return out[:W], out[W:]


def spread_right(field):
    c, s = field[0][:, :HALF_W], field[0][:, HALF_W:]
    d, t = field[1][:, :HALF_W], field[1][:, HALF_W:]
    return lanes(c + t, t - c), lanes(d - s, -d - s)


def spread_left(field):
    c, s = field[0][:HALF_W], field[0][HALF_W:]
    d, t = field[1][:HALF_W], field[1][HALF_W:]
    return rows(c + t, t - c), rows(d - s, -d - s)


def gather_right(field):
    a, b = field[0][:, :HALF_W], field[0][:, HALF_W:]
    c, d = field[1][:, :HALF_W], field[1][:, HALF_W:]
    return lanes(a - b, -c - d), lanes(c - d, a + b)


def gather_left(field):
    a, b = field[0][:HALF_W], field[0][HALF_W:]
    c, d = field[1][:HALF_W], field[1][HALF_W:]
    return rows(a - b, -c - d), rows(c - d, a + b)


def times(a, b):
    return a[0] * b[0] - a[1] * b[1], a[0] * b[1] + a[1] * b[0]


def conj_times(a, b):
    return a[0] * b[0] + a[1] * b[1], a[0] * b[1] - a[1] * b[0]


def pair(ref, *at):
    return ref[(*at, 0)], ref[(*at, 1)]


def put(value, ref, *at):
    ref[(*at, 0)], ref[(*at, 1)] = value


def chunks(body):
    def step(i, carry):
        body(pl.multiple_of(i * CHUNK, CHUNK))
        return carry

    lax.fori_loop(0, W // CHUNK, step, 0)


def geometry(meta, slot):
    row, col = meta[1 + slot], meta[1 + SLOTS + slot]
    block = col // W
    first = pl.multiple_of(block * W, W)
    second = pl.multiple_of(block * W + W, W)
    return row, col - block * W, first, second


def masks(row, col, at):
    in_top = lax.broadcasted_iota(jnp.int32, (CHUNK, W), 0) + at >= row
    in_first = lax.broadcasted_iota(jnp.int32, (CHUNK, W), 1) >= col
    return in_top, in_first


def load_window(meta, slot, ext, win, u):
    row, col, first, second = geometry(meta, slot)

    def load(at):
        in_top, in_first = masks(row, col, at)
        here = pl.ds(at, CHUNK)
        for p in range(2):
            top = jnp.where(in_first, ext[0, p, here, pl.ds(first, W)], ext[0, p, here, pl.ds(second, W)])
            low = jnp.where(in_first, ext[1, p, here, pl.ds(first, W)], ext[1, p, here, pl.ds(second, W)])
            win[u, p, here, :] = jnp.where(in_top, top, low)

    chunks(load)


def add_window(meta, slot, win, u, gext):
    row, col, first, second = geometry(meta, slot)

    def add(at):
        in_top, in_first = masks(row, col, at)
        here = pl.ds(at, CHUNK)
        zero = jnp.zeros((CHUNK, W), F32)
        for p in range(2):
            value = win[u, p, here, :]
            for r, part in ((0, jnp.where(in_top, value, zero)), (1, jnp.where(in_top, zero, value))):
                gext[r, p, here, pl.ds(first, W)] += jnp.where(in_first, part, zero)
                gext[r, p, here, pl.ds(second, W)] += jnp.where(in_first, zero, part)

    chunks(add)


def turn(plane, row, col):
    return pltpu.roll(pltpu.roll(plane, col, 1), row, 0)


def tile_copies(planes, refs, ext, sems, out):
    own, right, down0, down1, corner = refs
    inner = [
        (own if planes is None else own.at[planes], ext.at[0, :, :, pl.ds(0, TC)]),
        (right, ext.at[0, :, :, pl.ds(TC, W)]),
        (down0, ext.at[1, :, :, pl.ds(0, W)]),
        (down1, ext.at[1, :, :, pl.ds(W, W)]),
        (corner, ext.at[1, :, :, pl.ds(TC, W)]),
    ]
    return [
        pltpu.make_async_copy(*((b, a) if out else (a, b)), sems.at[i])
        for i, (a, b) in enumerate(inner)
    ]


def run_copies(copies, between=None):
    for copy in copies:
        copy.start()
    if between is not None:
        between()
    for copy in copies:
        copy.wait()


def first_kernel(meta, own, right, down0, down1, corner, probe, amp, tab, fold, prop, amp_out, ext, turned, win, sems):
    step = pl.program_id(0)

    def fold_amplitudes(u):
        high = amp[u].astype(BF16)
        rest = amp[u] - high.astype(F32)
        mid = rest.astype(BF16)
        low = (rest - mid.astype(F32)).astype(BF16)
        right_way = dot(rows(high, mid, low), fold[0])
        out = dot(fold[1], lanes(*(right_way[i * W : (i + 1) * W].astype(BF16) for i in range(3))))
        amp_out[u] = out[:, :W] + out[:, W : 2 * W] + out[:, 2 * W :]

    pl.when(step == 0)(lambda: run_copies(tile_copies(pl.ds(0, 2), (own, right, down0, down1, corner), ext, sems, False)))

    @pl.when(step * GROUP < meta[0])
    def work():
        for u in range(GROUP):
            slot = step * GROUP + u
            load_window(meta, slot, ext, win, u)
            row, col, _, _ = geometry(meta, slot)
            for p in range(2):
                turned[u, p] = turn(probe[p], row, col)
        fields = [times(pair(turned, u), pair(win, u)) for u in range(GROUP)]
        fields = [hop_right(f, tab, 0, False) for f in fields]
        fields = [hop_left(f, tab, 1, False) for f in fields]
        for u, f in enumerate(fields):
            put(f, prop, u)
            fold_amplitudes(u)


def second_kernel(meta, own, right, down0, down1, corner, prop, amp, tab, gown, gright, gdown0, gdown1, gcorner, back, ext, gext, win, sems):
    step = pl.program_id(0)

    @pl.when(step == 0)
    def begin():
        def clear():
            gext[...] = jnp.zeros_like(gext)

        run_copies(tile_copies(pl.ds(2, 2), (own, right, down0, down1, corner), ext, sems, False), clear)

    @pl.when(step * GROUP < meta[0])
    def work():
        group = range(GROUP)
        for u in group:
            load_window(meta, step * GROUP + u, ext, win, u)
        fields = [times(pair(prop, u), pair(win, u)) for u in group]
        fields = [spread_left(half_left(f, tab, 1)) for f in fields]
        fields = [spread_right(half_right(f, tab, 0)) for f in fields]
        chi = []
        for u, f in enumerate(fields):
            factor = 1.0 - amp[u] * lax.rsqrt(f[0] * f[0] + f[1] * f[1] + 1.0)
            chi.append((factor * f[0], factor * f[1]))
        fields = [half_right(gather_right(f), tab, 1) for f in chi]
        fields = [half_left(gather_left(f), tab, 0) for f in fields]
        for u, f in enumerate(fields):
            put(conj_times(pair(win, u), f), back, u)
        for u, f in enumerate(fields):
            put(conj_times(pair(prop, u), f), win, u)
        for u in group:
            slot = step * GROUP + u
            pl.when(slot < meta[0])(lambda: add_window(meta, slot, win, u, gext))

    @pl.when(step == SLOTS // GROUP - 1)
    def end():
        run_copies(tile_copies(None, (gown, gright, gdown0, gdown1, gcorner), gext, sems, True))


def third_kernel(meta, own, right, down0, down1, corner, probe, back, tab, gown, gright, gdown0, gdown1, gcorner, gprobe, ext, gext, turned, win, sems):
    step = pl.program_id(0)

    @pl.when(step == 0)
    def begin():
        def clear():
            gext[...] = jnp.zeros_like(gext)
            gprobe[...] = jnp.zeros_like(gprobe)

        run_copies(tile_copies(pl.ds(0, 2), (own, right, down0, down1, corner), ext, sems, False), clear)

    @pl.when(step * GROUP < meta[0])
    def work():
        group = range(GROUP)
        for u in group:
            slot = step * GROUP + u
            load_window(meta, slot, ext, win, u)
            row, col, _, _ = geometry(meta, slot)
            for p in range(2):
                turned[u, p] = turn(probe[p], row, col)
        fields = [hop_left(pair(back, u), tab, 0, True) for u in group]
        fields = [hop_right(f, tab, 1, True) for f in fields]
        for u, f in enumerate(fields):
            grad, probe_part = conj_times(pair(turned, u), f), conj_times(pair(win, u), f)
            put(grad, win, u)
            put(probe_part, turned, u)

        def finish(slot, u):
            add_window(meta, slot, win, u, gext)
            row, col, _, _ = geometry(meta, slot)
            for p in range(2):
                gprobe[p] += turn(turned[u, p], W - row, W - col)

        for u in group:
            slot = step * GROUP + u
            pl.when(slot < meta[0])(lambda: finish(slot, u))

    @pl.when(step == SLOTS // GROUP - 1)
    def end():
        run_copies(tile_copies(None, (gown, gright, gdown0, gdown1, gcorner), gext, sems, True))


ANYWHERE = pl.BlockSpec(memory_space=pl.ANY)
WHOLE = pl.BlockSpec(memory_space=pltpu.VMEM)
SCALARS = pl.BlockSpec(memory_space=pltpu.SMEM)
FIELDS = pl.BlockSpec((GROUP, 2, W, W), lambda i: (i, 0, 0, 0))
PLANES = pl.BlockSpec((GROUP, W, W), lambda i: (i, 0, 0))


def shape(*dims):
    return jax.ShapeDtypeStruct(dims, F32)


FIELDS_SHAPE = shape(SLOTS, 2, W, W)
TILE_SHAPES = [shape(2, W, TC)] + [shape(2, W, W)] * 4
EXT_SCRATCH = pltpu.VMEM((2, 2, W, EXT), F32)
GROUP_SCRATCH = pltpu.VMEM((GROUP, 2, W, W), F32)
SEMS = pltpu.SemaphoreType.DMA((5,))


def call(kernel, in_specs, out_specs, out_shape, scratch, products):
    return pl.pallas_call(
        kernel,
        grid=(SLOTS // GROUP,),
        in_specs=in_specs,
        out_specs=out_specs,
        out_shape=out_shape,
        scratch_shapes=scratch,
        compiler_params=pltpu.CompilerParams(
            vmem_limit_bytes=56 * 2**20, dimension_semantics=("arbitrary",)
        ),
        cost_estimate=pl.CostEstimate(
            flops=SLOTS * products * 2 * W**3, bytes_accessed=12 * 2**20, transcendentals=0
        ),
    )


def first_call(*args):
    return call(
        first_kernel,
        [SCALARS] + [ANYWHERE] * 5 + [WHOLE, PLANES, WHOLE, WHOLE],
        [FIELDS, PLANES],
        [FIELDS_SHAPE, shape(SLOTS, W, W)],
        [EXT_SCRATCH, GROUP_SCRATCH, GROUP_SCRATCH, SEMS],
        24,
    )(*args)


def second_call(*args):
    return call(
        second_kernel,
        [SCALARS] + [ANYWHERE] * 5 + [FIELDS, PLANES, WHOLE],
        [ANYWHERE] * 5 + [FIELDS],
        TILE_SHAPES + [FIELDS_SHAPE],
        [EXT_SCRATCH, EXT_SCRATCH, GROUP_SCRATCH, SEMS],
        24,
    )(*args)


def third_call(*args):
    return call(
        third_kernel,
        [SCALARS] + [ANYWHERE] * 5 + [WHOLE, FIELDS, WHOLE],
        [ANYWHERE] * 5 + [WHOLE],
        TILE_SHAPES + [shape(2, W, W)],
        [EXT_SCRATCH, EXT_SCRATCH, GROUP_SCRATCH, GROUP_SCRATCH, SEMS],
        24,
    )(*args)


def shift(value, axis, steps):
    count = lax.axis_size(axis)
    first, last = (max(0, -steps), min(count, count - steps))
    return lax.ppermute(value, axis, [(source, source + steps) for source in range(first, last)])


def fetch(tile):
    first_half = tile[:, :, :W]
    down0 = shift(first_half, "row", -1)
    down1 = shift(tile[:, :, W:], "row", -1)
    right = shift(first_half, "col", -1)
    corner = shift(down0, "col", -1)
    return right, down0, down1, corner


def hand_back(gright, gdown0, gdown1, gcorner):
    corner_back = shift(gcorner, "col", 1)
    down1_back = shift(gdown1, "row", 1)
    right_back = shift(gright, "col", 1)
    down0_back = shift(gdown0 + corner_back, "row", 1)
    return jnp.concatenate([right_back + down0_back, down1_back], axis=2)


def sum_all(value, axes):
    count = lax.axis_size(axes)
    shares = value.reshape(count, -1, value.shape[-1])
    mine = lax.all_to_all(shares, axes, 0, 0, tiled=True).sum(axis=0)
    spread = jnp.broadcast_to(mine[None], shares.shape)
    return lax.all_to_all(spread, axes, 0, 0, tiled=True).reshape(value.shape)


def body(object_slab, probe_wave, scan_offsets, live_counts, amplitudes):
    rows_tile, cols_tile = object_slab.shape[1:]
    local_rows = scan_offsets[:, 0] - lax.axis_index("row") * rows_tile
    local_cols = scan_offsets[:, 1] - lax.axis_index("col") * cols_tile
    meta = jnp.concatenate([live_counts, local_rows, local_cols])
    hop, dft, fold = jnp.asarray(hop_tables()), jnp.asarray(dft_tables()), jnp.asarray(fold_tables())
    near_one = fetch(object_slab[:2])
    near_two = fetch(object_slab[2:])
    prop, amp = first_call(meta, object_slab, *near_one, probe_wave, amplitudes, hop, fold)
    *grads_two, back = second_call(meta, object_slab, *near_two, prop, amp, dft)
    *grads_one, gprobe = third_call(meta, object_slab, *near_one, probe_wave, back, hop)
    back_two = hand_back(*grads_two[1:])
    back_one = hand_back(*grads_one[1:])
    probe_grad = sum_all(gprobe, ("row", "col"))
    object_grad = jnp.concatenate([grads_one[0] + back_one, grads_two[0] + back_two], axis=0)
    return object_grad, probe_grad


def solution(mesh):
    return jax.shard_map(
        body,
        mesh=mesh,
        in_specs=(
            P(None, "row", "col"),
            P(),
            P(("row", "col"), None),
            P(("row", "col")),
            P(("row", "col"), None, None),
        ),
        out_specs=(P(None, "row", "col"), P()),
        check_vma=False,
    )
```

```python
import math

import jax
import jax.numpy as jnp
import ml_dtypes
import numpy as np
from jax import lax
from jax.experimental import pallas as pl
from jax.experimental.pallas import tpu as pltpu
from jax.sharding import PartitionSpec as P

W = 256
HALF_W = 128
TC = 512
EXT = TC + W
SLOTS = 8
GROUP = 4
CHUNK = 32
F32 = jnp.float32
BF16 = jnp.bfloat16

RE, IM, NEG_IM = 0, 1, 2


def split_host(table):
    high = table.astype(np.float32).astype(ml_dtypes.bfloat16)
    low = (table - high.astype(np.float64)).astype(np.float32).astype(ml_dtypes.bfloat16)
    return [high, low]


def hop_tables():
    index = np.arange(W)
    dft = np.exp(-2j * np.pi / W * (index[:, None] * index[None, :] % W)) / math.sqrt(W)
    freqs = np.where(index < W // 2, index, index - W) / W
    fresnel = np.exp(-1j * np.pi * (W / 4.0) * freqs**2)
    hop = np.conj(dft) @ (fresnel[:, None] * dft)
    hop = hop * np.exp(1j * np.pi * index / W)
    out = []
    for table in (hop, hop.T):
        for part in (table.real, table.imag, -table.imag):
            out.extend(split_host(part))
    return np.stack(out)


def dft_tables():
    index = np.arange(W)
    angles = 2.0 * np.pi / W * (index[:, None] + 0.5) * (index[None, :HALF_W] + 0.5)
    table = np.concatenate([np.cos(angles), np.sin(angles)], axis=1) / math.sqrt(W)
    return np.stack(split_host(table) + split_host(table.T))


def fold_tables():
    source = np.concatenate([np.arange(HALF_W), np.arange(W - 1, HALF_W - 1, -1)])
    table = np.zeros((W, W), np.float32)
    table[source, np.arange(W)] = 1.0
    return np.stack([table, table.T]).astype(ml_dtypes.bfloat16)


def split(x):
    high = x.astype(BF16)
    return high, (x - high.astype(F32)).astype(BF16)


def lanes(*parts):
    return jnp.concatenate(parts, axis=1)


def rows(*parts):
    return jnp.concatenate(parts, axis=0)


def dot(a, b):
    return jnp.dot(a, b, preferred_element_type=F32)


def half_right(field, tab, at):
    high, low = tab[2 * at], tab[2 * at + 1]
    rh, rl = split(field[0])
    ih, il = split(field[1])
    out = dot(rows(lanes(rh, rl, rh), lanes(ih, il, ih)), rows(high, high, low))
    return out[:W], out[W:]


def half_left(field, tab, at):
    high, low = tab[2 * at], tab[2 * at + 1]
    rh, rl = split(field[0])
    ih, il = split(field[1])
    out = dot(lanes(high, high, low), lanes(rows(rh, rl, rh), rows(ih, il, ih)))
    return out[:, :W], out[:, W:]


def hop_parts(tab, at, conj):
    im, neg = (IM, NEG_IM) if not conj else (NEG_IM, IM)

    def three(a, b):
        a, b = 2 * (3 * at + a), 2 * (3 * at + b)
        return [tab[a], tab[b], tab[a], tab[b], tab[a + 1], tab[b + 1]]

    return three(RE, neg), three(im, RE)


def hop_right(field, tab, at, conj):
    rh, rl = split(field[0])
    ih, il = split(field[1])
    to_re, to_im = hop_parts(tab, at, conj)
    out = dot(lanes(rh, ih, rl, il, rh, ih), lanes(rows(*to_re), rows(*to_im)))
    return out[:, :W], out[:, W:]


def hop_left(field, tab, at, conj):
    rh, rl = split(field[0])
    ih, il = split(field[1])
    to_re, to_im = hop_parts(tab, at, conj)
    out = dot(rows(lanes(*to_re), lanes(*to_im)), rows(rh, ih, rl, il, rh, ih))
    return out[:W], out[W:]


def spread_right(field):
    c, s = field[0][:, :HALF_W], field[0][:, HALF_W:]
    d, t = field[1][:, :HALF_W], field[1][:, HALF_W:]
    return lanes(c + t, t - c), lanes(d - s, -d - s)


def spread_left(field):
    c, s = field[0][:HALF_W], field[0][HALF_W:]
    d, t = field[1][:HALF_W], field[1][HALF_W:]
    return rows(c + t, t - c), rows(d - s, -d - s)


def gather_right(field):
    a, b = field[0][:, :HALF_W], field[0][:, HALF_W:]
    c, d = field[1][:, :HALF_W], field[1][:, HALF_W:]
    return lanes(a - b, -c - d), lanes(c - d, a + b)


def gather_left(field):
    a, b = field[0][:HALF_W], field[0][HALF_W:]
    c, d = field[1][:HALF_W], field[1][HALF_W:]
    return rows(a - b, -c - d), rows(c - d, a + b)


def times(a, b):
    return a[0] * b[0] - a[1] * b[1], a[0] * b[1] + a[1] * b[0]


def conj_times(a, b):
    return a[0] * b[0] + a[1] * b[1], a[0] * b[1] - a[1] * b[0]


def pair(ref, *at):
    return ref[(*at, 0)], ref[(*at, 1)]


def put(value, ref, *at):
    ref[(*at, 0)], ref[(*at, 1)] = value


def chunks(body):
    def step(i, carry):
        body(pl.multiple_of(i * CHUNK, CHUNK))
        return carry

    lax.fori_loop(0, W // CHUNK, step, 0)


def geometry(meta, slot):
    row, col = meta[1 + slot], meta[1 + SLOTS + slot]
    block = col // W
    first = pl.multiple_of(block * W, W)
    second = pl.multiple_of(block * W + W, W)
    return row, col - block * W, first, second


def masks(row, col, at):
    in_top = lax.broadcasted_iota(jnp.int32, (CHUNK, W), 0) + at >= row
    in_first = lax.broadcasted_iota(jnp.int32, (CHUNK, W), 1) >= col
    return in_top, in_first


def load_window(meta, slot, ext, planes, win, u):
    row, col, first, second = geometry(meta, slot)
    border = row // CHUNK

    def load(i, carry):
        here = pl.ds(pl.multiple_of(i * CHUNK, CHUNK), CHUNK)
        _, in_first = masks(row, col, 0)
        low = (i < border).astype(jnp.int32)
        for p in planes:
            win[u, p, here, :] = jnp.where(
                in_first, ext[low, p, here, pl.ds(first, W)], ext[low, p, here, pl.ds(second, W)]
            )
        return carry

    lax.fori_loop(0, W // CHUNK, load, 0, unroll=2)
    at = pl.multiple_of(border * CHUNK, CHUNK)
    here = pl.ds(at, CHUNK)
    in_top, in_first = masks(row, col, at)
    for p in planes:
        low = jnp.where(in_first, ext[1, p, here, pl.ds(first, W)], ext[1, p, here, pl.ds(second, W)])
        win[u, p, here, :] = jnp.where(in_top, win[u, p, here, :], low)


def add_window(meta, slot, win, u, planes, gext):
    row, col, first, second = geometry(meta, slot)
    border = row // CHUNK
    zero = jnp.zeros((CHUNK, W), F32)

    def add(i, carry):
        at = pl.multiple_of(i * CHUNK, CHUNK)
        here = pl.ds(at, CHUNK)
        in_top, in_first = masks(row, col, at)
        low = (i < border).astype(jnp.int32)
        keep = jnp.logical_or(in_top, i < border)
        for p in planes:
            value = jnp.where(keep, win[u, p, here, :], zero)
            gext[low, p, here, pl.ds(first, W)] += jnp.where(in_first, value, zero)
            gext[low, p, here, pl.ds(second, W)] += jnp.where(in_first, zero, value)
        return carry

    lax.fori_loop(0, W // CHUNK, add, 0, unroll=2)
    at = pl.multiple_of(border * CHUNK, CHUNK)
    here = pl.ds(at, CHUNK)
    in_top, in_first = masks(row, col, at)
    for p in planes:
        value = jnp.where(in_top, zero, win[u, p, here, :])
        gext[1, p, here, pl.ds(first, W)] += jnp.where(in_first, value, zero)
        gext[1, p, here, pl.ds(second, W)] += jnp.where(in_first, zero, value)


def turn_probe(meta, slot, twice, turned, u):
    row, col, _, _ = geometry(meta, slot)
    for p in range(2):
        here = pl.ds(W - row, W)
        turned[u, p] = pltpu.roll(lanes(twice[p, 0, here, :], twice[p, 1, here, :]), col, 1)


def add_probe(meta, slot, part, u, acc):
    row, col, _, _ = geometry(meta, slot)
    for p in range(2):
        here = pl.ds(W - row, W)
        value = pltpu.roll(part[u, p], W - col, 1)
        acc[p, 0, here, :] += value[:, :HALF_W]
        acc[p, 1, here, :] += value[:, HALF_W:]


def tile_copies(refs, ext, sems):
    own, right, down0, down1, corner = refs
    return [
        (own, ext.at[0, :, :, pl.ds(0, TC)], sems.at[0]),
        (right, ext.at[0, :, :, pl.ds(TC, W)], sems.at[1]),
        (down0, ext.at[1, :, :, pl.ds(0, W)], sems.at[2]),
        (down1, ext.at[1, :, :, pl.ds(W, W)], sems.at[3]),
        (corner, ext.at[1, :, :, pl.ds(TC, W)], sems.at[4]),
    ]


def start_copies(copies):
    copies = [pltpu.make_async_copy(*copy) for copy in copies]
    for copy in copies:
        copy.start()
    return copies


def wait_copies(copies):
    for copy in copies:
        copy.wait()


def first_kernel(meta, own, right, down0, down1, corner, twice, amp, tab, fold, prop, amp_out, ext, turned, win, sems):
    step = pl.program_id(0)

    def fold_amplitudes(u):
        high = amp[u].astype(BF16)
        rest = amp[u] - high.astype(F32)
        mid = rest.astype(BF16)
        low = (rest - mid.astype(F32)).astype(BF16)
        right_way = dot(rows(high, mid, low), fold[0])
        out = dot(fold[1], lanes(*(right_way[i * W : (i + 1) * W].astype(BF16) for i in range(3))))
        amp_out[u] = out[:, :W] + out[:, W : 2 * W] + out[:, 2 * W :]

    @pl.when(step == 0)
    def begin():
        one = pl.ds(0, 2)
        refs = (own.at[one], right.at[one], down0.at[one], down1, corner)
        wait_copies(start_copies(tile_copies(refs, ext, sems)))

    @pl.when(step * GROUP < meta[0])
    def work():
        for u in range(GROUP):
            slot = step * GROUP + u
            load_window(meta, slot, ext, (0, 1), win, u)
            turn_probe(meta, slot, twice, turned, u)
        fields = [times(pair(turned, u), pair(win, u)) for u in range(GROUP)]
        fields = [hop_right(f, tab, 0, False) for f in fields]
        fields = [hop_left(f, tab, 1, False) for f in fields]
        for u, f in enumerate(fields):
            put(f, prop, u)
            fold_amplitudes(u)


def second_kernel(meta, own, right, down0, down1_one, down1_two, corner_one, corner_two, twice, prop, amp, dft, hop,
                  gown, gright, gdown0, gdown1, gcorner, gprobe, ext, gext, acc, turned, win, sems):
    step = pl.program_id(0)
    group = range(GROUP)
    one, two = pl.ds(0, 2), pl.ds(2, 2)
    refs_one = (own.at[one], right.at[one], down0.at[one], down1_one, corner_one)
    refs_two = (own.at[two], right.at[two], down0.at[two], down1_two, corner_two)
    copies_one = tile_copies(refs_one, ext.at[:, one], sems.at[0])
    copies_two = tile_copies(refs_two, ext.at[:, two], sems.at[1])

    @pl.when(step == 0)
    def begin():
        started = start_copies(copies_two)
        start_copies(copies_one)
        gext[...] = jnp.zeros_like(gext)
        acc[...] = jnp.zeros_like(acc)
        wait_copies(started)

    live = step * GROUP < meta[0]

    @pl.when(live)
    def stage_one():
        for u in group:
            load_window(meta, step * GROUP + u, ext, (2, 3), win, u)
        fields = [times(pair(prop, u), (win[u, 2], win[u, 3])) for u in group]
        fields = [spread_left(half_left(f, dft, 1)) for f in fields]
        fields = [spread_right(half_right(f, dft, 0)) for f in fields]
        chi = []
        for u, f in enumerate(fields):
            factor = 1.0 - amp[u] * lax.rsqrt(f[0] * f[0] + f[1] * f[1] + 1.0)
            chi.append((factor * f[0], factor * f[1]))
        fields = [half_right(gather_right(f), dft, 1) for f in chi]
        fields = [half_left(gather_left(f), dft, 0) for f in fields]
        waves = [conj_times((win[u, 2], win[u, 3]), f) for u, f in enumerate(fields)]
        for u, f in enumerate(fields):
            win[u, 2], win[u, 3] = conj_times(pair(prop, u), f)
        waves = [hop_left(f, hop, 0, True) for f in waves]
        waves = [hop_right(f, hop, 1, True) for f in waves]
        for u, f in enumerate(waves):
            put(f, prop, u)

    @pl.when(step == 0)
    def arrive():
        wait_copies([pltpu.make_async_copy(*copy) for copy in copies_one])

    @pl.when(live)
    def stage_two():
        for u in group:
            slot = step * GROUP + u
            load_window(meta, slot, ext, (0, 1), win, u)
            turn_probe(meta, slot, twice, turned, u)
        for u in group:
            wave = pair(prop, u)
            grad, part = conj_times(pair(turned, u), wave), conj_times(pair(win, u), wave)
            put(grad, win, u)
            put(part, turned, u)

        def finish(slot, u):
            add_window(meta, slot, win, u, range(4), gext)
            add_probe(meta, slot, turned, u, acc)

        for u in group:
            slot = step * GROUP + u
            pl.when(slot < meta[0])(lambda: finish(slot, u))

    @pl.when(step == SLOTS // GROUP - 1)
    def end():
        refs = (gown, gright, gdown0, gdown1, gcorner)
        outs = start_copies([(b, a, sem) for a, b, sem in tile_copies(refs, gext, sems.at[0])])
        for p in range(2):
            gprobe[p] = lanes(acc[p, 0, :W, :] + acc[p, 0, W:, :], acc[p, 1, :W, :] + acc[p, 1, W:, :])
        wait_copies(outs)


ANYWHERE = pl.BlockSpec(memory_space=pl.ANY)
WHOLE = pl.BlockSpec(memory_space=pltpu.VMEM)
SCALARS = pl.BlockSpec(memory_space=pltpu.SMEM)
FIELDS = pl.BlockSpec((GROUP, 2, W, W), lambda i: (i, 0, 0, 0))
PLANES = pl.BlockSpec((GROUP, W, W), lambda i: (i, 0, 0))


def shape(*dims):
    return jax.ShapeDtypeStruct(dims, F32)


FIELDS_SHAPE = shape(SLOTS, 2, W, W)


def call(kernel, in_specs, out_specs, out_shape, scratch, products):
    return pl.pallas_call(
        kernel,
        grid=(SLOTS // GROUP,),
        in_specs=in_specs,
        out_specs=out_specs,
        out_shape=out_shape,
        scratch_shapes=scratch,
        compiler_params=pltpu.CompilerParams(
            vmem_limit_bytes=56 * 2**20, dimension_semantics=("arbitrary",)
        ),
        cost_estimate=pl.CostEstimate(
            flops=SLOTS * products * 2 * W**3, bytes_accessed=12 * 2**20, transcendentals=0
        ),
    )


def first_call(*args):
    return call(
        first_kernel,
        [SCALARS] + [ANYWHERE] * 5 + [WHOLE, PLANES, WHOLE, WHOLE],
        [FIELDS, PLANES],
        [FIELDS_SHAPE, shape(SLOTS, W, W)],
        [
            pltpu.VMEM((2, 2, W, EXT), F32),
            pltpu.VMEM((GROUP, 2, W, W), F32),
            pltpu.VMEM((GROUP, 2, W, W), F32),
            pltpu.SemaphoreType.DMA((5,)),
        ],
        30,
    )(*args)


def second_call(*args):
    return call(
        second_kernel,
        [SCALARS] + [ANYWHERE] * 7 + [WHOLE, FIELDS, PLANES, WHOLE, WHOLE],
        [ANYWHERE] * 5 + [WHOLE],
        [shape(4, W, TC)] + [shape(4, W, W)] * 4 + [shape(2, W, W)],
        [
            pltpu.VMEM((2, 4, W, EXT), F32),
            pltpu.VMEM((2, 4, W, EXT), F32),
            pltpu.VMEM((2, 2, 2 * W, HALF_W), F32),
            pltpu.VMEM((GROUP, 2, W, W), F32),
            pltpu.VMEM((GROUP, 4, W, W), F32),
            pltpu.SemaphoreType.DMA((2, 5)),
        ],
        48,
    )(*args)


def shift(value, axis, steps):
    count = lax.axis_size(axis)
    first, last = (max(0, -steps), min(count, count - steps))
    return lax.ppermute(value, axis, [(source, source + steps) for source in range(first, last)])


def sum_all(value, axes):
    count = lax.axis_size(axes)
    shares = value.reshape(count, -1, value.shape[-1])
    mine = lax.all_to_all(shares, axes, 0, 0, tiled=True).sum(axis=0)
    spread = jnp.broadcast_to(mine[None], shares.shape)
    return lax.all_to_all(spread, axes, 0, 0, tiled=True).reshape(value.shape)


def probe_twice(probe):
    halves = probe.reshape(2, W, 2, HALF_W).transpose(0, 2, 1, 3)
    return jnp.concatenate([halves, halves], axis=2)


def body(object_slab, probe_wave, scan_offsets, live_counts, amplitudes):
    rows_tile, cols_tile = object_slab.shape[1:]
    local_rows = scan_offsets[:, 0] - lax.axis_index("row") * rows_tile
    local_cols = scan_offsets[:, 1] - lax.axis_index("col") * cols_tile
    meta = jnp.concatenate([live_counts, local_rows, local_cols])
    hop, dft, fold = jnp.asarray(hop_tables()), jnp.asarray(dft_tables()), jnp.asarray(fold_tables())
    twice = probe_twice(probe_wave)
    first_half = object_slab[:, :, :W]
    down0 = shift(first_half, "row", -1)
    down1_one = shift(object_slab[:2, :, W:], "row", -1)
    down1_two = shift(object_slab[2:, :, W:], "row", -1)
    right = shift(first_half, "col", -1)
    corner_one = shift(down0[:2], "col", -1)
    corner_two = shift(down0[2:], "col", -1)
    prop, amp = first_call(
        meta, object_slab, right, down0, down1_one, corner_one, twice, amplitudes, hop, fold
    )
    gown, gright, gdown0, gdown1, gcorner, gprobe = second_call(
        meta, object_slab, right, down0, down1_one, down1_two, corner_one, corner_two, twice, prop, amp, dft, hop
    )
    corner_back = shift(gcorner, "col", 1)
    down1_back = shift(gdown1, "row", 1)
    right_back = shift(gright, "col", 1)
    down0_back = shift(gdown0 + corner_back, "row", 1)
    probe_grad = sum_all(gprobe, ("row", "col"))
    object_grad = gown + jnp.concatenate([right_back + down0_back, down1_back], axis=2)
    return object_grad, probe_grad


def solution(mesh):
    return jax.shard_map(
        body,
        mesh=mesh,
        in_specs=(
            P(None, "row", "col"),
            P(),
            P(("row", "col"), None),
            P(("row", "col")),
            P(("row", "col"), None, None),
        ),
        out_specs=(P(None, "row", "col"), P()),
        check_vma=False,
    )
```

```python
import math

import jax
import jax.numpy as jnp
import ml_dtypes
import numpy as np
from jax import lax
from jax.experimental import pallas as pl
from jax.experimental.pallas import tpu as pltpu
from jax.sharding import PartitionSpec as P

W = 256
HALF_W = 128
TC = 512
EXT = TC + W
SLOTS = 8
GROUP = 4
PREPARED = 2
CHUNK = 32
F32 = jnp.float32
BF16 = jnp.bfloat16

RE, IM, NEG_IM = 0, 1, 2


def split_host(table):
    high = table.astype(np.float32).astype(ml_dtypes.bfloat16)
    low = (table - high.astype(np.float64)).astype(np.float32).astype(ml_dtypes.bfloat16)
    return [high, low]


def hop_tables():
    index = np.arange(W)
    dft = np.exp(-2j * np.pi / W * (index[:, None] * index[None, :] % W)) / math.sqrt(W)
    freqs = np.where(index < W // 2, index, index - W) / W
    fresnel = np.exp(-1j * np.pi * (W / 4.0) * freqs**2)
    hop = np.conj(dft) @ (fresnel[:, None] * dft)
    hop = hop * np.exp(1j * np.pi * index / W)
    out = []
    for table in (hop, hop.T):
        for part in (table.real, table.imag, -table.imag):
            out.extend(split_host(part))
    return np.stack(out)


def dft_tables():
    index = np.arange(W)
    angles = 2.0 * np.pi / W * (index[:, None] + 0.5) * (index[None, :HALF_W] + 0.5)
    table = np.concatenate([np.cos(angles), np.sin(angles)], axis=1) / math.sqrt(W)
    return np.stack(split_host(table) + split_host(table.T))


def fold_tables():
    source = np.concatenate([np.arange(HALF_W), np.arange(W - 1, HALF_W - 1, -1)])
    table = np.zeros((W, W), np.float32)
    table[source, np.arange(W)] = 1.0
    return np.stack([table, table.T]).astype(ml_dtypes.bfloat16)


def split(x):
    high = x.astype(BF16)
    return high, (x - high.astype(F32)).astype(BF16)


def lanes(*parts):
    return jnp.concatenate(parts, axis=1)


def rows(*parts):
    return jnp.concatenate(parts, axis=0)


def dot(a, b):
    return jnp.dot(a, b, preferred_element_type=F32)


def half_right(field, tab, at):
    high, low = tab[2 * at], tab[2 * at + 1]
    rh, rl = split(field[0])
    ih, il = split(field[1])
    out = dot(rows(lanes(rh, rl, rh), lanes(ih, il, ih)), rows(high, high, low))
    return out[:W], out[W:]


def half_left(field, tab, at):
    high, low = tab[2 * at], tab[2 * at + 1]
    rh, rl = split(field[0])
    ih, il = split(field[1])
    out = dot(lanes(high, high, low), lanes(rows(rh, rl, rh), rows(ih, il, ih)))
    return out[:, :W], out[:, W:]


def hop_parts(tab, at, conj):
    im, neg = (IM, NEG_IM) if not conj else (NEG_IM, IM)

    def three(a, b):
        a, b = 2 * (3 * at + a), 2 * (3 * at + b)
        return [tab[a], tab[b], tab[a], tab[b], tab[a + 1], tab[b + 1]]

    return three(RE, neg), three(im, RE)


def hop_right(field, tab, at, conj):
    rh, rl = split(field[0])
    ih, il = split(field[1])
    to_re, to_im = hop_parts(tab, at, conj)
    out = dot(lanes(rh, ih, rl, il, rh, ih), lanes(rows(*to_re), rows(*to_im)))
    return out[:, :W], out[:, W:]


def hop_left(field, tab, at, conj):
    rh, rl = split(field[0])
    ih, il = split(field[1])
    to_re, to_im = hop_parts(tab, at, conj)
    out = dot(rows(lanes(*to_re), lanes(*to_im)), rows(rh, ih, rl, il, rh, ih))
    return out[:W], out[W:]


def spread_right(field):
    c, s = field[0][:, :HALF_W], field[0][:, HALF_W:]
    d, t = field[1][:, :HALF_W], field[1][:, HALF_W:]
    return lanes(c + t, t - c), lanes(d - s, -d - s)


def spread_left(field):
    c, s = field[0][:HALF_W], field[0][HALF_W:]
    d, t = field[1][:HALF_W], field[1][HALF_W:]
    return rows(c + t, t - c), rows(d - s, -d - s)


def gather_right(field):
    a, b = field[0][:, :HALF_W], field[0][:, HALF_W:]
    c, d = field[1][:, :HALF_W], field[1][:, HALF_W:]
    return lanes(a - b, -c - d), lanes(c - d, a + b)


def gather_left(field):
    a, b = field[0][:HALF_W], field[0][HALF_W:]
    c, d = field[1][:HALF_W], field[1][HALF_W:]
    return rows(a - b, -c - d), rows(c - d, a + b)


def times(a, b):
    return a[0] * b[0] - a[1] * b[1], a[0] * b[1] + a[1] * b[0]


def conj_times(a, b):
    return a[0] * b[0] + a[1] * b[1], a[0] * b[1] - a[1] * b[0]


def pair(ref, *at):
    return ref[(*at, 0)], ref[(*at, 1)]


def put(value, ref, *at):
    ref[(*at, 0)], ref[(*at, 1)] = value


def chunks(body):
    def step(i, carry):
        body(pl.multiple_of(i * CHUNK, CHUNK))
        return carry

    lax.fori_loop(0, W // CHUNK, step, 0)


def geometry(meta, slot):
    row, col = meta[1 + slot], meta[1 + SLOTS + slot]
    block = col // W
    first = pl.multiple_of(block * W, W)
    second = pl.multiple_of(block * W + W, W)
    return row, col - block * W, first, second


def masks(row, col, at):
    in_top = lax.broadcasted_iota(jnp.int32, (CHUNK, W), 0) + at >= row
    in_first = lax.broadcasted_iota(jnp.int32, (CHUNK, W), 1) >= col
    return in_top, in_first


def load_window(meta, slot, ext, planes, win, u):
    row, col, first, second = geometry(meta, slot)
    border = row // CHUNK

    def load(i, carry):
        here = pl.ds(pl.multiple_of(i * CHUNK, CHUNK), CHUNK)
        _, in_first = masks(row, col, 0)
        low = (i < border).astype(jnp.int32)
        for p in planes:
            win[u, p, here, :] = jnp.where(
                in_first, ext[low, p, here, pl.ds(first, W)], ext[low, p, here, pl.ds(second, W)]
            )
        return carry

    lax.fori_loop(0, W // CHUNK, load, 0, unroll=2)
    at = pl.multiple_of(border * CHUNK, CHUNK)
    here = pl.ds(at, CHUNK)
    in_top, in_first = masks(row, col, at)
    for p in planes:
        low = jnp.where(in_first, ext[1, p, here, pl.ds(first, W)], ext[1, p, here, pl.ds(second, W)])
        win[u, p, here, :] = jnp.where(in_top, win[u, p, here, :], low)


def add_window(meta, slot, win, u, planes, gext):
    row, col, first, second = geometry(meta, slot)
    border = row // CHUNK
    zero = jnp.zeros((CHUNK, W), F32)

    def add(i, carry):
        at = pl.multiple_of(i * CHUNK, CHUNK)
        here = pl.ds(at, CHUNK)
        in_top, in_first = masks(row, col, at)
        low = (i < border).astype(jnp.int32)
        keep = jnp.logical_or(in_top, i < border)
        for p in planes:
            value = jnp.where(keep, win[u, p, here, :], zero)
            gext[low, p, here, pl.ds(first, W)] += jnp.where(in_first, value, zero)
            gext[low, p, here, pl.ds(second, W)] += jnp.where(in_first, zero, value)
        return carry

    lax.fori_loop(0, W // CHUNK, add, 0, unroll=2)
    at = pl.multiple_of(border * CHUNK, CHUNK)
    here = pl.ds(at, CHUNK)
    in_top, in_first = masks(row, col, at)
    for p in planes:
        value = jnp.where(in_top, zero, win[u, p, here, :])
        gext[1, p, here, pl.ds(first, W)] += jnp.where(in_first, value, zero)
        gext[1, p, here, pl.ds(second, W)] += jnp.where(in_first, zero, value)


def turn_probe(meta, slot, twice, turned, u):
    row, col, _, _ = geometry(meta, slot)
    for p in range(2):
        here = pl.ds(W - row, W)
        turned[u, p] = pltpu.roll(lanes(twice[p, 0, here, :], twice[p, 1, here, :]), col, 1)


def add_probe(meta, slot, part, u, acc):
    row, col, _, _ = geometry(meta, slot)
    for p in range(2):
        here = pl.ds(W - row, W)
        value = pltpu.roll(part[u, p], W - col, 1)
        acc[p, 0, here, :] += value[:, :HALF_W]
        acc[p, 1, here, :] += value[:, HALF_W:]


def tile_copies(refs, ext, sems):
    own, right, down0, down1, corner = refs
    return [
        (own, ext.at[0, :, :, pl.ds(0, TC)], sems.at[0]),
        (right, ext.at[0, :, :, pl.ds(TC, W)], sems.at[1]),
        (down0, ext.at[1, :, :, pl.ds(0, W)], sems.at[2]),
        (down1, ext.at[1, :, :, pl.ds(W, W)], sems.at[3]),
        (corner, ext.at[1, :, :, pl.ds(TC, W)], sems.at[4]),
    ]


def start_copies(copies):
    copies = [pltpu.make_async_copy(*copy) for copy in copies]
    for copy in copies:
        copy.start()
    return copies


def wait_copies(copies):
    for copy in copies:
        copy.wait()


def prepare_kernel(meta, twice, amp, fold, amp_out, turned):
    step = pl.program_id(0)

    def fold_amplitudes(u):
        high = amp[u].astype(BF16)
        rest = amp[u] - high.astype(F32)
        mid = rest.astype(BF16)
        low = (rest - mid.astype(F32)).astype(BF16)
        right_way = dot(rows(high, mid, low), fold[0])
        out = dot(fold[1], lanes(*(right_way[i * W : (i + 1) * W].astype(BF16) for i in range(3))))
        amp_out[u] = out[:, :W] + out[:, W : 2 * W] + out[:, 2 * W :]

    for u in range(PREPARED):
        fold_amplitudes(u)
        turn_probe(meta, step * PREPARED + u, twice, turned, u)


def first_kernel(meta, own, right, down0, down1, corner, turned, tab, prop, ext, win, sems):
    step = pl.program_id(0)

    @pl.when(step == 0)
    def begin():
        refs = (own.at[pl.ds(0, 2)], right.at[pl.ds(0, 2)], down0, down1, corner)
        wait_copies(start_copies(tile_copies(refs, ext, sems)))

    @pl.when(step * GROUP < meta[0])
    def work():
        for u in range(GROUP):
            load_window(meta, step * GROUP + u, ext, (0, 1), win, u)
        fields = [times(pair(turned, u), pair(win, u)) for u in range(GROUP)]
        fields = [hop_right(f, tab, 0, False) for f in fields]
        fields = [hop_left(f, tab, 1, False) for f in fields]
        for u, f in enumerate(fields):
            put(f, prop, u)


def second_kernel(meta, own, right, down0_one, down0_two, down1_one, down1_two, corner_one, corner_two, turned_in, hop_in,
                  prop, amp, dft, gown0, gown1, gright, gdown0, gdown1, gcorner, gprobe,
                  ext, gext, acc, turned, hop, win, sems):
    step = pl.program_id(0)
    group = range(GROUP)
    one, two = pl.ds(0, 2), pl.ds(2, 2)
    refs_one = (own.at[one], right.at[one], down0_one, down1_one, corner_one)
    refs_two = (own.at[two], right.at[two], down0_two, down1_two, corner_two)
    copies_one = tile_copies(refs_one, ext.at[:, one], sems.at[0])
    copies_two = tile_copies(refs_two, ext.at[:, two], sems.at[1])
    copy_turned = (turned_in, turned, sems.at[2, 0])
    copy_hop = (hop_in, hop, sems.at[2, 1])

    @pl.when(step == 0)
    def begin():
        started = start_copies(copies_two)
        start_copies([copy_hop] + copies_one + [copy_turned])
        gext[...] = jnp.zeros_like(gext)
        acc[...] = jnp.zeros_like(acc)
        wait_copies(started)

    live = step * GROUP < meta[0]

    @pl.when(live)
    def stage_one():
        for u in group:
            load_window(meta, step * GROUP + u, ext, (2, 3), win, u)
        fields = [times(pair(prop, u), (win[u, 2], win[u, 3])) for u in group]
        fields = [spread_left(half_left(f, dft, 1)) for f in fields]
        fields = [spread_right(half_right(f, dft, 0)) for f in fields]
        chi = []
        for u, f in enumerate(fields):
            factor = 1.0 - amp[u] * lax.rsqrt(f[0] * f[0] + f[1] * f[1] + 1.0)
            chi.append((factor * f[0], factor * f[1]))
        fields = [half_right(gather_right(f), dft, 1) for f in chi]
        fields = [half_left(gather_left(f), dft, 0) for f in fields]
        waves = [conj_times((win[u, 2], win[u, 3]), f) for u, f in enumerate(fields)]
        for u, f in enumerate(fields):
            win[u, 2], win[u, 3] = conj_times(pair(prop, u), f)
        for u, f in enumerate(waves):
            put(f, prop, u)

    @pl.when(step == 0)
    def arrive():
        wait_copies([pltpu.make_async_copy(*copy) for copy in [copy_hop] + copies_one + [copy_turned]])

    @pl.when(live)
    def stage_two():
        for u in group:
            load_window(meta, step * GROUP + u, ext, (0, 1), win, u)
        waves = [hop_left(pair(prop, u), hop, 0, True) for u in group]
        waves = [hop_right(f, hop, 1, True) for f in waves]
        for u, wave in enumerate(waves):
            probe = pair(turned, step * GROUP + u)
            grad, part = conj_times(probe, wave), conj_times(pair(win, u), wave)
            put(grad, win, u)
            put(part, prop, u)

        def finish(slot, u):
            add_window(meta, slot, win, u, range(4), gext)
            add_probe(meta, slot, prop, u, acc)

        for u in group:
            slot = step * GROUP + u
            pl.when(slot < meta[0])(lambda: finish(slot, u))

    @pl.when(step == SLOTS // GROUP - 1)
    def end():
        sem = sems.at[0]
        outs = start_copies([
            (gext.at[1, :, :, pl.ds(W, W)], gdown1, sem.at[0]),
            (gext.at[1, :, :, pl.ds(TC, W)], gcorner, sem.at[1]),
            (gext.at[1, :, :, pl.ds(0, W)], gdown0, sem.at[2]),
            (gext.at[0, :, :, pl.ds(TC, W)], gright, sem.at[3]),
            (gext.at[0, :, :, pl.ds(0, W)], gown0, sem.at[4]),
            (gext.at[0, :, :, pl.ds(W, W)], gown1, sems.at[1, 0]),
        ])
        for p in range(2):
            gprobe[p] = lanes(acc[p, 0, :W, :] + acc[p, 0, W:, :], acc[p, 1, :W, :] + acc[p, 1, W:, :])
        wait_copies(outs)


ANYWHERE = pl.BlockSpec(memory_space=pl.ANY)
WHOLE = pl.BlockSpec(memory_space=pltpu.VMEM)
SCALARS = pl.BlockSpec(memory_space=pltpu.SMEM)
FIELDS = pl.BlockSpec((GROUP, 2, W, W), lambda i: (i, 0, 0, 0))
PLANES = pl.BlockSpec((GROUP, W, W), lambda i: (i, 0, 0))


def shape(*dims):
    return jax.ShapeDtypeStruct(dims, F32)


FIELDS_SHAPE = shape(SLOTS, 2, W, W)


def call(kernel, steps, in_specs, out_specs, out_shape, scratch, products):
    return pl.pallas_call(
        kernel,
        grid=(steps,),
        in_specs=in_specs,
        out_specs=out_specs,
        out_shape=out_shape,
        scratch_shapes=scratch,
        compiler_params=pltpu.CompilerParams(
            vmem_limit_bytes=56 * 2**20, dimension_semantics=("arbitrary",)
        ),
        cost_estimate=pl.CostEstimate(
            flops=SLOTS * products * 2 * W**3, bytes_accessed=12 * 2**20, transcendentals=0
        ),
    )


def prepare_call(*args):
    return call(
        prepare_kernel,
        SLOTS // PREPARED,
        [SCALARS, WHOLE, pl.BlockSpec((PREPARED, W, W), lambda i: (i, 0, 0)), WHOLE],
        [
            pl.BlockSpec((PREPARED, W, W), lambda i: (i, 0, 0)),
            pl.BlockSpec((PREPARED, 2, W, W), lambda i: (i, 0, 0, 0)),
        ],
        [shape(SLOTS, W, W), FIELDS_SHAPE],
        [],
        6,
    )(*args)


def first_call(*args):
    return call(
        first_kernel,
        SLOTS // GROUP,
        [SCALARS] + [ANYWHERE] * 5 + [FIELDS, WHOLE],
        FIELDS,
        FIELDS_SHAPE,
        [
            pltpu.VMEM((2, 2, W, EXT), F32),
            pltpu.VMEM((GROUP, 2, W, W), F32),
            pltpu.SemaphoreType.DMA((5,)),
        ],
        24,
    )(*args)


def second_call(*args):
    return call(
        second_kernel,
        SLOTS // GROUP,
        [SCALARS] + [ANYWHERE] * 10 + [FIELDS, PLANES, WHOLE],
        [ANYWHERE] * 6 + [WHOLE],
        [shape(4, W, W)] * 6 + [shape(2, W, W)],
        [
            pltpu.VMEM((2, 4, W, EXT), F32),
            pltpu.VMEM((2, 4, W, EXT), F32),
            pltpu.VMEM((2, 2, 2 * W, HALF_W), F32),
            pltpu.VMEM((SLOTS, 2, W, W), F32),
            pltpu.VMEM((12, W, W), BF16),
            pltpu.VMEM((GROUP, 4, W, W), F32),
            pltpu.SemaphoreType.DMA((3, 5)),
        ],
        48,
    )(*args)


def shift(value, axis, steps):
    count = lax.axis_size(axis)
    first, last = (max(0, -steps), min(count, count - steps))
    return lax.ppermute(value, axis, [(source, source + steps) for source in range(first, last)])


def add_shares(value, axis):
    count = lax.axis_size(axis)
    shares = value.reshape(count, -1, value.shape[-1])
    return lax.all_to_all(shares, axis, 0, 0, tiled=True).sum(axis=0)


def hand_out(value, axis):
    spread = jnp.broadcast_to(value[None], (lax.axis_size(axis), *value.shape))
    return lax.all_to_all(spread, axis, 0, 0, tiled=True)


def probe_twice(probe):
    halves = probe.reshape(2, W, 2, HALF_W).transpose(0, 2, 1, 3)
    return jnp.concatenate([halves, halves], axis=2)


def body(object_slab, probe_wave, scan_offsets, live_counts, amplitudes):
    rows_tile, cols_tile = object_slab.shape[1:]
    local_rows = scan_offsets[:, 0] - lax.axis_index("row") * rows_tile
    local_cols = scan_offsets[:, 1] - lax.axis_index("col") * cols_tile
    meta = jnp.concatenate([live_counts, local_rows, local_cols])
    hop, dft, fold = jnp.asarray(hop_tables()), jnp.asarray(dft_tables()), jnp.asarray(fold_tables())
    twice = probe_twice(probe_wave)
    down0_one = shift(object_slab[:2, :, :W], "row", -1)
    down1_one = shift(object_slab[:2, :, W:], "row", -1)
    right = shift(object_slab[:, :, :W], "col", -1)
    down0_two = shift(object_slab[2:, :, :W], "row", -1)
    down0_one, last_part = lax.optimization_barrier((down0_one, object_slab[2:, :, W:]))
    down1_two = shift(last_part, "row", -1)
    corner_one = shift(down0_one, "col", -1)
    amp, turned = prepare_call(meta, twice, amplitudes, fold)
    prop = first_call(meta, object_slab, right, down0_one, down1_one, corner_one, turned, hop)
    down0_two, prop = lax.optimization_barrier((down0_two, prop))
    corner_two = shift(down0_two, "col", -1)
    gown0, gown1, gright, gdown0, gdown1, gcorner, gprobe = second_call(
        meta, object_slab, right, down0_one, down0_two, down1_one, down1_two, corner_one, corner_two, turned, hop,
        prop, amp, dft,
    )
    corner_back = shift(gcorner, "col", 1)
    down1_back = shift(gdown1, "row", 1)
    share = add_shares(gprobe, "row")
    gdown0, gright, share = lax.optimization_barrier((gdown0 + corner_back, gright, share))
    down0_back = shift(gdown0, "row", 1)
    right_back = shift(gright, "col", 1)
    share = hand_out(share, "col").sum(axis=0)
    own0, own1 = lax.optimization_barrier((gown0 + right_back, gown1 + down1_back))
    probe_grad = hand_out(share, "row").reshape(probe_wave.shape)
    object_grad = jnp.concatenate([own0 + down0_back, own1], axis=2)
    return object_grad, probe_grad


def solution(mesh):
    return jax.shard_map(
        body,
        mesh=mesh,
        in_specs=(
            P(None, "row", "col"),
            P(),
            P(("row", "col"), None),
            P(("row", "col")),
            P(("row", "col"), None, None),
        ),
        out_specs=(P(None, "row", "col"), P()),
        check_vma=False,
    )
```

```python
import math

import jax
import jax.numpy as jnp
import ml_dtypes
import numpy as np
from jax import lax
from jax.experimental import pallas as pl
from jax.experimental.pallas import tpu as pltpu
from jax.sharding import PartitionSpec as P

W = 256
HALF_W = 128
TC = 512
EXT = TC + W
SLOTS = 8
GROUP = 4
PREPARED = 2
CHUNK = 32
F32 = jnp.float32
BF16 = jnp.bfloat16

RE, IM, NEG_IM = 0, 1, 2


def split_host(table):
    high = table.astype(np.float32).astype(ml_dtypes.bfloat16)
    low = (table - high.astype(np.float64)).astype(np.float32).astype(ml_dtypes.bfloat16)
    return [high, low]


def hop_tables():
    index = np.arange(W)
    dft = np.exp(-2j * np.pi / W * (index[:, None] * index[None, :] % W)) / math.sqrt(W)
    freqs = np.where(index < W // 2, index, index - W) / W
    fresnel = np.exp(-1j * np.pi * (W / 4.0) * freqs**2)
    hop = np.conj(dft) @ (fresnel[:, None] * dft)
    hop = hop * np.exp(1j * np.pi * index / W)
    out = []
    for table in (hop, hop.T):
        for part in (table.real, table.imag, -table.imag):
            out.extend(split_host(part))
    return np.stack(out)


def dft_tables():
    index = np.arange(W)
    angles = 2.0 * np.pi / W * (index[:, None] + 0.5) * (index[None, :HALF_W] + 0.5)
    table = np.concatenate([np.cos(angles), np.sin(angles)], axis=1) / math.sqrt(W)
    return np.stack(split_host(table) + split_host(table.T))


def fold_tables():
    source = np.concatenate([np.arange(HALF_W), np.arange(W - 1, HALF_W - 1, -1)])
    table = np.zeros((W, W), np.float32)
    table[source, np.arange(W)] = 1.0
    return np.stack([table, table.T]).astype(ml_dtypes.bfloat16)


def split(x):
    high = x.astype(BF16)
    return high, (x - high.astype(F32)).astype(BF16)


def lanes(*parts):
    return jnp.concatenate(parts, axis=1)


def rows(*parts):
    return jnp.concatenate(parts, axis=0)


def dot(a, b):
    return jnp.dot(a, b, preferred_element_type=F32)


def half_right(field, tab, at):
    high, low = tab[2 * at], tab[2 * at + 1]
    rh, rl = split(field[0])
    ih, il = split(field[1])
    out = dot(rows(lanes(rh, rl, rh), lanes(ih, il, ih)), rows(high, high, low))
    return out[:W], out[W:]


def half_left(field, tab, at):
    high, low = tab[2 * at], tab[2 * at + 1]
    rh, rl = split(field[0])
    ih, il = split(field[1])
    out = dot(lanes(high, high, low), lanes(rows(rh, rl, rh), rows(ih, il, ih)))
    return out[:, :W], out[:, W:]


def hop_parts(tab, at, conj):
    im, neg = (IM, NEG_IM) if not conj else (NEG_IM, IM)

    def three(a, b):
        a, b = 2 * (3 * at + a), 2 * (3 * at + b)
        return [tab[a], tab[b], tab[a], tab[b], tab[a + 1], tab[b + 1]]

    return three(RE, neg), three(im, RE)


def hop_right(field, tab, at, conj):
    rh, rl = split(field[0])
    ih, il = split(field[1])
    to_re, to_im = hop_parts(tab, at, conj)
    out = dot(lanes(rh, ih, rl, il, rh, ih), lanes(rows(*to_re), rows(*to_im)))
    return out[:, :W], out[:, W:]


def hop_left(field, tab, at, conj):
    rh, rl = split(field[0])
    ih, il = split(field[1])
    to_re, to_im = hop_parts(tab, at, conj)
    out = dot(rows(lanes(*to_re), lanes(*to_im)), rows(rh, ih, rl, il, rh, ih))
    return out[:W], out[W:]


def spread_right(field):
    c, s = field[0][:, :HALF_W], field[0][:, HALF_W:]
    d, t = field[1][:, :HALF_W], field[1][:, HALF_W:]
    return lanes(c + t, t - c), lanes(d - s, -d - s)


def spread_left(field):
    c, s = field[0][:HALF_W], field[0][HALF_W:]
    d, t = field[1][:HALF_W], field[1][HALF_W:]
    return rows(c + t, t - c), rows(d - s, -d - s)


def gather_right(field):
    a, b = field[0][:, :HALF_W], field[0][:, HALF_W:]
    c, d = field[1][:, :HALF_W], field[1][:, HALF_W:]
    return lanes(a - b, -c - d), lanes(c - d, a + b)


def gather_left(field):
    a, b = field[0][:HALF_W], field[0][HALF_W:]
    c, d = field[1][:HALF_W], field[1][HALF_W:]
    return rows(a - b, -c - d), rows(c - d, a + b)


def times(a, b):
    return a[0] * b[0] - a[1] * b[1], a[0] * b[1] + a[1] * b[0]


def conj_times(a, b):
    return a[0] * b[0] + a[1] * b[1], a[0] * b[1] - a[1] * b[0]


def pair(ref, *at):
    return ref[(*at, 0)], ref[(*at, 1)]


def put(value, ref, *at):
    ref[(*at, 0)], ref[(*at, 1)] = value


def chunks(body):
    def step(i, carry):
        body(pl.multiple_of(i * CHUNK, CHUNK))
        return carry

    lax.fori_loop(0, W // CHUNK, step, 0)


def geometry(meta, slot):
    row, col = meta[1 + slot], meta[1 + SLOTS + slot]
    block = col // W
    first = pl.multiple_of(block * W, W)
    second = pl.multiple_of(block * W + W, W)
    return row, col - block * W, first, second


def masks(row, col, at):
    in_top = lax.broadcasted_iota(jnp.int32, (CHUNK, W), 0) + at >= row
    in_first = lax.broadcasted_iota(jnp.int32, (CHUNK, W), 1) >= col
    return in_top, in_first


def load_window(meta, slot, ext, planes, win, u):
    row, col, first, second = geometry(meta, slot)
    border = row // CHUNK

    def load(i, carry):
        here = pl.ds(pl.multiple_of(i * CHUNK, CHUNK), CHUNK)
        _, in_first = masks(row, col, 0)
        low = (i < border).astype(jnp.int32)
        for p in planes:
            win[u, p, here, :] = jnp.where(
                in_first, ext[low, p, here, pl.ds(first, W)], ext[low, p, here, pl.ds(second, W)]
            )
        return carry

    lax.fori_loop(0, W // CHUNK, load, 0, unroll=2)
    at = pl.multiple_of(border * CHUNK, CHUNK)
    here = pl.ds(at, CHUNK)
    in_top, in_first = masks(row, col, at)
    for p in planes:
        low = jnp.where(in_first, ext[1, p, here, pl.ds(first, W)], ext[1, p, here, pl.ds(second, W)])
        win[u, p, here, :] = jnp.where(in_top, win[u, p, here, :], low)


def add_window(meta, slot, win, u, planes, gext):
    row, col, first, second = geometry(meta, slot)
    border = row // CHUNK
    zero = jnp.zeros((CHUNK, W), F32)

    def add(i, carry):
        at = pl.multiple_of(i * CHUNK, CHUNK)
        here = pl.ds(at, CHUNK)
        in_top, in_first = masks(row, col, at)
        low = (i < border).astype(jnp.int32)
        keep = jnp.logical_or(in_top, i < border)
        for p in planes:
            value = jnp.where(keep, win[u, p, here, :], zero)
            gext[low, p, here, pl.ds(first, W)] += jnp.where(in_first, value, zero)
            gext[low, p, here, pl.ds(second, W)] += jnp.where(in_first, zero, value)
        return carry

    lax.fori_loop(0, W // CHUNK, add, 0, unroll=2)
    at = pl.multiple_of(border * CHUNK, CHUNK)
    here = pl.ds(at, CHUNK)
    in_top, in_first = masks(row, col, at)
    for p in planes:
        value = jnp.where(in_top, zero, win[u, p, here, :])
        gext[1, p, here, pl.ds(first, W)] += jnp.where(in_first, value, zero)
        gext[1, p, here, pl.ds(second, W)] += jnp.where(in_first, zero, value)


def turn_probe(meta, slot, twice, turned, u):
    row, col, _, _ = geometry(meta, slot)
    for p in range(2):
        here = pl.ds(W - row, W)
        turned[u, p] = pltpu.roll(lanes(twice[p, 0, here, :], twice[p, 1, here, :]), col, 1)


def add_probe(meta, slot, part, u, acc):
    row, col, _, _ = geometry(meta, slot)
    for p in range(2):
        here = pl.ds(W - row, W)
        value = pltpu.roll(part[u, p], W - col, 1)
        acc[p, 0, here, :] += value[:, :HALF_W]
        acc[p, 1, here, :] += value[:, HALF_W:]


def tile_copies(refs, ext, sems):
    own, right, down0, down1, corner = refs
    return [
        (own, ext.at[0, :, :, pl.ds(0, TC)], sems.at[0]),
        (right, ext.at[0, :, :, pl.ds(TC, W)], sems.at[1]),
        (down0, ext.at[1, :, :, pl.ds(0, W)], sems.at[2]),
        (down1, ext.at[1, :, :, pl.ds(W, W)], sems.at[3]),
        (corner, ext.at[1, :, :, pl.ds(TC, W)], sems.at[4]),
    ]


def start_copies(copies):
    copies = [pltpu.make_async_copy(*copy) for copy in copies]
    for copy in copies:
        copy.start()
    return copies


def wait_copies(copies):
    for copy in copies:
        copy.wait()


def prepare_kernel(meta, twice, amp, fold, amp_out, turned):
    step = pl.program_id(0)

    def fold_amplitudes(u):
        high = amp[u].astype(BF16)
        rest = amp[u] - high.astype(F32)
        mid = rest.astype(BF16)
        low = (rest - mid.astype(F32)).astype(BF16)
        right_way = dot(rows(high, mid, low), fold[0])
        out = dot(fold[1], lanes(*(right_way[i * W : (i + 1) * W].astype(BF16) for i in range(3))))
        amp_out[u] = out[:, :W] + out[:, W : 2 * W] + out[:, 2 * W :]

    for u in range(PREPARED):
        fold_amplitudes(u)
        turn_probe(meta, step * PREPARED + u, twice, turned, u)


def first_kernel(meta, own, right, down0, down1, corner, turned, tab, prop, ext, win, sems):
    step = pl.program_id(0)

    @pl.when(step == 0)
    def begin():
        refs = (own.at[pl.ds(0, 2)], right.at[pl.ds(0, 2)], down0, down1, corner)
        wait_copies(start_copies(tile_copies(refs, ext, sems)))

    @pl.when(step * GROUP < meta[0])
    def work():
        for u in range(GROUP):
            load_window(meta, step * GROUP + u, ext, (0, 1), win, u)
        fields = [times(pair(turned, u), pair(win, u)) for u in range(GROUP)]
        fields = [hop_right(f, tab, 0, False) for f in fields]
        fields = [hop_left(f, tab, 1, False) for f in fields]
        for u, f in enumerate(fields):
            put(f, prop, u)


def second_kernel(meta, own, right, down0_one, down0_two, down1_one, down1_two, corner_one, corner_two, turned_in, hop_in,
                  prop, amp, dft, gown0, gown1, gright, gdown0, gdown1, gcorner, gprobe,
                  ext, gext, acc, turned, hop, win, sems):
    step = pl.program_id(0)
    group = range(GROUP)
    one, two = pl.ds(0, 2), pl.ds(2, 2)
    refs_one = (own.at[one], right.at[one], down0_one, down1_one, corner_one)
    refs_two = (own.at[two], right.at[two], down0_two, down1_two, corner_two)
    copies_one = tile_copies(refs_one, ext.at[:, one], sems.at[0])
    copies_two = tile_copies(refs_two, ext.at[:, two], sems.at[1])
    copy_turned = (turned_in, turned, sems.at[2, 0])
    copy_hop = (hop_in, hop, sems.at[2, 1])

    @pl.when(step == 0)
    def begin():
        started = start_copies(copies_two)
        start_copies([copy_hop] + copies_one + [copy_turned])
        gext[...] = jnp.zeros_like(gext)
        acc[...] = jnp.zeros_like(acc)
        wait_copies(started)

    live = step * GROUP < meta[0]

    @pl.when(live)
    def stage_one():
        for u in group:
            load_window(meta, step * GROUP + u, ext, (2, 3), win, u)
        fields = [times(pair(prop, u), (win[u, 2], win[u, 3])) for u in group]
        fields = [spread_left(half_left(f, dft, 1)) for f in fields]
        fields = [spread_right(half_right(f, dft, 0)) for f in fields]
        chi = []
        for u, f in enumerate(fields):
            factor = 1.0 - amp[u] * lax.rsqrt(f[0] * f[0] + f[1] * f[1] + 1.0)
            chi.append((factor * f[0], factor * f[1]))
        fields = [half_right(gather_right(f), dft, 1) for f in chi]
        fields = [half_left(gather_left(f), dft, 0) for f in fields]
        waves = [conj_times((win[u, 2], win[u, 3]), f) for u, f in enumerate(fields)]
        for u, f in enumerate(fields):
            win[u, 2], win[u, 3] = conj_times(pair(prop, u), f)
        for u, f in enumerate(waves):
            put(f, prop, u)

    @pl.when(step == 0)
    def arrive():
        wait_copies([pltpu.make_async_copy(*copy) for copy in [copy_hop] + copies_one + [copy_turned]])

    @pl.when(live)
    def stage_two():
        for u in group:
            load_window(meta, step * GROUP + u, ext, (0, 1), win, u)
        waves = [hop_left(pair(prop, u), hop, 0, True) for u in group]
        waves = [hop_right(f, hop, 1, True) for f in waves]
        for u, wave in enumerate(waves):
            probe = pair(turned, step * GROUP + u)
            grad, part = conj_times(probe, wave), conj_times(pair(win, u), wave)
            put(grad, win, u)
            put(part, prop, u)

        def finish(slot, u):
            add_window(meta, slot, win, u, range(4), gext)
            add_probe(meta, slot, prop, u, acc)

        for u in group:
            slot = step * GROUP + u
            pl.when(slot < meta[0])(lambda: finish(slot, u))

    @pl.when(step == SLOTS // GROUP - 1)
    def end():
        sem = sems.at[0]
        outs = start_copies([
            (gext.at[1, :, :, pl.ds(W, W)], gdown1, sem.at[0]),
            (gext.at[1, :, :, pl.ds(TC, W)], gcorner, sem.at[1]),
            (gext.at[1, :, :, pl.ds(0, W)], gdown0, sem.at[2]),
            (gext.at[0, :, :, pl.ds(TC, W)], gright, sem.at[3]),
            (gext.at[0, :, :, pl.ds(0, W)], gown0, sem.at[4]),
            (gext.at[0, :, :, pl.ds(W, W)], gown1, sems.at[1, 0]),
        ])
        for p in range(2):
            gprobe[p] = lanes(acc[p, 0, :W, :] + acc[p, 0, W:, :], acc[p, 1, :W, :] + acc[p, 1, W:, :])
        wait_copies(outs)


ANYWHERE = pl.BlockSpec(memory_space=pl.ANY)
WHOLE = pl.BlockSpec(memory_space=pltpu.VMEM)
SCALARS = pl.BlockSpec(memory_space=pltpu.SMEM)
FIELDS = pl.BlockSpec((GROUP, 2, W, W), lambda i: (i, 0, 0, 0))
PLANES = pl.BlockSpec((GROUP, W, W), lambda i: (i, 0, 0))


def shape(*dims):
    return jax.ShapeDtypeStruct(dims, F32)


FIELDS_SHAPE = shape(SLOTS, 2, W, W)


def call(kernel, steps, in_specs, out_specs, out_shape, scratch, products):
    return pl.pallas_call(
        kernel,
        grid=(steps,),
        in_specs=in_specs,
        out_specs=out_specs,
        out_shape=out_shape,
        scratch_shapes=scratch,
        compiler_params=pltpu.CompilerParams(
            vmem_limit_bytes=56 * 2**20, dimension_semantics=("arbitrary",)
        ),
        cost_estimate=pl.CostEstimate(
            flops=SLOTS * products * 2 * W**3, bytes_accessed=12 * 2**20, transcendentals=0
        ),
    )


def prepare_call(*args):
    return call(
        prepare_kernel,
        SLOTS // PREPARED,
        [SCALARS, WHOLE, pl.BlockSpec((PREPARED, W, W), lambda i: (i, 0, 0)), WHOLE],
        [
            pl.BlockSpec((PREPARED, W, W), lambda i: (i, 0, 0)),
            pl.BlockSpec((PREPARED, 2, W, W), lambda i: (i, 0, 0, 0)),
        ],
        [shape(SLOTS, W, W), FIELDS_SHAPE],
        [],
        6,
    )(*args)


def first_call(*args):
    return call(
        first_kernel,
        SLOTS // GROUP,
        [SCALARS] + [ANYWHERE] * 5 + [FIELDS, WHOLE],
        FIELDS,
        FIELDS_SHAPE,
        [
            pltpu.VMEM((2, 2, W, EXT), F32),
            pltpu.VMEM((GROUP, 2, W, W), F32),
            pltpu.SemaphoreType.DMA((5,)),
        ],
        24,
    )(*args)


def second_call(*args):
    return call(
        second_kernel,
        SLOTS // GROUP,
        [SCALARS] + [ANYWHERE] * 10 + [FIELDS, PLANES, WHOLE],
        [ANYWHERE] * 6 + [WHOLE],
        [shape(4, W, W)] * 6 + [shape(2, W, W)],
        [
            pltpu.VMEM((2, 4, W, EXT), F32),
            pltpu.VMEM((2, 4, W, EXT), F32),
            pltpu.VMEM((2, 2, 2 * W, HALF_W), F32),
            pltpu.VMEM((SLOTS, 2, W, W), F32),
            pltpu.VMEM((12, W, W), BF16),
            pltpu.VMEM((GROUP, 4, W, W), F32),
            pltpu.SemaphoreType.DMA((3, 5)),
        ],
        48,
    )(*args)


def shift(value, axis, steps):
    count = lax.axis_size(axis)
    first, last = (max(0, -steps), min(count, count - steps))
    return lax.ppermute(value, axis, [(source, source + steps) for source in range(first, last)])


def add_shares(value, axis):
    count = lax.axis_size(axis)
    shares = value.reshape(count, -1, value.shape[-1])
    return lax.all_to_all(shares, axis, 0, 0, tiled=True).sum(axis=0)


def hand_out(value, axis):
    spread = jnp.broadcast_to(value[None], (lax.axis_size(axis), *value.shape))
    return lax.all_to_all(spread, axis, 0, 0, tiled=True)


def probe_twice(probe):
    halves = probe.reshape(2, W, 2, HALF_W).transpose(0, 2, 1, 3)
    return jnp.concatenate([halves, halves], axis=2)


def body(object_slab, probe_wave, scan_offsets, live_counts, amplitudes):
    rows_tile, cols_tile = object_slab.shape[1:]
    local_rows = scan_offsets[:, 0] - lax.axis_index("row") * rows_tile
    local_cols = scan_offsets[:, 1] - lax.axis_index("col") * cols_tile
    meta = jnp.concatenate([live_counts, local_rows, local_cols])
    hop, dft, fold = jnp.asarray(hop_tables()), jnp.asarray(dft_tables()), jnp.asarray(fold_tables())
    twice = probe_twice(probe_wave)
    down0_one = shift(object_slab[:2, :, :W], "row", -1)
    down1_one = shift(object_slab[:2, :, W:], "row", -1)
    right = shift(object_slab[:, :, :W], "col", -1)
    down0_two = shift(object_slab[2:, :, :W], "row", -1)
    down0_one, last_part = lax.optimization_barrier((down0_one, object_slab[2:, :, W:]))
    down1_two = shift(last_part, "row", -1)
    corner_one = shift(down0_one, "col", -1)
    amp, turned = prepare_call(meta, twice, amplitudes, fold)
    prop = first_call(meta, object_slab, right, down0_one, down1_one, corner_one, turned, hop)
    down0_two, prop = lax.optimization_barrier((down0_two, prop))
    corner_two = shift(down0_two, "col", -1)
    gown0, gown1, gright, gdown0, gdown1, gcorner, gprobe = second_call(
        meta, object_slab, right, down0_one, down0_two, down1_one, down1_two, corner_one, corner_two, turned, hop,
        prop, amp, dft,
    )
    corner_back = shift(gcorner, "col", 1)
    share = add_shares(gprobe, "row")
    gdown0, gdown1, gright, share = lax.optimization_barrier((gdown0, gdown1, gright, share))
    down1_back = shift(gdown1, "row", 1)
    down0_back = shift(gdown0 + corner_back, "row", 1)
    right_back = shift(gright, "col", 1)
    share = hand_out(share, "col").sum(axis=0)
    own0, own1 = lax.optimization_barrier((gown0 + right_back, gown1 + down1_back))
    probe_grad = hand_out(share, "row").reshape(probe_wave.shape)
    object_grad = jnp.concatenate([own0 + down0_back, own1], axis=2)
    return object_grad, probe_grad


def solution(mesh):
    return jax.shard_map(
        body,
        mesh=mesh,
        in_specs=(
            P(None, "row", "col"),
            P(),
            P(("row", "col"), None),
            P(("row", "col")),
            P(("row", "col"), None, None),
        ),
        out_specs=(P(None, "row", "col"), P()),
        check_vma=False,
    )
```

```python
import math

import jax
import jax.numpy as jnp
import ml_dtypes
import numpy as np
from jax import lax
from jax.experimental import pallas as pl
from jax.experimental.pallas import tpu as pltpu
from jax.sharding import PartitionSpec as P

W = 256
HALF_W = 128
TC = 512
EXT = TC + W
SLOTS = 8
GROUP = 4
PREPARED = 2
CHUNK = 32
F32 = jnp.float32
BF16 = jnp.bfloat16

RE, IM, NEG_IM = 0, 1, 2


def split_host(table):
    high = table.astype(np.float32).astype(ml_dtypes.bfloat16)
    low = (table - high.astype(np.float64)).astype(np.float32).astype(ml_dtypes.bfloat16)
    return [high, low]


def hop_tables():
    index = np.arange(W)
    dft = np.exp(-2j * np.pi / W * (index[:, None] * index[None, :] % W)) / math.sqrt(W)
    freqs = np.where(index < W // 2, index, index - W) / W
    fresnel = np.exp(-1j * np.pi * (W / 4.0) * freqs**2)
    hop = np.conj(dft) @ (fresnel[:, None] * dft)
    hop = hop * np.exp(1j * np.pi * index / W)
    out = []
    for table in (hop, hop.T):
        for part in (table.real, table.imag, -table.imag):
            out.extend(split_host(part))
    return np.stack(out)


def dft_tables():
    index = np.arange(W)
    angles = 2.0 * np.pi / W * (index[:, None] + 0.5) * (index[None, :HALF_W] + 0.5)
    table = np.concatenate([np.cos(angles), np.sin(angles)], axis=1) / math.sqrt(W)
    return np.stack(split_host(table) + split_host(table.T))


def fold_tables():
    source = np.concatenate([np.arange(HALF_W), np.arange(W - 1, HALF_W - 1, -1)])
    table = np.zeros((W, W), np.float32)
    table[source, np.arange(W)] = 1.0
    return np.stack([table, table.T]).astype(ml_dtypes.bfloat16)


def split(x):
    high = x.astype(BF16)
    return high, (x - high.astype(F32)).astype(BF16)


def lanes(*parts):
    return jnp.concatenate(parts, axis=1)


def rows(*parts):
    return jnp.concatenate(parts, axis=0)


def dot(a, b):
    return jnp.dot(a, b, preferred_element_type=F32)


def half_right(field, tab, at):
    high, low = tab[2 * at], tab[2 * at + 1]
    rh, rl = split(field[0])
    ih, il = split(field[1])
    out = dot(rows(lanes(rh, rl, rh), lanes(ih, il, ih)), rows(high, high, low))
    return out[:W], out[W:]


def half_left(field, tab, at):
    high, low = tab[2 * at], tab[2 * at + 1]
    rh, rl = split(field[0])
    ih, il = split(field[1])
    out = dot(lanes(high, high, low), lanes(rows(rh, rl, rh), rows(ih, il, ih)))
    return out[:, :W], out[:, W:]


def hop_parts(tab, at, conj):
    im, neg = (IM, NEG_IM) if not conj else (NEG_IM, IM)

    def three(a, b):
        a, b = 2 * (3 * at + a), 2 * (3 * at + b)
        return [tab[a], tab[b], tab[a], tab[b], tab[a + 1], tab[b + 1]]

    return three(RE, neg), three(im, RE)


def hop_right(field, tab, at, conj):
    rh, rl = split(field[0])
    ih, il = split(field[1])
    to_re, to_im = hop_parts(tab, at, conj)
    out = dot(lanes(rh, ih, rl, il, rh, ih), lanes(rows(*to_re), rows(*to_im)))
    return out[:, :W], out[:, W:]


def hop_left(field, tab, at, conj):
    rh, rl = split(field[0])
    ih, il = split(field[1])
    to_re, to_im = hop_parts(tab, at, conj)
    out = dot(rows(lanes(*to_re), lanes(*to_im)), rows(rh, ih, rl, il, rh, ih))
    return out[:W], out[W:]


def spread_right(field):
    c, s = field[0][:, :HALF_W], field[0][:, HALF_W:]
    d, t = field[1][:, :HALF_W], field[1][:, HALF_W:]
    return lanes(c + t, t - c), lanes(d - s, -d - s)


def spread_left(field):
    c, s = field[0][:HALF_W], field[0][HALF_W:]
    d, t = field[1][:HALF_W], field[1][HALF_W:]
    return rows(c + t, t - c), rows(d - s, -d - s)


def gather_right(field):
    a, b = field[0][:, :HALF_W], field[0][:, HALF_W:]
    c, d = field[1][:, :HALF_W], field[1][:, HALF_W:]
    return lanes(a - b, -c - d), lanes(c - d, a + b)


def gather_left(field):
    a, b = field[0][:HALF_W], field[0][HALF_W:]
    c, d = field[1][:HALF_W], field[1][HALF_W:]
    return rows(a - b, -c - d), rows(c - d, a + b)


def times(a, b):
    return a[0] * b[0] - a[1] * b[1], a[0] * b[1] + a[1] * b[0]


def conj_times(a, b):
    return a[0] * b[0] + a[1] * b[1], a[0] * b[1] - a[1] * b[0]


def pair(ref, *at):
    return ref[(*at, 0)], ref[(*at, 1)]


def put(value, ref, *at):
    ref[(*at, 0)], ref[(*at, 1)] = value


def chunks(body):
    def step(i, carry):
        body(pl.multiple_of(i * CHUNK, CHUNK))
        return carry

    lax.fori_loop(0, W // CHUNK, step, 0)


def geometry(meta, slot):
    row, col = meta[1 + slot], meta[1 + SLOTS + slot]
    block = col // W
    first = pl.multiple_of(block * W, W)
    second = pl.multiple_of(block * W + W, W)
    return row, col - block * W, first, second


def masks(row, col, at):
    in_top = lax.broadcasted_iota(jnp.int32, (CHUNK, W), 0) + at >= row
    in_first = lax.broadcasted_iota(jnp.int32, (CHUNK, W), 1) >= col
    return in_top, in_first


def load_window(meta, slot, ext, planes, win, u):
    row, col, first, second = geometry(meta, slot)
    border = row // CHUNK

    def load(i, carry):
        here = pl.ds(pl.multiple_of(i * CHUNK, CHUNK), CHUNK)
        _, in_first = masks(row, col, 0)
        low = (i < border).astype(jnp.int32)
        for p in planes:
            win[u, p, here, :] = jnp.where(
                in_first, ext[low, p, here, pl.ds(first, W)], ext[low, p, here, pl.ds(second, W)]
            )
        return carry

    lax.fori_loop(0, W // CHUNK, load, 0, unroll=True)
    at = pl.multiple_of(border * CHUNK, CHUNK)
    here = pl.ds(at, CHUNK)
    in_top, in_first = masks(row, col, at)
    for p in planes:
        low = jnp.where(in_first, ext[1, p, here, pl.ds(first, W)], ext[1, p, here, pl.ds(second, W)])
        win[u, p, here, :] = jnp.where(in_top, win[u, p, here, :], low)


def add_window(meta, slot, win, u, planes, gext):
    row, col, first, second = geometry(meta, slot)
    border = row // CHUNK
    zero = jnp.zeros((CHUNK, W), F32)
    alive = slot < meta[0]

    def add(i, carry):
        at = pl.multiple_of(i * CHUNK, CHUNK)
        here = pl.ds(at, CHUNK)
        in_top, in_first = masks(row, col, at)
        low = (i < border).astype(jnp.int32)
        keep = jnp.logical_and(jnp.logical_or(in_top, i < border), alive)
        for p in planes:
            value = jnp.where(keep, win[u, p, here, :], zero)
            gext[low, p, here, pl.ds(first, W)] += jnp.where(in_first, value, zero)
            gext[low, p, here, pl.ds(second, W)] += jnp.where(in_first, zero, value)
        return carry

    lax.fori_loop(0, W // CHUNK, add, 0, unroll=True)
    at = pl.multiple_of(border * CHUNK, CHUNK)
    here = pl.ds(at, CHUNK)
    in_top, in_first = masks(row, col, at)
    for p in planes:
        value = jnp.where(jnp.logical_and(jnp.logical_not(in_top), alive), win[u, p, here, :], zero)
        gext[1, p, here, pl.ds(first, W)] += jnp.where(in_first, value, zero)
        gext[1, p, here, pl.ds(second, W)] += jnp.where(in_first, zero, value)


def turn_probe(meta, slot, twice, turned, u):
    row, col, _, _ = geometry(meta, slot)
    for p in range(2):
        here = pl.ds(W - row, W)
        turned[u, p] = pltpu.roll(lanes(twice[p, 0, here, :], twice[p, 1, here, :]), col, 1)


def add_probe(meta, slot, part, u, acc):
    row, col, _, _ = geometry(meta, slot)
    for p in range(2):
        here = pl.ds(W - row, W)
        value = jnp.where(slot < meta[0], pltpu.roll(part[u, p], W - col, 1), 0.0)
        acc[p, 0, here, :] += value[:, :HALF_W]
        acc[p, 1, here, :] += value[:, HALF_W:]


def tile_copies(refs, ext, sems):
    own, right, down0, down1, corner = refs
    return [
        (own, ext.at[0, :, :, pl.ds(0, TC)], sems.at[0]),
        (right, ext.at[0, :, :, pl.ds(TC, W)], sems.at[1]),
        (down0, ext.at[1, :, :, pl.ds(0, W)], sems.at[2]),
        (down1, ext.at[1, :, :, pl.ds(W, W)], sems.at[3]),
        (corner, ext.at[1, :, :, pl.ds(TC, W)], sems.at[4]),
    ]


def start_copies(copies):
    copies = [pltpu.make_async_copy(*copy) for copy in copies]
    for copy in copies:
        copy.start()
    return copies


def wait_copies(copies):
    for copy in copies:
        copy.wait()


def prepare_kernel(meta, probe, amp, fold, amp_out, turned, twice):
    step = pl.program_id(0)

    def fold_amplitudes(u):
        high = amp[u].astype(BF16)
        rest = amp[u] - high.astype(F32)
        mid = rest.astype(BF16)
        low = (rest - mid.astype(F32)).astype(BF16)
        right_way = dot(rows(high, mid, low), fold[0])
        out = dot(fold[1], lanes(*(right_way[i * W : (i + 1) * W].astype(BF16) for i in range(3))))
        amp_out[u] = out[:, :W] + out[:, W : 2 * W] + out[:, 2 * W :]

    @pl.when(step == 0)
    def double_probe():
        for p in range(2):
            for half in range(2):
                part = probe[p, :, half * HALF_W : (half + 1) * HALF_W]
                twice[p, half, :W, :] = part
                twice[p, half, W:, :] = part

    for u in range(PREPARED):
        fold_amplitudes(u)
        turn_probe(meta, step * PREPARED + u, twice, turned, u)


def first_kernel(meta, own, right, down0, down1, corner, turned, tab, prop, ext, win, sems):
    step = pl.program_id(0)

    @pl.when(step == 0)
    def begin():
        one = pl.ds(0, 2)
        refs = (own.at[one], right.at[one], down0, down1, corner)
        wait_copies(start_copies(tile_copies(refs, ext, sems)))

    @pl.when(step * GROUP < meta[0])
    def work():
        for u in range(GROUP):
            load_window(meta, step * GROUP + u, ext, (0, 1), win, u)
        fields = [times(pair(turned, u), pair(win, u)) for u in range(GROUP)]
        fields = [hop_right(f, tab, 0, False) for f in fields]
        fields = [hop_left(f, tab, 1, False) for f in fields]
        for u, f in enumerate(fields):
            put(f, prop, u)


def second_kernel(meta, own, right, down0_one, down0_two, down1_one, corner_one, turned_in, hop_in, down1_two, corner_two,
                  prop, amp, dft, gown, gright, gdown0, gdown1, gcorner, gprobe,
                  ext, gext, acc, turned, hop, win, sems):
    step = pl.program_id(0)
    group = range(GROUP)
    one, two = pl.ds(0, 2), pl.ds(2, 2)
    refs_one = (own.at[one], right.at[one], down0_one, down1_one, corner_one)
    refs_two = (own.at[two], right.at[two], down0_two, down1_two, corner_two)
    copies_one = tile_copies(refs_one, ext.at[:, one], sems.at[0])
    copies_two = tile_copies(refs_two, ext.at[:, two], sems.at[1])
    copy_turned = (turned_in, turned, sems.at[2, 0])
    copy_hop = (hop_in, hop, sems.at[2, 1])

    @pl.when(step == 0)
    def begin():
        started = start_copies(copies_two)
        start_copies([copy_hop] + copies_one + [copy_turned])
        gext[...] = jnp.zeros_like(gext)
        acc[...] = jnp.zeros_like(acc)
        wait_copies(started)

    live = step * GROUP < meta[0]

    @pl.when(live)
    def stage_one():
        for u in group:
            load_window(meta, step * GROUP + u, ext, (2, 3), win, u)
        fields = [times(pair(prop, u), (win[u, 2], win[u, 3])) for u in group]
        fields = [spread_left(half_left(f, dft, 1)) for f in fields]
        fields = [spread_right(half_right(f, dft, 0)) for f in fields]
        chi = []
        for u, f in enumerate(fields):
            factor = 1.0 - amp[u] * lax.rsqrt(f[0] * f[0] + f[1] * f[1] + 1.0)
            chi.append((factor * f[0], factor * f[1]))
        fields = [half_right(gather_right(f), dft, 1) for f in chi]
        fields = [half_left(gather_left(f), dft, 0) for f in fields]
        waves = [conj_times((win[u, 2], win[u, 3]), f) for u, f in enumerate(fields)]
        for u, f in enumerate(fields):
            win[u, 2], win[u, 3] = conj_times(pair(prop, u), f)
        for u, f in enumerate(waves):
            put(f, prop, u)

    @pl.when(step == 0)
    def arrive():
        wait_copies([pltpu.make_async_copy(*copy) for copy in [copy_hop] + copies_one + [copy_turned]])

    @pl.when(live)
    def stage_two():
        for u in group:
            load_window(meta, step * GROUP + u, ext, (0, 1), win, u)
        waves = [hop_left(pair(prop, u), hop, 0, True) for u in group]
        waves = [hop_right(f, hop, 1, True) for f in waves]
        for u, wave in enumerate(waves):
            probe = pair(turned, step * GROUP + u)
            grad, part = conj_times(probe, wave), conj_times(pair(win, u), wave)
            put(grad, win, u)
            put(part, prop, u)

        def finish(slot, u):
            add_window(meta, slot, win, u, range(4), gext)
            add_probe(meta, slot, prop, u, acc)

        for u in group:
            slot = step * GROUP + u
            finish(slot, u)

    @pl.when(step == SLOTS // GROUP - 1)
    def end():
        sem = sems.at[0]
        outs = start_copies([
            (gext.at[1, :, :, pl.ds(W, W)], gdown1, sem.at[0]),
            (gext.at[1, :, :, pl.ds(TC, W)], gcorner, sem.at[1]),
            (gext.at[1, :, :, pl.ds(0, W)], gdown0, sem.at[2]),
            (gext.at[0, :, :, pl.ds(TC, W)], gright, sem.at[3]),
            (gext.at[0, :, :, pl.ds(0, TC)], gown, sem.at[4]),
        ])
        for p in range(2):
            gprobe[p] = lanes(acc[p, 0, :W, :] + acc[p, 0, W:, :], acc[p, 1, :W, :] + acc[p, 1, W:, :])
        wait_copies(outs)


ANYWHERE = pl.BlockSpec(memory_space=pl.ANY)
WHOLE = pl.BlockSpec(memory_space=pltpu.VMEM)
SCALARS = pl.BlockSpec(memory_space=pltpu.SMEM)
FIELDS = pl.BlockSpec((GROUP, 2, W, W), lambda i: (i, 0, 0, 0))
PLANES = pl.BlockSpec((GROUP, W, W), lambda i: (i, 0, 0))


def shape(*dims):
    return jax.ShapeDtypeStruct(dims, F32)


FIELDS_SHAPE = shape(SLOTS, 2, W, W)


def call(kernel, steps, in_specs, out_specs, out_shape, scratch, products, mebibytes):
    return pl.pallas_call(
        kernel,
        grid=(steps,),
        in_specs=in_specs,
        out_specs=out_specs,
        out_shape=out_shape,
        scratch_shapes=scratch,
        compiler_params=pltpu.CompilerParams(
            vmem_limit_bytes=mebibytes * 2**20, dimension_semantics=("arbitrary",)
        ),
        cost_estimate=pl.CostEstimate(
            flops=SLOTS * products * 2 * W**3, bytes_accessed=products * 2**18, transcendentals=0
        ),
    )


def prepare_call(*args):
    return call(
        prepare_kernel,
        SLOTS // PREPARED,
        [SCALARS, WHOLE, pl.BlockSpec((PREPARED, W, W), lambda i: (i, 0, 0)), WHOLE],
        [
            pl.BlockSpec((PREPARED, W, W), lambda i: (i, 0, 0)),
            pl.BlockSpec((PREPARED, 2, W, W), lambda i: (i, 0, 0, 0)),
        ],
        [shape(SLOTS, W, W), FIELDS_SHAPE],
        [pltpu.VMEM((2, 2, 2 * W, HALF_W), F32)],
        0,
        16,
    )(*args)


def first_call(*args):
    return call(
        first_kernel,
        SLOTS // GROUP,
        [SCALARS] + [ANYWHERE] * 3 + [WHOLE, WHOLE, FIELDS, WHOLE],
        FIELDS,
        FIELDS_SHAPE,
        [
            pltpu.VMEM((2, 2, W, EXT), F32),
            pltpu.VMEM((GROUP, 2, W, W), F32),
            pltpu.SemaphoreType.DMA((5,)),
        ],
        24,
        32,
    )(*args)


def second_call(*args):
    return call(
        second_kernel,
        SLOTS // GROUP,
        [SCALARS] + [ANYWHERE] * 8 + [WHOLE, WHOLE, FIELDS, PLANES, WHOLE],
        [ANYWHERE] * 5 + [WHOLE],
        [shape(4, W, TC)] + [shape(4, W, W)] * 4 + [shape(2, W, W)],
        [
            pltpu.VMEM((2, 4, W, EXT), F32),
            pltpu.VMEM((2, 4, W, EXT), F32),
            pltpu.VMEM((2, 2, 2 * W, HALF_W), F32),
            pltpu.VMEM((SLOTS, 2, W, W), F32),
            pltpu.VMEM((12, W, W), BF16),
            pltpu.VMEM((GROUP, 4, W, W), F32),
            pltpu.SemaphoreType.DMA((3, 5)),
        ],
        48,
        50,
    )(*args)


def add_kernel(base, *refs):
    parts, out = refs[:-1], refs[-1]
    for i, part in enumerate(parts):
        here = pl.ds(i * W, W)
        out[:, :, here] = base[:, :, here] + part[...]


def add_call(base, *parts):
    block = pl.BlockSpec((1, W, W * len(parts)), lambda i: (i, 0, 0))
    part = pl.BlockSpec((1, W, W), lambda i: (i, 0, 0))
    return pl.pallas_call(
        add_kernel,
        grid=(4,),
        in_specs=[block] + [part] * len(parts),
        out_specs=block,
        out_shape=shape(4, W, TC),
        input_output_aliases={0: 0},
        compiler_params=pltpu.CompilerParams(vmem_limit_bytes=8 * 2**20),
        cost_estimate=pl.CostEstimate(flops=2**19, bytes_accessed=2**22, transcendentals=0),
    )(base, *parts)


def shift(value, axis, steps):
    count = lax.axis_size(axis)
    first, last = (max(0, -steps), min(count, count - steps))
    return lax.ppermute(value, axis, [(source, source + steps) for source in range(first, last)])


def add_shares(value, axis):
    count = lax.axis_size(axis)
    shares = value.reshape(count, -1, value.shape[-1])
    return lax.all_to_all(shares, axis, 0, 0, tiled=True).sum(axis=0)


def hand_out(value, axis):
    spread = jnp.broadcast_to(value[None], (lax.axis_size(axis), *value.shape))
    return lax.all_to_all(spread, axis, 0, 0, tiled=True)


def ring_sum(value, pairs):
    first = lax.ppermute(value, "row", pairs)
    second = lax.ppermute(first, "row", pairs)
    third = lax.ppermute(second, "row", pairs)
    return (value + second) + (first + third)


def body(object_slab, probe_wave, scan_offsets, live_counts, amplitudes):
    rows_tile, cols_tile = object_slab.shape[1:]
    local_rows = scan_offsets[:, 0] - lax.axis_index("row") * rows_tile
    local_cols = scan_offsets[:, 1] - lax.axis_index("col") * cols_tile
    meta = jnp.concatenate([live_counts, local_rows, local_cols])
    hop, dft, fold = jnp.asarray(hop_tables()), jnp.asarray(dft_tables()), jnp.asarray(fold_tables())
    down0_one = shift(object_slab[:2, :, :W], "row", -1)
    down1_one = shift(object_slab[:2, :, W:], "row", -1)
    right = shift(object_slab[:, :, :W], "col", -1)
    down0_two = shift(object_slab[2:, :, :W], "row", -1)
    amp, turned = prepare_call(meta, probe_wave, amplitudes, fold)
    down0_one, turned, last_part = lax.optimization_barrier((down0_one, turned, object_slab[2:, :, W:]))
    corner_one = shift(down0_one, "col", -1)
    down1_two = shift(last_part, "row", -1)
    prop = first_call(meta, object_slab, right, down0_one, down1_one, corner_one, turned, hop)
    down0_two, prop = lax.optimization_barrier((down0_two, prop))
    corner_two = shift(down0_two, "col", -1)
    gown, gright, gdown0, gdown1, gcorner, gprobe = second_call(
        meta, object_slab, right, down0_one, down0_two, down1_one, corner_one, turned, hop, down1_two, corner_two,
        prop, amp, dft,
    )
    side = lax.axis_size("row") // 4
    to_left_x = [(i, (i - side) % (4 * side)) for i in range(4 * side)]
    to_left_y = [(i, i - i % side + (i - 1) % side) for i in range(4 * side)]
    corner_back = shift(gcorner, "col", 1)
    down1_back = shift(gdown1, "row", 1)
    share = add_shares(gprobe, "col")
    gdown0, share = lax.optimization_barrier((gdown0 + corner_back, share))
    down0_back = shift(gdown0, "row", 1)
    right_back = shift(gright, "col", 1)
    share = ring_sum(ring_sum(share, to_left_x), to_left_y)
    gown, share = lax.optimization_barrier((add_call(gown, right_back, down1_back), share))
    probe_grad = hand_out(share, "col").reshape(probe_wave.shape)
    return add_call(gown, down0_back), probe_grad


def solution(mesh):
    return jax.shard_map(
        body,
        mesh=mesh,
        in_specs=(
            P(None, "row", "col"),
            P(),
            P(("row", "col"), None),
            P(("row", "col")),
            P(("row", "col"), None, None),
        ),
        out_specs=(P(None, "row", "col"), P()),
        check_vma=False,
    )
```

```python
import math

import jax
import jax.numpy as jnp
import ml_dtypes
import numpy as np
from jax import lax
from jax.experimental import pallas as pl
from jax.experimental.pallas import tpu as pltpu
from jax.sharding import PartitionSpec as P

W = 256
HALF_W = 128
TC = 512
EXT = TC + W
SLOTS = 8
GROUP = 4
PREPARED = 2
CHUNK = 32
F32 = jnp.float32
BF16 = jnp.bfloat16

RE, IM, NEG_IM = 0, 1, 2


def split_host(table):
    high = table.astype(np.float32).astype(ml_dtypes.bfloat16)
    low = (table - high.astype(np.float64)).astype(np.float32).astype(ml_dtypes.bfloat16)
    return [high, low]


def hop_tables():
    index = np.arange(W)
    dft = np.exp(-2j * np.pi / W * (index[:, None] * index[None, :] % W)) / math.sqrt(W)
    freqs = np.where(index < W // 2, index, index - W) / W
    fresnel = np.exp(-1j * np.pi * (W / 4.0) * freqs**2)
    hop = np.conj(dft) @ (fresnel[:, None] * dft)
    hop = hop * np.exp(1j * np.pi * index / W)
    out = []
    for table in (hop, hop.T):
        for part in (table.real, table.imag, -table.imag):
            out.extend(split_host(part))
    return np.stack(out)


def dft_tables():
    index = np.arange(W)
    angles = 2.0 * np.pi / W * (index[:, None] + 0.5) * (index[None, :HALF_W] + 0.5)
    table = np.concatenate([np.cos(angles), np.sin(angles)], axis=1) / math.sqrt(W)
    return np.stack(split_host(table) + split_host(table.T))


def fold_tables():
    source = np.concatenate([np.arange(HALF_W), np.arange(W - 1, HALF_W - 1, -1)])
    table = np.zeros((W, W), np.float32)
    table[source, np.arange(W)] = 1.0
    return np.stack([table, table.T]).astype(ml_dtypes.bfloat16)


def split(x):
    high = x.astype(BF16)
    return high, (x - high.astype(F32)).astype(BF16)


def lanes(*parts):
    return jnp.concatenate(parts, axis=1)


def rows(*parts):
    return jnp.concatenate(parts, axis=0)


def dot(a, b):
    return jnp.dot(a, b, preferred_element_type=F32)


def half_right(field, tab, at):
    high, low = tab[2 * at], tab[2 * at + 1]
    rh, rl = split(field[0])
    ih, il = split(field[1])
    out = dot(rows(lanes(rh, rl, rh), lanes(ih, il, ih)), rows(high, high, low))
    return out[:W], out[W:]


def half_left(field, tab, at):
    high, low = tab[2 * at], tab[2 * at + 1]
    rh, rl = split(field[0])
    ih, il = split(field[1])
    out = dot(lanes(high, high, low), lanes(rows(rh, rl, rh), rows(ih, il, ih)))
    return out[:, :W], out[:, W:]


def hop_parts(tab, at, conj):
    im, neg = (IM, NEG_IM) if not conj else (NEG_IM, IM)

    def three(a, b):
        a, b = 2 * (3 * at + a), 2 * (3 * at + b)
        return [tab[a], tab[b], tab[a], tab[b], tab[a + 1], tab[b + 1]]

    return three(RE, neg), three(im, RE)


def hop_right(field, tab, at, conj):
    rh, rl = split(field[0])
    ih, il = split(field[1])
    to_re, to_im = hop_parts(tab, at, conj)
    out = dot(lanes(rh, ih, rl, il, rh, ih), lanes(rows(*to_re), rows(*to_im)))
    return out[:, :W], out[:, W:]


def hop_left(field, tab, at, conj):
    rh, rl = split(field[0])
    ih, il = split(field[1])
    to_re, to_im = hop_parts(tab, at, conj)
    out = dot(rows(lanes(*to_re), lanes(*to_im)), rows(rh, ih, rl, il, rh, ih))
    return out[:W], out[W:]


def spread_right(field):
    c, s = field[0][:, :HALF_W], field[0][:, HALF_W:]
    d, t = field[1][:, :HALF_W], field[1][:, HALF_W:]
    return lanes(c + t, t - c), lanes(d - s, -d - s)


def spread_left(field):
    c, s = field[0][:HALF_W], field[0][HALF_W:]
    d, t = field[1][:HALF_W], field[1][HALF_W:]
    return rows(c + t, t - c), rows(d - s, -d - s)


def gather_right(field):
    a, b = field[0][:, :HALF_W], field[0][:, HALF_W:]
    c, d = field[1][:, :HALF_W], field[1][:, HALF_W:]
    return lanes(a - b, -c - d), lanes(c - d, a + b)


def gather_left(field):
    a, b = field[0][:HALF_W], field[0][HALF_W:]
    c, d = field[1][:HALF_W], field[1][HALF_W:]
    return rows(a - b, -c - d), rows(c - d, a + b)


def times(a, b):
    return a[0] * b[0] - a[1] * b[1], a[0] * b[1] + a[1] * b[0]


def conj_times(a, b):
    return a[0] * b[0] + a[1] * b[1], a[0] * b[1] - a[1] * b[0]


def pair(ref, *at):
    return ref[(*at, 0)], ref[(*at, 1)]


def put(value, ref, *at):
    ref[(*at, 0)], ref[(*at, 1)] = value


def chunks(body):
    def step(i, carry):
        body(pl.multiple_of(i * CHUNK, CHUNK))
        return carry

    lax.fori_loop(0, W // CHUNK, step, 0)


def geometry(meta, slot):
    row, col = meta[1 + slot], meta[1 + SLOTS + slot]
    block = col // W
    first = pl.multiple_of(block * W, W)
    second = pl.multiple_of(block * W + W, W)
    return row, col - block * W, first, second


def masks(row, col, at):
    in_top = lax.broadcasted_iota(jnp.int32, (CHUNK, W), 0) + at >= row
    in_first = lax.broadcasted_iota(jnp.int32, (CHUNK, W), 1) >= col
    return in_top, in_first


def load_window(meta, slot, ext, planes, win, u):
    row, col, first, second = geometry(meta, slot)
    border = row // CHUNK

    def load(i, carry):
        here = pl.ds(pl.multiple_of(i * CHUNK, CHUNK), CHUNK)
        _, in_first = masks(row, col, 0)
        low = (i < border).astype(jnp.int32)
        for p in planes:
            win[u, p, here, :] = jnp.where(
                in_first, ext[low, p, here, pl.ds(first, W)], ext[low, p, here, pl.ds(second, W)]
            )
        return carry

    lax.fori_loop(0, W // CHUNK, load, 0, unroll=True)
    at = pl.multiple_of(border * CHUNK, CHUNK)
    here = pl.ds(at, CHUNK)
    in_top, in_first = masks(row, col, at)
    for p in planes:
        low = jnp.where(in_first, ext[1, p, here, pl.ds(first, W)], ext[1, p, here, pl.ds(second, W)])
        win[u, p, here, :] = jnp.where(in_top, win[u, p, here, :], low)


def add_window(meta, slot, win, u, planes, gext):
    row, col, first, second = geometry(meta, slot)
    border = row // CHUNK
    zero = jnp.zeros((CHUNK, W), F32)
    alive = slot < meta[0]

    def add(i, carry):
        at = pl.multiple_of(i * CHUNK, CHUNK)
        here = pl.ds(at, CHUNK)
        in_top, in_first = masks(row, col, at)
        low = (i < border).astype(jnp.int32)
        keep = jnp.logical_and(jnp.logical_or(in_top, i < border), alive)
        for p in planes:
            value = jnp.where(keep, win[u, p, here, :], zero)
            gext[low, p, here, pl.ds(first, W)] += jnp.where(in_first, value, zero)
            gext[low, p, here, pl.ds(second, W)] += jnp.where(in_first, zero, value)
        return carry

    lax.fori_loop(0, W // CHUNK, add, 0, unroll=True)
    at = pl.multiple_of(border * CHUNK, CHUNK)
    here = pl.ds(at, CHUNK)
    in_top, in_first = masks(row, col, at)
    for p in planes:
        value = jnp.where(jnp.logical_and(jnp.logical_not(in_top), alive), win[u, p, here, :], zero)
        gext[1, p, here, pl.ds(first, W)] += jnp.where(in_first, value, zero)
        gext[1, p, here, pl.ds(second, W)] += jnp.where(in_first, zero, value)


def turn_probe(meta, slot, twice, turned, u):
    row, col, _, _ = geometry(meta, slot)
    for p in range(2):
        here = pl.ds(W - row, W)
        turned[u, p] = pltpu.roll(lanes(twice[p, 0, here, :], twice[p, 1, here, :]), col, 1)


def add_probe(meta, slot, part, u, acc):
    row, col, _, _ = geometry(meta, slot)
    for p in range(2):
        here = pl.ds(W - row, W)
        value = jnp.where(slot < meta[0], pltpu.roll(part[u, p], W - col, 1), 0.0)
        acc[p, 0, here, :] += value[:, :HALF_W]
        acc[p, 1, here, :] += value[:, HALF_W:]


def tile_copies(refs, ext, sems):
    own, right, down0, down1, corner = refs
    return [
        (own, ext.at[0, :, :, pl.ds(0, TC)], sems.at[0]),
        (right, ext.at[0, :, :, pl.ds(TC, W)], sems.at[1]),
        (down0, ext.at[1, :, :, pl.ds(0, W)], sems.at[2]),
        (down1, ext.at[1, :, :, pl.ds(W, W)], sems.at[3]),
        (corner, ext.at[1, :, :, pl.ds(TC, W)], sems.at[4]),
    ]


def start_copies(copies):
    copies = [pltpu.make_async_copy(*copy) for copy in copies]
    for copy in copies:
        copy.start()
    return copies


def wait_copies(copies):
    for copy in copies:
        copy.wait()


def prepare_kernel(meta, probe, amp, fold, amp_out, turned, twice):
    step = pl.program_id(0)

    def fold_amplitudes(u):
        high = amp[u].astype(BF16)
        rest = amp[u] - high.astype(F32)
        mid = rest.astype(BF16)
        low = (rest - mid.astype(F32)).astype(BF16)
        right_way = dot(rows(high, mid, low), fold[0])
        out = dot(fold[1], lanes(*(right_way[i * W : (i + 1) * W].astype(BF16) for i in range(3))))
        amp_out[u] = out[:, :W] + out[:, W : 2 * W] + out[:, 2 * W :]

    @pl.when(step == 0)
    def double_probe():
        for p in range(2):
            for half in range(2):
                part = probe[p, :, half * HALF_W : (half + 1) * HALF_W]
                twice[p, half, :W, :] = part
                twice[p, half, W:, :] = part

    for u in range(PREPARED):
        fold_amplitudes(u)
        turn_probe(meta, step * PREPARED + u, twice, turned, u)


def first_kernel(meta, own, right, down0, down1, corner, turned, tab, prop, ext, win, sems):
    step = pl.program_id(0)

    @pl.when(step == 0)
    def begin():
        one = pl.ds(0, 2)
        refs = (own.at[one], right.at[one], down0, down1, corner)
        wait_copies(start_copies(tile_copies(refs, ext, sems)))

    @pl.when(step * GROUP < meta[0])
    def work():
        for u in range(GROUP):
            load_window(meta, step * GROUP + u, ext, (0, 1), win, u)
        fields = [times(pair(turned, u), pair(win, u)) for u in range(GROUP)]
        fields = [hop_right(f, tab, 0, False) for f in fields]
        fields = [hop_left(f, tab, 1, False) for f in fields]
        for u, f in enumerate(fields):
            put(f, prop, u)


def second_kernel(meta, own, right, down0_one, down0_two, down1_one, corner_one, turned_in, hop_in, prop_in, amp_in,
                  down1_two, corner_two, dft, gown, gright, gdown0, gdown1, gcorner, gprobe,
                  ext, gext, acc, turned, hop, prop, amp, win, sems):
    step = pl.program_id(0)
    group = range(GROUP)
    one, two = pl.ds(0, 2), pl.ds(2, 2)
    refs_one = (own.at[one], right.at[one], down0_one, down1_one, corner_one)
    refs_two = (own.at[two], right.at[two], down0_two, down1_two, corner_two)
    copies_one = tile_copies(refs_one, ext.at[:, one], sems.at[0])
    copies_two = tile_copies(refs_two, ext.at[:, two], sems.at[1])
    now, later = pl.ds(0, GROUP), pl.ds(GROUP, SLOTS - GROUP)
    copies_now = copies_two + [
        (prop_in.at[now], prop.at[now], sems.at[2, 0]),
        (amp_in.at[now], amp.at[now], sems.at[2, 1]),
    ]
    copies_later = [(hop_in, hop, sems.at[2, 2])] + copies_one + [
        (turned_in, turned, sems.at[2, 3]),
        (prop_in.at[later], prop.at[later], sems.at[2, 4]),
        (amp_in.at[later], amp.at[later], sems.at[2, 5]),
    ]

    @pl.when(step == 0)
    def begin():
        started = start_copies(copies_now)
        start_copies(copies_later)
        gext[...] = jnp.zeros_like(gext)
        acc[...] = jnp.zeros_like(acc)
        wait_copies(started)

    live = step * GROUP < meta[0]

    @pl.when(live)
    def stage_one():
        for u in group:
            load_window(meta, step * GROUP + u, ext, (2, 3), win, u)
        fields = [times(pair(prop, step * GROUP + u), (win[u, 2], win[u, 3])) for u in group]
        fields = [spread_left(half_left(f, dft, 1)) for f in fields]
        fields = [spread_right(half_right(f, dft, 0)) for f in fields]
        chi = []
        for u, f in enumerate(fields):
            factor = 1.0 - amp[step * GROUP + u] * lax.rsqrt(f[0] * f[0] + f[1] * f[1] + 1.0)
            chi.append((factor * f[0], factor * f[1]))
        fields = [half_right(gather_right(f), dft, 1) for f in chi]
        fields = [half_left(gather_left(f), dft, 0) for f in fields]
        waves = [conj_times((win[u, 2], win[u, 3]), f) for u, f in enumerate(fields)]
        for u, f in enumerate(fields):
            win[u, 2], win[u, 3] = conj_times(pair(prop, step * GROUP + u), f)
        for u, f in enumerate(waves):
            put(f, prop, step * GROUP + u)

    @pl.when(step == 0)
    def arrive():
        wait_copies([pltpu.make_async_copy(*copy) for copy in copies_later])

    @pl.when(live)
    def stage_two():
        for u in group:
            load_window(meta, step * GROUP + u, ext, (0, 1), win, u)
            add_window(meta, step * GROUP + u, win, u, (2, 3), gext)
        waves = [hop_left(pair(prop, step * GROUP + u), hop, 0, True) for u in group]
        waves = [hop_right(f, hop, 1, True) for f in waves]
        for u, wave in enumerate(waves):
            probe = pair(turned, step * GROUP + u)
            grad, part = conj_times(probe, wave), conj_times(pair(win, u), wave)
            put(grad, win, u)
            put(part, prop, step * GROUP + u)

        def finish(slot, u):
            add_window(meta, slot, win, u, (0, 1), gext)
            add_probe(meta, slot, prop, slot, acc)

        for u in group:
            slot = step * GROUP + u
            finish(slot, u)

    @pl.when(step == SLOTS // GROUP - 1)
    def end():
        sem = sems.at[0]
        outs = start_copies([
            (gext.at[1, :, :, pl.ds(W, W)], gdown1, sem.at[0]),
            (gext.at[1, :, :, pl.ds(TC, W)], gcorner, sem.at[1]),
            (gext.at[1, :, :, pl.ds(0, W)], gdown0, sem.at[2]),
            (gext.at[0, :, :, pl.ds(TC, W)], gright, sem.at[3]),
            (gext.at[0, :, :, pl.ds(0, TC)], gown, sem.at[4]),
        ])
        for p in range(2):
            gprobe[p] = lanes(acc[p, 0, :W, :] + acc[p, 0, W:, :], acc[p, 1, :W, :] + acc[p, 1, W:, :])
        wait_copies(outs)


ANYWHERE = pl.BlockSpec(memory_space=pl.ANY)
WHOLE = pl.BlockSpec(memory_space=pltpu.VMEM)
SCALARS = pl.BlockSpec(memory_space=pltpu.SMEM)
FIELDS = pl.BlockSpec((GROUP, 2, W, W), lambda i: (i, 0, 0, 0))
PLANES = pl.BlockSpec((GROUP, W, W), lambda i: (i, 0, 0))


def shape(*dims):
    return jax.ShapeDtypeStruct(dims, F32)


FIELDS_SHAPE = shape(SLOTS, 2, W, W)


def call(kernel, steps, in_specs, out_specs, out_shape, scratch, products, mebibytes):
    return pl.pallas_call(
        kernel,
        grid=(steps,),
        in_specs=in_specs,
        out_specs=out_specs,
        out_shape=out_shape,
        scratch_shapes=scratch,
        compiler_params=pltpu.CompilerParams(
            vmem_limit_bytes=mebibytes * 2**20, dimension_semantics=("arbitrary",)
        ),
        cost_estimate=pl.CostEstimate(
            flops=SLOTS * products * 2 * W**3, bytes_accessed=products * 2**18, transcendentals=0
        ),
    )


def prepare_call(*args):
    return call(
        prepare_kernel,
        SLOTS // PREPARED,
        [SCALARS, WHOLE, pl.BlockSpec((PREPARED, W, W), lambda i: (i, 0, 0)), WHOLE],
        [
            pl.BlockSpec((PREPARED, W, W), lambda i: (i, 0, 0)),
            pl.BlockSpec((PREPARED, 2, W, W), lambda i: (i, 0, 0, 0)),
        ],
        [shape(SLOTS, W, W), FIELDS_SHAPE],
        [pltpu.VMEM((2, 2, 2 * W, HALF_W), F32)],
        0,
        16,
    )(*args)


def first_call(*args):
    return call(
        first_kernel,
        SLOTS // GROUP,
        [SCALARS] + [ANYWHERE] * 3 + [WHOLE, WHOLE, FIELDS, WHOLE],
        FIELDS,
        FIELDS_SHAPE,
        [
            pltpu.VMEM((2, 2, W, EXT), F32),
            pltpu.VMEM((GROUP, 2, W, W), F32),
            pltpu.SemaphoreType.DMA((5,)),
        ],
        24,
        52,
    )(*args)


def second_call(*args):
    return call(
        second_kernel,
        SLOTS // GROUP,
        [SCALARS] + [ANYWHERE] * 10 + [WHOLE] * 3,
        [ANYWHERE] * 5 + [WHOLE],
        [shape(4, W, TC)] + [shape(4, W, W)] * 4 + [shape(2, W, W)],
        [
            pltpu.VMEM((2, 4, W, EXT), F32),
            pltpu.VMEM((2, 4, W, EXT), F32),
            pltpu.VMEM((2, 2, 2 * W, HALF_W), F32),
            pltpu.VMEM((SLOTS, 2, W, W), F32),
            pltpu.VMEM((12, W, W), BF16),
            pltpu.VMEM((SLOTS, 2, W, W), F32),
            pltpu.VMEM((SLOTS, W, W), F32),
            pltpu.VMEM((GROUP, 4, W, W), F32),
            pltpu.SemaphoreType.DMA((3, 6)),
        ],
        48,
        50,
    )(*args)


def add_kernel(base, right, down0, down1, out):
    first, second = pl.ds(0, W), pl.ds(W, W)
    out[:, :, first] = base[:, :, first] + (right[...] + down0[...])
    out[:, :, second] = base[:, :, second] + down1[...]


def add_call(*args):
    whole = pl.BlockSpec((1, W, TC), lambda i: (i, 0, 0))
    part = pl.BlockSpec((1, W, W), lambda i: (i, 0, 0))
    return pl.pallas_call(
        add_kernel,
        grid=(4,),
        in_specs=[whole] + [part] * 3,
        out_specs=whole,
        out_shape=shape(4, W, TC),
        compiler_params=pltpu.CompilerParams(vmem_limit_bytes=8 * 2**20),
        cost_estimate=pl.CostEstimate(flops=2**20, bytes_accessed=7 * 2**20, transcendentals=0),
    )(*args)


def shift(value, axis, steps):
    count = lax.axis_size(axis)
    first, last = (max(0, -steps), min(count, count - steps))
    return lax.ppermute(value, axis, [(source, source + steps) for source in range(first, last)])


def add_shares(value, axis):
    count = lax.axis_size(axis)
    shares = value.reshape(count, -1, value.shape[-1])
    return lax.all_to_all(shares, axis, 0, 0, tiled=True).sum(axis=0)


def hand_out(value, axis):
    spread = jnp.broadcast_to(value[None], (lax.axis_size(axis), *value.shape))
    return lax.all_to_all(spread, axis, 0, 0, tiled=True)


def ring_sum(value, pairs):
    first = lax.ppermute(value, "row", pairs)
    second = lax.ppermute(first, "row", pairs)
    third = lax.ppermute(second, "row", pairs)
    return (value + second) + (first + third)


def body(object_slab, probe_wave, scan_offsets, live_counts, amplitudes):
    rows_tile, cols_tile = object_slab.shape[1:]
    local_rows = scan_offsets[:, 0] - lax.axis_index("row") * rows_tile
    local_cols = scan_offsets[:, 1] - lax.axis_index("col") * cols_tile
    meta = jnp.concatenate([live_counts, local_rows, local_cols])
    hop, dft, fold = jnp.asarray(hop_tables()), jnp.asarray(dft_tables()), jnp.asarray(fold_tables())
    first_part, rest = lax.optimization_barrier((object_slab[:2, :, :W], object_slab))
    down0_one = shift(first_part, "row", -1)
    down1_one = shift(rest[:2, :, W:], "row", -1)
    right = shift(rest[:, :, :W], "col", -1)
    down0_two = shift(rest[2:, :, :W], "row", -1)
    amp, turned = prepare_call(meta, probe_wave, amplitudes, fold)
    down0_one, turned, last_part = lax.optimization_barrier((down0_one, turned, rest[2:, :, W:]))
    corner_one = shift(down0_one, "col", -1)
    down1_two = shift(last_part, "row", -1)
    prop = first_call(meta, object_slab, right, down0_one, down1_one, corner_one, turned, hop)
    down0_two, prop = lax.optimization_barrier((down0_two, prop))
    corner_two = shift(down0_two, "col", -1)
    gown, gright, gdown0, gdown1, gcorner, gprobe = second_call(
        meta, object_slab, right, down0_one, down0_two, down1_one, corner_one, turned, hop, prop, amp,
        down1_two, corner_two, dft,
    )
    side = lax.axis_size("row") // 4
    to_left_x = [(i, (i - side) % (4 * side)) for i in range(4 * side)]
    to_left_y = [(i, i - i % side + (i - 1) % side) for i in range(4 * side)]
    corner_back = shift(gcorner, "col", 1)
    down1_back = shift(gdown1, "row", 1)
    share = add_shares(gprobe, "col")
    down0_back = shift(gdown0 + corner_back, "row", 1)
    right_back = shift(gright, "col", 1)
    share = ring_sum(ring_sum(share, to_left_x), to_left_y)
    probe_grad = hand_out(share, "col").reshape(probe_wave.shape)
    return add_call(gown, right_back, down0_back, down1_back), probe_grad


def solution(mesh):
    return jax.shard_map(
        body,
        mesh=mesh,
        in_specs=(
            P(None, "row", "col"),
            P(),
            P(("row", "col"), None),
            P(("row", "col")),
            P(("row", "col"), None, None),
        ),
        out_specs=(P(None, "row", "col"), P()),
        check_vma=False,
    )
```

```python
import math

import jax
import jax.numpy as jnp
import ml_dtypes
import numpy as np
from jax import lax
from jax.experimental import pallas as pl
from jax.experimental.pallas import tpu as pltpu
from jax.sharding import PartitionSpec as P

W = 256
HALF_W = 128
TC = 512
EXT = TC + W
SLOTS = 8
GROUP = 4
PREPARED = 2
CHUNK = 32
F32 = jnp.float32
BF16 = jnp.bfloat16

RE, IM, NEG_IM = 0, 1, 2


def split_host(table):
    high = table.astype(np.float32).astype(ml_dtypes.bfloat16)
    low = (table - high.astype(np.float64)).astype(np.float32).astype(ml_dtypes.bfloat16)
    return [high, low]


def hop_tables():
    index = np.arange(W)
    dft = np.exp(-2j * np.pi / W * (index[:, None] * index[None, :] % W)) / math.sqrt(W)
    freqs = np.where(index < W // 2, index, index - W) / W
    fresnel = np.exp(-1j * np.pi * (W / 4.0) * freqs**2)
    hop = np.conj(dft) @ (fresnel[:, None] * dft)
    hop = hop * np.exp(1j * np.pi * index / W)
    out = []
    for table in (hop, hop.T):
        for part in (table.real, table.imag, -table.imag):
            out.extend(split_host(part))
    return np.stack(out)


def dft_tables():
    index = np.arange(W)
    angles = 2.0 * np.pi / W * (index[:, None] + 0.5) * (index[None, :HALF_W] + 0.5)
    table = np.concatenate([np.cos(angles), np.sin(angles)], axis=1) / math.sqrt(W)
    return np.stack(split_host(table) + split_host(table.T))


def fold_tables():
    source = np.concatenate([np.arange(HALF_W), np.arange(W - 1, HALF_W - 1, -1)])
    table = np.zeros((W, W), np.float32)
    table[source, np.arange(W)] = 1.0
    return np.stack([table, table.T]).astype(ml_dtypes.bfloat16)


def split(x):
    high = x.astype(BF16)
    return high, (x - high.astype(F32)).astype(BF16)


def lanes(*parts):
    return jnp.concatenate(parts, axis=1)


def rows(*parts):
    return jnp.concatenate(parts, axis=0)


def dot(a, b):
    return jnp.dot(a, b, preferred_element_type=F32)


def half_right(field, tab, at):
    high, low = tab[2 * at], tab[2 * at + 1]
    rh, rl = split(field[0])
    ih, il = split(field[1])
    out = dot(rows(lanes(rh, rl, rh), lanes(ih, il, ih)), rows(high, high, low))
    return out[:W], out[W:]


def half_left(field, tab, at):
    high, low = tab[2 * at], tab[2 * at + 1]
    rh, rl = split(field[0])
    ih, il = split(field[1])
    out = dot(lanes(high, high, low), lanes(rows(rh, rl, rh), rows(ih, il, ih)))
    return out[:, :W], out[:, W:]


def hop_parts(tab, at, conj):
    im, neg = (IM, NEG_IM) if not conj else (NEG_IM, IM)

    def three(a, b):
        a, b = 2 * (3 * at + a), 2 * (3 * at + b)
        return [tab[a], tab[b], tab[a], tab[b], tab[a + 1], tab[b + 1]]

    return three(RE, neg), three(im, RE)


def hop_right(field, tab, at, conj):
    rh, rl = split(field[0])
    ih, il = split(field[1])
    to_re, to_im = hop_parts(tab, at, conj)
    out = dot(lanes(rh, ih, rl, il, rh, ih), lanes(rows(*to_re), rows(*to_im)))
    return out[:, :W], out[:, W:]


def hop_left(field, tab, at, conj):
    rh, rl = split(field[0])
    ih, il = split(field[1])
    to_re, to_im = hop_parts(tab, at, conj)
    out = dot(rows(lanes(*to_re), lanes(*to_im)), rows(rh, ih, rl, il, rh, ih))
    return out[:W], out[W:]


def spread_right(field):
    c, s = field[0][:, :HALF_W], field[0][:, HALF_W:]
    d, t = field[1][:, :HALF_W], field[1][:, HALF_W:]
    return lanes(c + t, t - c), lanes(d - s, -d - s)


def spread_left(field):
    c, s = field[0][:HALF_W], field[0][HALF_W:]
    d, t = field[1][:HALF_W], field[1][HALF_W:]
    return rows(c + t, t - c), rows(d - s, -d - s)


def gather_right(field):
    a, b = field[0][:, :HALF_W], field[0][:, HALF_W:]
    c, d = field[1][:, :HALF_W], field[1][:, HALF_W:]
    return lanes(a - b, -c - d), lanes(c - d, a + b)


def gather_left(field):
    a, b = field[0][:HALF_W], field[0][HALF_W:]
    c, d = field[1][:HALF_W], field[1][HALF_W:]
    return rows(a - b, -c - d), rows(c - d, a + b)


def times(a, b):
    return a[0] * b[0] - a[1] * b[1], a[0] * b[1] + a[1] * b[0]


def conj_times(a, b):
    return a[0] * b[0] + a[1] * b[1], a[0] * b[1] - a[1] * b[0]


def pair(ref, *at):
    return ref[(*at, 0)], ref[(*at, 1)]


def put(value, ref, *at):
    ref[(*at, 0)], ref[(*at, 1)] = value


def chunks(body):
    def step(i, carry):
        body(pl.multiple_of(i * CHUNK, CHUNK))
        return carry

    lax.fori_loop(0, W // CHUNK, step, 0)


def geometry(meta, slot):
    row, col = meta[1 + slot], meta[1 + SLOTS + slot]
    block = col // W
    first = pl.multiple_of(block * W, W)
    second = pl.multiple_of(block * W + W, W)
    return row, col - block * W, first, second


def masks(row, col, at):
    in_top = lax.broadcasted_iota(jnp.int32, (CHUNK, W), 0) + at >= row
    in_first = lax.broadcasted_iota(jnp.int32, (CHUNK, W), 1) >= col
    return in_top, in_first


def load_window(meta, slot, ext, planes, win, u):
    row, col, first, second = geometry(meta, slot)
    border = row // CHUNK

    def load(i, carry):
        here = pl.ds(pl.multiple_of(i * CHUNK, CHUNK), CHUNK)
        _, in_first = masks(row, col, 0)
        low = (i < border).astype(jnp.int32)
        for p in planes:
            win[u, p, here, :] = jnp.where(
                in_first, ext[low, p, here, pl.ds(first, W)], ext[low, p, here, pl.ds(second, W)]
            )
        return carry

    lax.fori_loop(0, W // CHUNK, load, 0, unroll=True)
    at = pl.multiple_of(border * CHUNK, CHUNK)
    here = pl.ds(at, CHUNK)
    in_top, in_first = masks(row, col, at)
    for p in planes:
        low = jnp.where(in_first, ext[1, p, here, pl.ds(first, W)], ext[1, p, here, pl.ds(second, W)])
        win[u, p, here, :] = jnp.where(in_top, win[u, p, here, :], low)


def add_window(meta, slot, win, u, planes, gext):
    row, col, first, second = geometry(meta, slot)
    border = row // CHUNK
    zero = jnp.zeros((CHUNK, W), F32)
    alive = slot < meta[0]

    def add(i, carry):
        at = pl.multiple_of(i * CHUNK, CHUNK)
        here = pl.ds(at, CHUNK)
        in_top, in_first = masks(row, col, at)
        low = (i < border).astype(jnp.int32)
        keep = jnp.logical_and(jnp.logical_or(in_top, i < border), alive)
        for p in planes:
            value = jnp.where(keep, win[u, p, here, :], zero)
            gext[low, p, here, pl.ds(first, W)] += jnp.where(in_first, value, zero)
            gext[low, p, here, pl.ds(second, W)] += jnp.where(in_first, zero, value)
        return carry

    lax.fori_loop(0, W // CHUNK, add, 0, unroll=True)
    at = pl.multiple_of(border * CHUNK, CHUNK)
    here = pl.ds(at, CHUNK)
    in_top, in_first = masks(row, col, at)
    for p in planes:
        value = jnp.where(jnp.logical_and(jnp.logical_not(in_top), alive), win[u, p, here, :], zero)
        gext[1, p, here, pl.ds(first, W)] += jnp.where(in_first, value, zero)
        gext[1, p, here, pl.ds(second, W)] += jnp.where(in_first, zero, value)


def turn_probe(meta, slot, twice, turned, u):
    row, col, _, _ = geometry(meta, slot)
    for p in range(2):
        here = pl.ds(W - row, W)
        turned[u, p] = pltpu.roll(lanes(twice[p, 0, here, :], twice[p, 1, here, :]), col, 1)


def add_probe(meta, slot, part, u, acc):
    row, col, _, _ = geometry(meta, slot)
    for p in range(2):
        here = pl.ds(W - row, W)
        value = jnp.where(slot < meta[0], pltpu.roll(part[u, p], W - col, 1), 0.0)
        acc[p, 0, here, :] += value[:, :HALF_W]
        acc[p, 1, here, :] += value[:, HALF_W:]


def tile_copies(refs, ext, sems):
    own, right, down0, down1, corner = refs
    return [
        (own, ext.at[0, :, :, pl.ds(0, TC)], sems.at[0]),
        (right, ext.at[0, :, :, pl.ds(TC, W)], sems.at[1]),
        (down0, ext.at[1, :, :, pl.ds(0, W)], sems.at[2]),
        (down1, ext.at[1, :, :, pl.ds(W, W)], sems.at[3]),
        (corner, ext.at[1, :, :, pl.ds(TC, W)], sems.at[4]),
    ]


def start_copies(copies):
    copies = [pltpu.make_async_copy(*copy) for copy in copies]
    for copy in copies:
        copy.start()
    return copies


def wait_copies(copies):
    for copy in copies:
        copy.wait()


def prepare_kernel(meta, probe, amp, fold, amp_out, turned, twice):
    step = pl.program_id(0)

    def fold_amplitudes(u):
        high = amp[u].astype(BF16)
        rest = amp[u] - high.astype(F32)
        mid = rest.astype(BF16)
        low = (rest - mid.astype(F32)).astype(BF16)
        right_way = dot(rows(high, mid, low), fold[0])
        out = dot(fold[1], lanes(*(right_way[i * W : (i + 1) * W].astype(BF16) for i in range(3))))
        amp_out[u] = out[:, :W] + out[:, W : 2 * W] + out[:, 2 * W :]

    @pl.when(step == 0)
    def double_probe():
        for p in range(2):
            for half in range(2):
                part = probe[p, :, half * HALF_W : (half + 1) * HALF_W]
                twice[p, half, :W, :] = part
                twice[p, half, W:, :] = part

    for u in range(PREPARED):
        fold_amplitudes(u)
        turn_probe(meta, step * PREPARED + u, twice, turned, u)


def first_kernel(meta, own, right, down0, down1, corner, turned, tab, prop, ext, win, sems):
    step = pl.program_id(0)

    @pl.when(step == 0)
    def begin():
        one = pl.ds(0, 2)
        refs = (own.at[one], right.at[one], down0, down1, corner)
        wait_copies(start_copies(tile_copies(refs, ext, sems)))

    @pl.when(step * GROUP < meta[0])
    def work():
        for u in range(GROUP):
            load_window(meta, step * GROUP + u, ext, (0, 1), win, u)
        fields = [times(pair(turned, u), pair(win, u)) for u in range(GROUP)]
        fields = [hop_right(f, tab, 0, False) for f in fields]
        fields = [hop_left(f, tab, 1, False) for f in fields]
        for u, f in enumerate(fields):
            put(f, prop, u)


def second_kernel(meta, own, right, down0_one, down0_two, down1_one, corner_one, turned_in, hop_in, prop_in, amp_in,
                  down1_two, corner_two, dft, gown, gright, gdown0, gdown1, gcorner, gprobe,
                  ext, gext, acc, turned, hop, prop, amp, win, sems):
    step = pl.program_id(0)
    group = range(GROUP)
    one, two = pl.ds(0, 2), pl.ds(2, 2)
    refs_one = (own.at[one], right.at[one], down0_one, down1_one, corner_one)
    refs_two = (own.at[two], right.at[two], down0_two, down1_two, corner_two)
    copies_one = tile_copies(refs_one, ext.at[:, one], sems.at[0])
    copies_two = tile_copies(refs_two, ext.at[:, two], sems.at[1])
    now, later = pl.ds(0, GROUP), pl.ds(GROUP, SLOTS - GROUP)
    copies_now = copies_two + [
        (prop_in.at[now], prop.at[now], sems.at[2, 0]),
        (amp_in.at[now], amp.at[now], sems.at[2, 1]),
    ]
    copies_later = [(hop_in, hop, sems.at[2, 2])] + copies_one + [
        (turned_in, turned, sems.at[2, 3]),
        (prop_in.at[later], prop.at[later], sems.at[2, 4]),
        (amp_in.at[later], amp.at[later], sems.at[2, 5]),
    ]

    @pl.when(step == 0)
    def begin():
        started = start_copies(copies_now)
        start_copies(copies_later)
        gext[...] = jnp.zeros_like(gext)
        acc[...] = jnp.zeros_like(acc)
        wait_copies(started)

    live = step * GROUP < meta[0]

    @pl.when(live)
    def stage_one():
        for u in group:
            load_window(meta, step * GROUP + u, ext, (2, 3), win, u)
        fields = [times(pair(prop, step * GROUP + u), (win[u, 2], win[u, 3])) for u in group]
        fields = [spread_left(half_left(f, dft, 1)) for f in fields]
        fields = [spread_right(half_right(f, dft, 0)) for f in fields]
        chi = []
        for u, f in enumerate(fields):
            factor = 1.0 - amp[step * GROUP + u] * lax.rsqrt(f[0] * f[0] + f[1] * f[1] + 1.0)
            chi.append((factor * f[0], factor * f[1]))
        fields = [half_right(gather_right(f), dft, 1) for f in chi]
        fields = [half_left(gather_left(f), dft, 0) for f in fields]
        waves = [conj_times((win[u, 2], win[u, 3]), f) for u, f in enumerate(fields)]
        for u, f in enumerate(fields):
            win[u, 2], win[u, 3] = conj_times(pair(prop, step * GROUP + u), f)
        for u, f in enumerate(waves):
            put(f, prop, step * GROUP + u)

    @pl.when(step == 0)
    def arrive():
        wait_copies([pltpu.make_async_copy(*copy) for copy in copies_later])

    @pl.when(live)
    def stage_two():
        for u in group:
            load_window(meta, step * GROUP + u, ext, (0, 1), win, u)
            add_window(meta, step * GROUP + u, win, u, (2, 3), gext)
        waves = [hop_left(pair(prop, step * GROUP + u), hop, 0, True) for u in group]
        waves = [hop_right(f, hop, 1, True) for f in waves]
        for u, wave in enumerate(waves):
            probe = pair(turned, step * GROUP + u)
            grad, part = conj_times(probe, wave), conj_times(pair(win, u), wave)
            put(grad, win, u)
            put(part, prop, step * GROUP + u)

        def finish(slot, u):
            add_window(meta, slot, win, u, (0, 1), gext)
            add_probe(meta, slot, prop, slot, acc)

        for u in group:
            slot = step * GROUP + u
            finish(slot, u)

    @pl.when(step == SLOTS // GROUP - 1)
    def end():
        sem = sems.at[0]
        outs = start_copies([
            (gext.at[1, :, :, pl.ds(W, W)], gdown1, sem.at[0]),
            (gext.at[1, :, :, pl.ds(TC, W)], gcorner, sem.at[1]),
            (gext.at[1, :, :, pl.ds(0, W)], gdown0, sem.at[2]),
            (gext.at[0, :, :, pl.ds(TC, W)], gright, sem.at[3]),
            (gext.at[0, :, :, pl.ds(0, TC)], gown, sem.at[4]),
        ])
        for p in range(2):
            gprobe[p] = lanes(acc[p, 0, :W, :] + acc[p, 0, W:, :], acc[p, 1, :W, :] + acc[p, 1, W:, :])
        wait_copies(outs)


ANYWHERE = pl.BlockSpec(memory_space=pl.ANY)
WHOLE = pl.BlockSpec(memory_space=pltpu.VMEM)
SCALARS = pl.BlockSpec(memory_space=pltpu.SMEM)
FIELDS = pl.BlockSpec((GROUP, 2, W, W), lambda i: (i, 0, 0, 0))
PLANES = pl.BlockSpec((GROUP, W, W), lambda i: (i, 0, 0))


def shape(*dims):
    return jax.ShapeDtypeStruct(dims, F32)


FIELDS_SHAPE = shape(SLOTS, 2, W, W)


def call(kernel, steps, in_specs, out_specs, out_shape, scratch, products, mebibytes):
    return pl.pallas_call(
        kernel,
        grid=(steps,),
        in_specs=in_specs,
        out_specs=out_specs,
        out_shape=out_shape,
        scratch_shapes=scratch,
        compiler_params=pltpu.CompilerParams(
            vmem_limit_bytes=mebibytes * 2**20, dimension_semantics=("arbitrary",)
        ),
        cost_estimate=pl.CostEstimate(
            flops=SLOTS * products * 2 * W**3, bytes_accessed=products * 2**18, transcendentals=0
        ),
    )


def prepare_call(*args):
    return call(
        prepare_kernel,
        SLOTS // PREPARED,
        [SCALARS, WHOLE, pl.BlockSpec((PREPARED, W, W), lambda i: (i, 0, 0)), WHOLE],
        [
            pl.BlockSpec((PREPARED, W, W), lambda i: (i, 0, 0)),
            pl.BlockSpec((PREPARED, 2, W, W), lambda i: (i, 0, 0, 0)),
        ],
        [shape(SLOTS, W, W), FIELDS_SHAPE],
        [pltpu.VMEM((2, 2, 2 * W, HALF_W), F32)],
        0,
        16,
    )(*args)


def first_call(*args):
    return call(
        first_kernel,
        SLOTS // GROUP,
        [SCALARS] + [ANYWHERE] * 3 + [WHOLE, WHOLE, FIELDS, WHOLE],
        FIELDS,
        FIELDS_SHAPE,
        [
            pltpu.VMEM((2, 2, W, EXT), F32),
            pltpu.VMEM((GROUP, 2, W, W), F32),
            pltpu.SemaphoreType.DMA((5,)),
        ],
        24,
        52,
    )(*args)


def second_call(*args):
    return call(
        second_kernel,
        SLOTS // GROUP,
        [SCALARS] + [ANYWHERE] * 10 + [WHOLE] * 3,
        [ANYWHERE] * 5 + [WHOLE],
        [shape(4, W, TC)] + [shape(4, W, W)] * 4 + [shape(2, W, W)],
        [
            pltpu.VMEM((2, 4, W, EXT), F32),
            pltpu.VMEM((2, 4, W, EXT), F32),
            pltpu.VMEM((2, 2, 2 * W, HALF_W), F32),
            pltpu.VMEM((SLOTS, 2, W, W), F32),
            pltpu.VMEM((12, W, W), BF16),
            pltpu.VMEM((SLOTS, 2, W, W), F32),
            pltpu.VMEM((SLOTS, W, W), F32),
            pltpu.VMEM((GROUP, 4, W, W), F32),
            pltpu.SemaphoreType.DMA((3, 6)),
        ],
        48,
        50,
    )(*args)


def add_kernel(base, right, down0, down1, out):
    first, second = pl.ds(0, W), pl.ds(W, W)
    out[:, :, first] = base[:, :, first] + (right[...] + down0[...])
    out[:, :, second] = base[:, :, second] + down1[...]


def add_call(*args):
    whole = pl.BlockSpec((1, W, TC), lambda i: (i, 0, 0))
    part = pl.BlockSpec((1, W, W), lambda i: (i, 0, 0))
    return pl.pallas_call(
        add_kernel,
        grid=(4,),
        in_specs=[whole] + [part] * 3,
        out_specs=whole,
        out_shape=shape(4, W, TC),
        compiler_params=pltpu.CompilerParams(vmem_limit_bytes=8 * 2**20),
        cost_estimate=pl.CostEstimate(flops=2**20, bytes_accessed=7 * 2**20, transcendentals=0),
    )(*args)


def shift(value, axis, steps):
    count = lax.axis_size(axis)
    first, last = (max(0, -steps), min(count, count - steps))
    return lax.ppermute(value, axis, [(source, source + steps) for source in range(first, last)])


def add_shares(value, axis):
    count = lax.axis_size(axis)
    shares = value.reshape(count, -1, value.shape[-1])
    return lax.all_to_all(shares, axis, 0, 0, tiled=True).sum(axis=0)


def hand_out(value, axis):
    spread = jnp.broadcast_to(value[None], (lax.axis_size(axis), *value.shape))
    return lax.all_to_all(spread, axis, 0, 0, tiled=True)


def ring_sum(value, pairs):
    first = lax.ppermute(value, "row", pairs)
    second = lax.ppermute(first, "row", pairs)
    third = lax.ppermute(second, "row", pairs)
    return (value + second) + (first + third)


def body(object_slab, probe_wave, scan_offsets, live_counts, amplitudes):
    rows_tile, cols_tile = object_slab.shape[1:]
    local_rows = scan_offsets[:, 0] - lax.axis_index("row") * rows_tile
    local_cols = scan_offsets[:, 1] - lax.axis_index("col") * cols_tile
    meta = jnp.concatenate([live_counts, local_rows, local_cols])
    hop, dft, fold = jnp.asarray(hop_tables()), jnp.asarray(dft_tables()), jnp.asarray(fold_tables())
    first_part, rest = lax.optimization_barrier((object_slab[:2, :, :W], object_slab))
    down0_one = shift(first_part, "row", -1)
    down1_one = shift(rest[:2, :, W:], "row", -1)
    right = shift(rest[:, :, :W], "col", -1)
    down0_two = shift(rest[2:, :, :W], "row", -1)
    amp, turned = prepare_call(meta, probe_wave, amplitudes, fold)
    down0_one, turned, last_part = lax.optimization_barrier((down0_one, turned, rest[2:, :, W:]))
    corner_one = shift(down0_one, "col", -1)
    down1_two = shift(last_part, "row", -1)
    prop = first_call(meta, object_slab, right, down0_one, down1_one, corner_one, turned, hop)
    down0_two, prop = lax.optimization_barrier((down0_two, prop))
    corner_two = shift(down0_two, "col", -1)
    gown, gright, gdown0, gdown1, gcorner, gprobe = second_call(
        meta, object_slab, right, down0_one, down0_two, down1_one, corner_one, turned, hop, prop, amp,
        down1_two, corner_two, dft,
    )
    side = lax.axis_size("row") // 4
    to_left_x = [(i, (i - side) % (4 * side)) for i in range(4 * side)]
    to_left_y = [(i, i - i % side + (i - 1) % side) for i in range(4 * side)]
    corner_back = shift(gcorner, "col", 1)
    down1_back = shift(gdown1, "row", 1)
    share = add_shares(gprobe, "col")
    gdown0, share = lax.optimization_barrier((gdown0 + corner_back, share))
    down0_back = shift(gdown0, "row", 1)
    right_back = shift(gright, "col", 1)
    share = ring_sum(ring_sum(share, to_left_x), to_left_y)
    right_back, down1_back, share = lax.optimization_barrier((right_back, down1_back, share))
    probe_grad = hand_out(share, "col").reshape(probe_wave.shape)
    return add_call(gown, right_back, down0_back, down1_back), probe_grad


def solution(mesh):
    return jax.shard_map(
        body,
        mesh=mesh,
        in_specs=(
            P(None, "row", "col"),
            P(),
            P(("row", "col"), None),
            P(("row", "col")),
            P(("row", "col"), None, None),
        ),
        out_specs=(P(None, "row", "col"), P()),
        check_vma=False,
    )
```

```python
import functools
import math

import jax
import jax.numpy as jnp
import ml_dtypes
import numpy as np
from jax import lax
from jax.experimental import pallas as pl
from jax.experimental.pallas import tpu as pltpu
from jax.sharding import PartitionSpec as P

W = 256
HALF_W = 128
TC = 512
EXT = TC + W
SLOTS = 8
GROUP = 4
PREPARED = 2
CHUNK = 32
F32 = jnp.float32
BF16 = jnp.bfloat16

RE, IM, NEG_IM = 0, 1, 2


def split_host(table):
    high = table.astype(np.float32).astype(ml_dtypes.bfloat16)
    low = (table - high.astype(np.float64)).astype(np.float32).astype(ml_dtypes.bfloat16)
    return [high, low]


def hop_tables():
    index = np.arange(W)
    dft = np.exp(-2j * np.pi / W * (index[:, None] * index[None, :] % W)) / math.sqrt(W)
    freqs = np.where(index < W // 2, index, index - W) / W
    fresnel = np.exp(-1j * np.pi * (W / 4.0) * freqs**2)
    hop = np.conj(dft) @ (fresnel[:, None] * dft)
    hop = hop * np.exp(1j * np.pi * index / W)
    out = []
    for table in (hop, hop.T):
        for part in (table.real, table.imag, -table.imag):
            out.extend(split_host(part))
    return np.stack(out)


def dft_tables():
    index = np.arange(W)
    angles = 2.0 * np.pi / W * (index[:, None] + 0.5) * (index[None, :HALF_W] + 0.5)
    table = np.concatenate([np.cos(angles), np.sin(angles)], axis=1) / math.sqrt(W)
    return np.stack(split_host(table) + split_host(table.T))


def fold_tables():
    source = np.concatenate([np.arange(HALF_W), np.arange(W - 1, HALF_W - 1, -1)])
    table = np.zeros((W, W), np.float32)
    table[source, np.arange(W)] = 1.0
    return np.stack([table, table.T]).astype(ml_dtypes.bfloat16)


def split(x):
    high = x.astype(BF16)
    return high, (x - high.astype(F32)).astype(BF16)


def lanes(*parts):
    return jnp.concatenate(parts, axis=1)


def rows(*parts):
    return jnp.concatenate(parts, axis=0)


def dot(a, b):
    return jnp.dot(a, b, preferred_element_type=F32)


def half_right(field, tab, at):
    high, low = tab[2 * at], tab[2 * at + 1]
    rh, rl = split(field[0])
    ih, il = split(field[1])
    out = dot(rows(lanes(rh, rl, rh), lanes(ih, il, ih)), rows(high, high, low))
    return out[:W], out[W:]


def half_left(field, tab, at):
    high, low = tab[2 * at], tab[2 * at + 1]
    rh, rl = split(field[0])
    ih, il = split(field[1])
    out = dot(lanes(high, high, low), lanes(rows(rh, rl, rh), rows(ih, il, ih)))
    return out[:, :W], out[:, W:]


def hop_parts(tab, at, conj):
    im, neg = (IM, NEG_IM) if not conj else (NEG_IM, IM)

    def three(a, b):
        a, b = 2 * (3 * at + a), 2 * (3 * at + b)
        return [tab[a], tab[b], tab[a], tab[b], tab[a + 1], tab[b + 1]]

    return three(RE, neg), three(im, RE)


def hop_right(field, tab, at, conj):
    rh, rl = split(field[0])
    ih, il = split(field[1])
    to_re, to_im = hop_parts(tab, at, conj)
    out = dot(lanes(rh, ih, rl, il, rh, ih), lanes(rows(*to_re), rows(*to_im)))
    return out[:, :W], out[:, W:]


def hop_left(field, tab, at, conj):
    rh, rl = split(field[0])
    ih, il = split(field[1])
    to_re, to_im = hop_parts(tab, at, conj)
    out = dot(rows(lanes(*to_re), lanes(*to_im)), rows(rh, ih, rl, il, rh, ih))
    return out[:W], out[W:]


def spread_right(field):
    c, s = field[0][:, :HALF_W], field[0][:, HALF_W:]
    d, t = field[1][:, :HALF_W], field[1][:, HALF_W:]
    return lanes(c + t, t - c), lanes(d - s, -d - s)


def spread_left(field):
    c, s = field[0][:HALF_W], field[0][HALF_W:]
    d, t = field[1][:HALF_W], field[1][HALF_W:]
    return rows(c + t, t - c), rows(d - s, -d - s)


def gather_right(field):
    a, b = field[0][:, :HALF_W], field[0][:, HALF_W:]
    c, d = field[1][:, :HALF_W], field[1][:, HALF_W:]
    return lanes(a - b, -c - d), lanes(c - d, a + b)


def gather_left(field):
    a, b = field[0][:HALF_W], field[0][HALF_W:]
    c, d = field[1][:HALF_W], field[1][HALF_W:]
    return rows(a - b, -c - d), rows(c - d, a + b)


def times(a, b):
    return a[0] * b[0] - a[1] * b[1], a[0] * b[1] + a[1] * b[0]


def conj_times(a, b):
    return a[0] * b[0] + a[1] * b[1], a[0] * b[1] - a[1] * b[0]


def pair(ref, *at):
    return ref[(*at, 0)], ref[(*at, 1)]


def put(value, ref, *at):
    ref[(*at, 0)], ref[(*at, 1)] = value


def chunks(body):
    def step(i, carry):
        body(pl.multiple_of(i * CHUNK, CHUNK))
        return carry

    lax.fori_loop(0, W // CHUNK, step, 0)


def geometry(meta, slot):
    row, col = meta[1 + slot], meta[1 + SLOTS + slot]
    block = col // W
    first = pl.multiple_of(block * W, W)
    second = pl.multiple_of(block * W + W, W)
    return row, col - block * W, first, second


def masks(row, col, at):
    in_top = lax.broadcasted_iota(jnp.int32, (CHUNK, W), 0) + at >= row
    in_first = lax.broadcasted_iota(jnp.int32, (CHUNK, W), 1) >= col
    return in_top, in_first


def load_window(meta, slot, ext, planes, win, u):
    row, col, first, second = geometry(meta, slot)
    border = row // CHUNK

    def load(i, carry):
        here = pl.ds(pl.multiple_of(i * CHUNK, CHUNK), CHUNK)
        _, in_first = masks(row, col, 0)
        low = (i < border).astype(jnp.int32)
        for p in planes:
            win[u, p, here, :] = jnp.where(
                in_first, ext[low, p, here, pl.ds(first, W)], ext[low, p, here, pl.ds(second, W)]
            )
        return carry

    lax.fori_loop(0, W // CHUNK, load, 0, unroll=True)
    at = pl.multiple_of(border * CHUNK, CHUNK)
    here = pl.ds(at, CHUNK)
    in_top, in_first = masks(row, col, at)
    for p in planes:
        low = jnp.where(in_first, ext[1, p, here, pl.ds(first, W)], ext[1, p, here, pl.ds(second, W)])
        win[u, p, here, :] = jnp.where(in_top, win[u, p, here, :], low)


def add_window(meta, slot, win, u, planes, gext):
    row, col, first, second = geometry(meta, slot)
    border = row // CHUNK
    zero = jnp.zeros((CHUNK, W), F32)
    alive = slot < meta[0]

    def add(i, carry):
        at = pl.multiple_of(i * CHUNK, CHUNK)
        here = pl.ds(at, CHUNK)
        in_top, in_first = masks(row, col, at)
        low = (i < border).astype(jnp.int32)
        keep = jnp.logical_and(jnp.logical_or(in_top, i < border), alive)
        for p in planes:
            value = jnp.where(keep, win[u, p, here, :], zero)
            gext[low, p, here, pl.ds(first, W)] += jnp.where(in_first, value, zero)
            gext[low, p, here, pl.ds(second, W)] += jnp.where(in_first, zero, value)
        return carry

    lax.fori_loop(0, W // CHUNK, add, 0, unroll=True)
    at = pl.multiple_of(border * CHUNK, CHUNK)
    here = pl.ds(at, CHUNK)
    in_top, in_first = masks(row, col, at)
    for p in planes:
        value = jnp.where(jnp.logical_and(jnp.logical_not(in_top), alive), win[u, p, here, :], zero)
        gext[1, p, here, pl.ds(first, W)] += jnp.where(in_first, value, zero)
        gext[1, p, here, pl.ds(second, W)] += jnp.where(in_first, zero, value)


def turn_probe(meta, slot, twice, turned, u):
    row, col, _, _ = geometry(meta, slot)
    for p in range(2):
        here = pl.ds(W - row, W)
        turned[u, p] = pltpu.roll(lanes(twice[p, 0, here, :], twice[p, 1, here, :]), col, 1)


def add_probe(meta, slot, part, u, acc):
    row, col, _, _ = geometry(meta, slot)
    for p in range(2):
        here = pl.ds(W - row, W)
        value = jnp.where(slot < meta[0], pltpu.roll(part[u, p], W - col, 1), 0.0)
        acc[p, 0, here, :] += value[:, :HALF_W]
        acc[p, 1, here, :] += value[:, HALF_W:]


def tile_copies(refs, ext, sems):
    own, right, down0, down1, corner = refs
    return [
        (own, ext.at[0, :, :, pl.ds(0, TC)], sems.at[0]),
        (right, ext.at[0, :, :, pl.ds(TC, W)], sems.at[1]),
        (down0, ext.at[1, :, :, pl.ds(0, W)], sems.at[2]),
        (down1, ext.at[1, :, :, pl.ds(W, W)], sems.at[3]),
        (corner, ext.at[1, :, :, pl.ds(TC, W)], sems.at[4]),
    ]


def start_copies(copies):
    copies = [pltpu.make_async_copy(*copy) for copy in copies]
    for copy in copies:
        copy.start()
    return copies


def wait_copies(copies):
    for copy in copies:
        copy.wait()


def prepare_kernel(meta, probe, amp, fold, amp_out, turned, twice):
    step = pl.program_id(0)

    def fold_amplitudes(u):
        high = amp[u].astype(BF16)
        rest = amp[u] - high.astype(F32)
        mid = rest.astype(BF16)
        low = (rest - mid.astype(F32)).astype(BF16)
        right_way = dot(rows(high, mid, low), fold[0])
        out = dot(fold[1], lanes(*(right_way[i * W : (i + 1) * W].astype(BF16) for i in range(3))))
        amp_out[u] = out[:, :W] + out[:, W : 2 * W] + out[:, 2 * W :]

    @pl.when(step == 0)
    def double_probe():
        for p in range(2):
            for half in range(2):
                part = probe[p, :, half * HALF_W : (half + 1) * HALF_W]
                twice[p, half, :W, :] = part
                twice[p, half, W:, :] = part

    for u in range(PREPARED):
        fold_amplitudes(u)
        turn_probe(meta, step * PREPARED + u, twice, turned, u)


def first_kernel(start, meta, own, right, down0, down1, corner, turned_in, hop_in, prop, ext, turned, hop, win, sems):
    @pl.when(start < meta[0])
    def work():
        one, group = pl.ds(0, 2), pl.ds(start, GROUP)
        refs = (own.at[one], right.at[one], down0, down1, corner)
        started = start_copies(tile_copies(refs, ext, sems))
        rest = start_copies([(turned_in.at[group], turned, sems.at[5]), (hop_in, hop, sems.at[6])])
        wait_copies(started)
        for u in range(GROUP):
            load_window(meta, start + u, ext, (0, 1), win, u)
        wait_copies(rest)
        fields = [times(pair(turned, u), pair(win, u)) for u in range(GROUP)]
        fields = [hop_right(f, hop, 0, False) for f in fields]
        fields = [hop_left(f, hop, 1, False) for f in fields]
        for u, f in enumerate(fields):
            put(f, prop, u)


def second_kernel(meta, own, right, down0_one, down0_two, down1_one, corner_one, turned_in, hop_in, prop_now, prop_later, amp_in,
                  down1_two, corner_two, dft, gown, gright, gdown0, gdown1, gcorner, gprobe,
                  ext, gext, acc, turned, hop, prop, amp, win, sems):
    step = pl.program_id(0)
    group = range(GROUP)
    one, two = pl.ds(0, 2), pl.ds(2, 2)
    refs_one = (own.at[one], right.at[one], down0_one, down1_one, corner_one)
    refs_two = (own.at[two], right.at[two], down0_two, down1_two, corner_two)
    copies_one = tile_copies(refs_one, ext.at[:, one], sems.at[0])
    copies_two = tile_copies(refs_two, ext.at[:, two], sems.at[1])
    now, later = pl.ds(0, GROUP), pl.ds(GROUP, SLOTS - GROUP)
    copies_now = copies_two + [
        (prop_now, prop.at[now], sems.at[2, 0]),
        (amp_in.at[now], amp.at[now], sems.at[2, 1]),
    ]
    copies_later = [(hop_in, hop, sems.at[2, 2])] + copies_one + [
        (turned_in, turned, sems.at[2, 3]),
        (prop_later, prop.at[later], sems.at[2, 4]),
        (amp_in.at[later], amp.at[later], sems.at[2, 5]),
    ]

    @pl.when(step == 0)
    def begin():
        started = start_copies(copies_now)
        start_copies(copies_later)
        gext[...] = jnp.zeros_like(gext)
        acc[...] = jnp.zeros_like(acc)
        wait_copies(started)

    live = step * GROUP < meta[0]

    @pl.when(live)
    def stage_one():
        for u in group:
            load_window(meta, step * GROUP + u, ext, (2, 3), win, u)
        fields = [times(pair(prop, step * GROUP + u), (win[u, 2], win[u, 3])) for u in group]
        fields = [spread_left(half_left(f, dft, 1)) for f in fields]
        fields = [spread_right(half_right(f, dft, 0)) for f in fields]
        chi = []
        for u, f in enumerate(fields):
            factor = 1.0 - amp[step * GROUP + u] * lax.rsqrt(f[0] * f[0] + f[1] * f[1] + 1.0)
            chi.append((factor * f[0], factor * f[1]))
        fields = [half_right(gather_right(f), dft, 1) for f in chi]
        fields = [half_left(gather_left(f), dft, 0) for f in fields]
        waves = [conj_times((win[u, 2], win[u, 3]), f) for u, f in enumerate(fields)]
        for u, f in enumerate(fields):
            win[u, 2], win[u, 3] = conj_times(pair(prop, step * GROUP + u), f)
        for u, f in enumerate(waves):
            put(f, prop, step * GROUP + u)

    @pl.when(step == 0)
    def arrive():
        wait_copies([pltpu.make_async_copy(*copy) for copy in copies_later])

    @pl.when(live)
    def stage_two():
        for u in group:
            load_window(meta, step * GROUP + u, ext, (0, 1), win, u)
            add_window(meta, step * GROUP + u, win, u, (2, 3), gext)
        waves = [hop_left(pair(prop, step * GROUP + u), hop, 0, True) for u in group]
        waves = [hop_right(f, hop, 1, True) for f in waves]
        for u, wave in enumerate(waves):
            probe = pair(turned, step * GROUP + u)
            grad, part = conj_times(probe, wave), conj_times(pair(win, u), wave)
            put(grad, win, u)
            put(part, prop, step * GROUP + u)

        def finish(slot, u):
            add_window(meta, slot, win, u, (0, 1), gext)
            add_probe(meta, slot, prop, slot, acc)

        for u in group:
            slot = step * GROUP + u
            finish(slot, u)

    @pl.when(step == SLOTS // GROUP - 1)
    def end():
        sem = sems.at[0]
        outs = start_copies([
            (gext.at[1, :, :, pl.ds(W, W)], gdown1, sem.at[0]),
            (gext.at[1, :, :, pl.ds(TC, W)], gcorner, sem.at[1]),
            (gext.at[1, :, :, pl.ds(0, W)], gdown0, sem.at[2]),
            (gext.at[0, :, :, pl.ds(TC, W)], gright, sem.at[3]),
            (gext.at[0, :, :, pl.ds(0, TC)], gown, sem.at[4]),
        ])
        for p in range(2):
            gprobe[p] = lanes(acc[p, 0, :W, :] + acc[p, 0, W:, :], acc[p, 1, :W, :] + acc[p, 1, W:, :])
        wait_copies(outs)


ANYWHERE = pl.BlockSpec(memory_space=pl.ANY)
WHOLE = pl.BlockSpec(memory_space=pltpu.VMEM)
SCALARS = pl.BlockSpec(memory_space=pltpu.SMEM)
FIELDS = pl.BlockSpec((GROUP, 2, W, W), lambda i: (i, 0, 0, 0))
PLANES = pl.BlockSpec((GROUP, W, W), lambda i: (i, 0, 0))


def shape(*dims):
    return jax.ShapeDtypeStruct(dims, F32)


FIELDS_SHAPE = shape(SLOTS, 2, W, W)


def call(kernel, steps, in_specs, out_specs, out_shape, scratch, products, mebibytes):
    return pl.pallas_call(
        kernel,
        grid=(steps,),
        in_specs=in_specs,
        out_specs=out_specs,
        out_shape=out_shape,
        scratch_shapes=scratch,
        compiler_params=pltpu.CompilerParams(
            vmem_limit_bytes=mebibytes * 2**20, dimension_semantics=("arbitrary",)
        ),
        cost_estimate=pl.CostEstimate(
            flops=SLOTS * products * 2 * W**3, bytes_accessed=products * 2**18, transcendentals=0
        ),
    )


def prepare_call(*args):
    return call(
        prepare_kernel,
        SLOTS // PREPARED,
        [SCALARS, WHOLE, pl.BlockSpec((PREPARED, W, W), lambda i: (i, 0, 0)), WHOLE],
        [
            pl.BlockSpec((PREPARED, W, W), lambda i: (i, 0, 0)),
            pl.BlockSpec((PREPARED, 2, W, W), lambda i: (i, 0, 0, 0)),
        ],
        [shape(SLOTS, W, W), FIELDS_SHAPE],
        [pltpu.VMEM((2, 2, 2 * W, HALF_W), F32)],
        0,
        16,
    )(*args)


def first_call(start, products, *args):
    return call(
        functools.partial(first_kernel, start),
        1,
        [SCALARS] + [ANYWHERE] * 3 + [WHOLE, WHOLE] + [ANYWHERE] * 2,
        pl.BlockSpec((GROUP, 2, W, W), lambda i: (0, 0, 0, 0)),
        shape(GROUP, 2, W, W),
        [
            pltpu.VMEM((2, 2, W, EXT), F32),
            pltpu.VMEM((GROUP, 2, W, W), F32),
            pltpu.VMEM((12, W, W), BF16),
            pltpu.VMEM((GROUP, 2, W, W), F32),
            pltpu.SemaphoreType.DMA((7,)),
        ],
        products,
        52,
    )(*args)


def second_call(*args):
    return call(
        second_kernel,
        SLOTS // GROUP,
        [SCALARS] + [ANYWHERE] * 11 + [WHOLE] * 3,
        [ANYWHERE] * 5 + [WHOLE],
        [shape(4, W, TC)] + [shape(4, W, W)] * 4 + [shape(2, W, W)],
        [
            pltpu.VMEM((2, 4, W, EXT), F32),
            pltpu.VMEM((2, 4, W, EXT), F32),
            pltpu.VMEM((2, 2, 2 * W, HALF_W), F32),
            pltpu.VMEM((SLOTS, 2, W, W), F32),
            pltpu.VMEM((12, W, W), BF16),
            pltpu.VMEM((SLOTS, 2, W, W), F32),
            pltpu.VMEM((SLOTS, W, W), F32),
            pltpu.VMEM((GROUP, 4, W, W), F32),
            pltpu.SemaphoreType.DMA((3, 6)),
        ],
        48,
        50,
    )(*args)


def add_kernel(base, right, down0, down1, shares, out, shares_out):
    shares_out[...] = shares[...]
    first, second = pl.ds(0, W), pl.ds(W, W)
    out[:, :, first] = base[:, :, first] + (right[...] + down0[...])
    out[:, :, second] = base[:, :, second] + down1[...]


def add_call(*args):
    whole = pl.BlockSpec((1, W, TC), lambda i: (i, 0, 0))
    part = pl.BlockSpec((1, W, W), lambda i: (i, 0, 0))
    share = pl.BlockSpec((2, 64, W), lambda i: (i, 0, 0))
    return pl.pallas_call(
        add_kernel,
        grid=(4,),
        in_specs=[whole] + [part] * 3 + [share],
        out_specs=[whole, share],
        out_shape=[shape(4, W, TC), shape(8, 64, W)],
        compiler_params=pltpu.CompilerParams(vmem_limit_bytes=8 * 2**20),
        cost_estimate=pl.CostEstimate(flops=2**20, bytes_accessed=7 * 2**20, transcendentals=0),
    )(*args)


def shift(value, axis, steps):
    count = lax.axis_size(axis)
    first, last = (max(0, -steps), min(count, count - steps))
    return lax.ppermute(value, axis, [(source, source + steps) for source in range(first, last)])


def add_shares(value, axis):
    count = lax.axis_size(axis)
    shares = value.reshape(count, -1, value.shape[-1])
    return lax.all_to_all(shares, axis, 0, 0, tiled=True).sum(axis=0)


def hand_out(value, axis):
    spread = jnp.broadcast_to(value[None], (lax.axis_size(axis), *value.shape))
    return lax.all_to_all(spread, axis, 0, 0, tiled=True)


def ring_sum(value, pairs):
    first = lax.ppermute(value, "row", pairs)
    second = lax.ppermute(first, "row", pairs)
    third = lax.ppermute(second, "row", pairs)
    return (value + second) + (first + third)


def body(object_slab, probe_wave, scan_offsets, live_counts, amplitudes):
    rows_tile, cols_tile = object_slab.shape[1:]
    local_rows = scan_offsets[:, 0] - lax.axis_index("row") * rows_tile
    local_cols = scan_offsets[:, 1] - lax.axis_index("col") * cols_tile
    meta = jnp.concatenate([live_counts, local_rows, local_cols])
    hop, dft, fold = jnp.asarray(hop_tables()), jnp.asarray(dft_tables()), jnp.asarray(fold_tables())
    first_part, rest = lax.optimization_barrier((object_slab[:2, :, :W], object_slab))
    down0_one = shift(first_part, "row", -1)
    down1_one = shift(rest[:2, :, W:], "row", -1)
    right = shift(rest[:, :, :W], "col", -1)
    down0_two = shift(rest[2:, :, :W], "row", -1)
    amp, turned = prepare_call(meta, probe_wave, amplitudes, fold)
    down0_one, turned, last_part = lax.optimization_barrier((down0_one, turned, rest[2:, :, W:]))
    corner_one = shift(down0_one, "col", -1)
    down1_two = shift(last_part, "row", -1)
    near = (meta, object_slab, right, down0_one, down1_one, corner_one, turned, hop)
    prop_now = first_call(0, 12, *near)
    down0_two, prop_now, near = lax.optimization_barrier((down0_two, prop_now, near))
    corner_two = shift(down0_two, "col", -1)
    prop_later = first_call(GROUP, 0, *near)
    gown, gright, gdown0, gdown1, gcorner, gprobe = second_call(
        meta, object_slab, right, down0_one, down0_two, down1_one, corner_one, turned, hop, prop_now, prop_later, amp,
        down1_two, corner_two, dft,
    )
    side = lax.axis_size("row") // 4
    to_left_x = [(i, (i - side) % (4 * side)) for i in range(4 * side)]
    to_left_y = [(i, i - i % side + (i - 1) % side) for i in range(4 * side)]
    corner_back = shift(gcorner, "col", 1)
    down1_back = shift(gdown1, "row", 1)
    share = add_shares(gprobe, "col")
    gdown0, gright, share = lax.optimization_barrier((gdown0 + corner_back, gright, share))
    down0_back = shift(gdown0, "row", 1)
    right_back = shift(gright, "col", 1)
    share = ring_sum(ring_sum(share, to_left_x), to_left_y)
    right_back, down1_back, share = lax.optimization_barrier((right_back, down1_back, share))
    shares = hand_out(share, "col")
    object_grad, shares = add_call(gown, right_back, down0_back, down1_back, shares)
    return object_grad, shares.reshape(probe_wave.shape)


def solution(mesh):
    return jax.shard_map(
        body,
        mesh=mesh,
        in_specs=(
            P(None, "row", "col"),
            P(),
            P(("row", "col"), None),
            P(("row", "col")),
            P(("row", "col"), None, None),
        ),
        out_specs=(P(None, "row", "col"), P()),
        check_vma=False,
    )
```

```python
import math

import jax
import jax.numpy as jnp
import ml_dtypes
import numpy as np
from jax import lax
from jax.experimental import pallas as pl
from jax.experimental.pallas import tpu as pltpu
from jax.sharding import PartitionSpec as P

W = 256
HALF_W = 128
TC = 512
EXT = TC + W
SLOTS = 8
GROUP = 4
PREPARED = 2
ADDED = 2
CHUNK = 32
F32 = jnp.float32
BF16 = jnp.bfloat16

RE, IM, NEG_IM = 0, 1, 2


def split_host(table):
    high = table.astype(np.float32).astype(ml_dtypes.bfloat16)
    low = (table - high.astype(np.float64)).astype(np.float32).astype(ml_dtypes.bfloat16)
    return [high, low]


def hop_tables():
    index = np.arange(W)
    dft = np.exp(-2j * np.pi / W * (index[:, None] * index[None, :] % W)) / math.sqrt(W)
    freqs = np.where(index < W // 2, index, index - W) / W
    fresnel = np.exp(-1j * np.pi * (W / 4.0) * freqs**2)
    hop = np.conj(dft) @ (fresnel[:, None] * dft)
    hop = hop * np.exp(1j * np.pi * index / W)
    out = []
    for table in (hop, hop.T):
        for part in (table.real, table.imag, -table.imag):
            out.extend(split_host(part))
    return np.stack(out)


def dft_tables():
    index = np.arange(W)
    angles = 2.0 * np.pi / W * (index[:, None] + 0.5) * (index[None, :HALF_W] + 0.5)
    table = np.concatenate([np.cos(angles), np.sin(angles)], axis=1) / math.sqrt(W)
    return np.stack(split_host(table) + split_host(table.T))


def fold_tables():
    source = np.concatenate([np.arange(HALF_W), np.arange(W - 1, HALF_W - 1, -1)])
    table = np.zeros((W, W), np.float32)
    table[source, np.arange(W)] = 1.0
    return np.stack([table, table.T]).astype(ml_dtypes.bfloat16)


def split(x):
    high = x.astype(BF16)
    return high, (x - high.astype(F32)).astype(BF16)


def lanes(*parts):
    return jnp.concatenate(parts, axis=1)


def rows(*parts):
    return jnp.concatenate(parts, axis=0)


def dot(a, b):
    return jnp.dot(a, b, preferred_element_type=F32)


def half_right(field, tab, at):
    high, low = tab[2 * at], tab[2 * at + 1]
    rh, rl = split(field[0])
    ih, il = split(field[1])
    out = dot(rows(lanes(rh, rl, rh), lanes(ih, il, ih)), rows(high, high, low))
    return out[:W], out[W:]


def half_left(field, tab, at):
    high, low = tab[2 * at], tab[2 * at + 1]
    rh, rl = split(field[0])
    ih, il = split(field[1])
    out = dot(lanes(high, high, low), lanes(rows(rh, rl, rh), rows(ih, il, ih)))
    return out[:, :W], out[:, W:]


def hop_parts(tab, at, conj):
    im, neg = (IM, NEG_IM) if not conj else (NEG_IM, IM)

    def three(a, b):
        a, b = 2 * (3 * at + a), 2 * (3 * at + b)
        return [tab[a], tab[b], tab[a], tab[b], tab[a + 1], tab[b + 1]]

    return three(RE, neg), three(im, RE)


def hop_right(field, tab, at, conj):
    rh, rl = split(field[0])
    ih, il = split(field[1])
    to_re, to_im = hop_parts(tab, at, conj)
    out = dot(lanes(rh, ih, rl, il, rh, ih), lanes(rows(*to_re), rows(*to_im)))
    return out[:, :W], out[:, W:]


def hop_left(field, tab, at, conj):
    rh, rl = split(field[0])
    ih, il = split(field[1])
    to_re, to_im = hop_parts(tab, at, conj)
    out = dot(rows(lanes(*to_re), lanes(*to_im)), rows(rh, ih, rl, il, rh, ih))
    return out[:W], out[W:]


def spread_right(field):
    c, s = field[0][:, :HALF_W], field[0][:, HALF_W:]
    d, t = field[1][:, :HALF_W], field[1][:, HALF_W:]
    return lanes(c + t, t - c), lanes(d - s, -d - s)


def spread_left(field):
    c, s = field[0][:HALF_W], field[0][HALF_W:]
    d, t = field[1][:HALF_W], field[1][HALF_W:]
    return rows(c + t, t - c), rows(d - s, -d - s)


def gather_right(field):
    a, b = field[0][:, :HALF_W], field[0][:, HALF_W:]
    c, d = field[1][:, :HALF_W], field[1][:, HALF_W:]
    return lanes(a - b, -c - d), lanes(c - d, a + b)


def gather_left(field):
    a, b = field[0][:HALF_W], field[0][HALF_W:]
    c, d = field[1][:HALF_W], field[1][HALF_W:]
    return rows(a - b, -c - d), rows(c - d, a + b)


def times(a, b):
    return a[0] * b[0] - a[1] * b[1], a[0] * b[1] + a[1] * b[0]


def conj_times(a, b):
    return a[0] * b[0] + a[1] * b[1], a[0] * b[1] - a[1] * b[0]


def pair(ref, *at):
    return ref[(*at, 0)], ref[(*at, 1)]


def put(value, ref, *at):
    ref[(*at, 0)], ref[(*at, 1)] = value


def chunks(body):
    def step(i, carry):
        body(pl.multiple_of(i * CHUNK, CHUNK))
        return carry

    lax.fori_loop(0, W // CHUNK, step, 0)


def geometry(meta, slot):
    row, col = meta[1 + slot], meta[1 + SLOTS + slot]
    block = col // W
    first = pl.multiple_of(block * W, W)
    second = pl.multiple_of(block * W + W, W)
    return row, col - block * W, first, second


def masks(row, col, at):
    in_top = lax.broadcasted_iota(jnp.int32, (CHUNK, W), 0) + at >= row
    in_first = lax.broadcasted_iota(jnp.int32, (CHUNK, W), 1) >= col
    return in_top, in_first


def load_window(meta, slot, ext, planes, win, u):
    row, col, first, second = geometry(meta, slot)
    border = row // CHUNK

    def load(i, carry):
        here = pl.ds(pl.multiple_of(i * CHUNK, CHUNK), CHUNK)
        _, in_first = masks(row, col, 0)
        low = (i < border).astype(jnp.int32)
        for p in planes:
            win[u, p, here, :] = jnp.where(
                in_first, ext[low, p, here, pl.ds(first, W)], ext[low, p, here, pl.ds(second, W)]
            )
        return carry

    lax.fori_loop(0, W // CHUNK, load, 0, unroll=True)
    at = pl.multiple_of(border * CHUNK, CHUNK)
    here = pl.ds(at, CHUNK)
    in_top, in_first = masks(row, col, at)
    for p in planes:
        low = jnp.where(in_first, ext[1, p, here, pl.ds(first, W)], ext[1, p, here, pl.ds(second, W)])
        win[u, p, here, :] = jnp.where(in_top, win[u, p, here, :], low)


def add_window(meta, slot, win, u, planes, gext):
    row, col, first, second = geometry(meta, slot)
    border = row // CHUNK
    zero = jnp.zeros((CHUNK, W), F32)
    alive = slot < meta[0]

    def add(i, carry):
        at = pl.multiple_of(i * CHUNK, CHUNK)
        here = pl.ds(at, CHUNK)
        in_top, in_first = masks(row, col, at)
        low = (i < border).astype(jnp.int32)
        keep = jnp.logical_and(jnp.logical_or(in_top, i < border), alive)
        for p in planes:
            value = jnp.where(keep, win[u, p, here, :], zero)
            gext[low, p, here, pl.ds(first, W)] += jnp.where(in_first, value, zero)
            gext[low, p, here, pl.ds(second, W)] += jnp.where(in_first, zero, value)
        return carry

    lax.fori_loop(0, W // CHUNK, add, 0, unroll=True)
    at = pl.multiple_of(border * CHUNK, CHUNK)
    here = pl.ds(at, CHUNK)
    in_top, in_first = masks(row, col, at)
    for p in planes:
        value = jnp.where(jnp.logical_and(jnp.logical_not(in_top), alive), win[u, p, here, :], zero)
        gext[1, p, here, pl.ds(first, W)] += jnp.where(in_first, value, zero)
        gext[1, p, here, pl.ds(second, W)] += jnp.where(in_first, zero, value)


def turn_probe(meta, slot, twice, turned, u):
    row, col, _, _ = geometry(meta, slot)
    for p in range(2):
        here = pl.ds(W - row, W)
        turned[u, p] = pltpu.roll(lanes(twice[p, 0, here, :], twice[p, 1, here, :]), col, 1)


def add_probe(meta, slot, part, u, acc):
    row, col, _, _ = geometry(meta, slot)
    for p in range(2):
        here = pl.ds(W - row, W)
        value = jnp.where(slot < meta[0], pltpu.roll(part[u, p], W - col, 1), 0.0)
        acc[p, 0, here, :] += value[:, :HALF_W]
        acc[p, 1, here, :] += value[:, HALF_W:]


def tile_copies(refs, ext, sems):
    own, right, down0, down1, corner = refs
    return [
        (own, ext.at[0, :, :, pl.ds(0, TC)], sems.at[0]),
        (right, ext.at[0, :, :, pl.ds(TC, W)], sems.at[1]),
        (down0, ext.at[1, :, :, pl.ds(0, W)], sems.at[2]),
        (down1, ext.at[1, :, :, pl.ds(W, W)], sems.at[3]),
        (corner, ext.at[1, :, :, pl.ds(TC, W)], sems.at[4]),
    ]


def start_copies(copies):
    copies = [pltpu.make_async_copy(*copy) for copy in copies]
    for copy in copies:
        copy.start()
    return copies


def wait_copies(copies):
    for copy in copies:
        copy.wait()


def prepare_kernel(meta, probe, amp, fold, amp_out, turned, twice):
    step = pl.program_id(0)

    def fold_amplitudes(u):
        high = amp[u].astype(BF16)
        rest = amp[u] - high.astype(F32)
        mid = rest.astype(BF16)
        low = (rest - mid.astype(F32)).astype(BF16)
        right_way = dot(rows(high, mid, low), fold[0])
        out = dot(fold[1], lanes(*(right_way[i * W : (i + 1) * W].astype(BF16) for i in range(3))))
        amp_out[u] = out[:, :W] + out[:, W : 2 * W] + out[:, 2 * W :]

    @pl.when(step == 0)
    def double_probe():
        for p in range(2):
            for half in range(2):
                part = probe[p, :, half * HALF_W : (half + 1) * HALF_W]
                twice[p, half, :W, :] = part
                twice[p, half, W:, :] = part

    for u in range(PREPARED):
        fold_amplitudes(u)
        turn_probe(meta, step * PREPARED + u, twice, turned, u)


def first_kernel(meta, own, right, down0, down1, corner, turned, tab, prop, ext, win, sems):
    step = pl.program_id(0)

    @pl.when(step == 0)
    def begin():
        one = pl.ds(0, 2)
        refs = (own.at[one], right.at[one], down0, down1, corner)
        wait_copies(start_copies(tile_copies(refs, ext, sems)))

    @pl.when(step * GROUP < meta[0])
    def work():
        for u in range(GROUP):
            load_window(meta, step * GROUP + u, ext, (0, 1), win, u)
        fields = [times(pair(turned, u), pair(win, u)) for u in range(GROUP)]
        fields = [hop_right(f, tab, 0, False) for f in fields]
        fields = [hop_left(f, tab, 1, False) for f in fields]
        for u, f in enumerate(fields):
            put(f, prop, u)


def second_kernel(meta, own, right, down0_one, down0_two, down1_one, corner_one, turned_in, hop_in, prop_in, amp_in,
                  down1_two, corner_two, dft, gprobe, win,
                  ext, acc, turned, hop, prop, amp, sems):
    step = pl.program_id(0)
    group = range(GROUP)
    one, two = pl.ds(0, 2), pl.ds(2, 2)
    refs_one = (own.at[one], right.at[one], down0_one, down1_one, corner_one)
    refs_two = (own.at[two], right.at[two], down0_two, down1_two, corner_two)
    copies_one = tile_copies(refs_one, ext.at[:, one], sems.at[0])
    copies_two = tile_copies(refs_two, ext.at[:, two], sems.at[1])
    now, later = pl.ds(0, GROUP), pl.ds(GROUP, SLOTS - GROUP)
    copies_now = copies_two + [
        (prop_in.at[now], prop.at[now], sems.at[2, 0]),
        (amp_in.at[now], amp.at[now], sems.at[2, 1]),
    ]
    copies_later = [(hop_in, hop, sems.at[2, 2])] + copies_one + [
        (turned_in, turned, sems.at[2, 3]),
        (prop_in.at[later], prop.at[later], sems.at[2, 4]),
        (amp_in.at[later], amp.at[later], sems.at[2, 5]),
    ]

    @pl.when(step == 0)
    def begin():
        started = start_copies(copies_now)
        start_copies(copies_later)
        acc[...] = jnp.zeros_like(acc)
        wait_copies(started)

    live = step * GROUP < meta[0]

    @pl.when(live)
    def stage_one():
        for u in group:
            load_window(meta, step * GROUP + u, ext, (2, 3), win, u)
        fields = [times(pair(prop, step * GROUP + u), (win[u, 2], win[u, 3])) for u in group]
        fields = [spread_left(half_left(f, dft, 1)) for f in fields]
        fields = [spread_right(half_right(f, dft, 0)) for f in fields]
        chi = []
        for u, f in enumerate(fields):
            factor = 1.0 - amp[step * GROUP + u] * lax.rsqrt(f[0] * f[0] + f[1] * f[1] + 1.0)
            chi.append((factor * f[0], factor * f[1]))
        fields = [half_right(gather_right(f), dft, 1) for f in chi]
        fields = [half_left(gather_left(f), dft, 0) for f in fields]
        waves = [conj_times((win[u, 2], win[u, 3]), f) for u, f in enumerate(fields)]
        for u, f in enumerate(fields):
            win[u, 2], win[u, 3] = conj_times(pair(prop, step * GROUP + u), f)
        for u, f in enumerate(waves):
            put(f, prop, step * GROUP + u)

    @pl.when(step == 0)
    def arrive():
        wait_copies([pltpu.make_async_copy(*copy) for copy in copies_later])

    @pl.when(live)
    def stage_two():
        for u in group:
            load_window(meta, step * GROUP + u, ext, (0, 1), win, u)
        waves = [hop_left(pair(prop, step * GROUP + u), hop, 0, True) for u in group]
        waves = [hop_right(f, hop, 1, True) for f in waves]
        for u, wave in enumerate(waves):
            probe = pair(turned, step * GROUP + u)
            grad, part = conj_times(probe, wave), conj_times(pair(win, u), wave)
            put(grad, win, u)
            put(part, prop, step * GROUP + u)

        def finish(slot, u):
            add_probe(meta, slot, prop, slot, acc)

        for u in group:
            slot = step * GROUP + u
            finish(slot, u)

    @pl.when(step == SLOTS // GROUP - 1)
    def end():
        for p in range(2):
            gprobe[p] = lanes(acc[p, 0, :W, :] + acc[p, 0, W:, :], acc[p, 1, :W, :] + acc[p, 1, W:, :])


def third_kernel(meta, grads, gown, gright, gdown0, gdown1, gcorner, gext, sems):
    step = pl.program_id(0)

    @pl.when(step == 0)
    def begin():
        gext[...] = jnp.zeros_like(gext)

    for u in range(ADDED):
        slot = step * ADDED + u
        pl.when(slot < meta[0])(lambda: add_window(meta, slot, grads, u, range(4), gext))

    @pl.when(step == SLOTS // ADDED - 1)
    def end():
        wait_copies(start_copies([
            (gext.at[1, :, :, pl.ds(W, W)], gdown1, sems.at[0]),
            (gext.at[1, :, :, pl.ds(TC, W)], gcorner, sems.at[1]),
            (gext.at[1, :, :, pl.ds(0, W)], gdown0, sems.at[2]),
            (gext.at[0, :, :, pl.ds(TC, W)], gright, sems.at[3]),
            (gext.at[0, :, :, pl.ds(0, TC)], gown, sems.at[4]),
        ]))


ANYWHERE = pl.BlockSpec(memory_space=pl.ANY)
WHOLE = pl.BlockSpec(memory_space=pltpu.VMEM)
SCALARS = pl.BlockSpec(memory_space=pltpu.SMEM)
FIELDS = pl.BlockSpec((GROUP, 2, W, W), lambda i: (i, 0, 0, 0))
PLANES = pl.BlockSpec((GROUP, W, W), lambda i: (i, 0, 0))


def shape(*dims):
    return jax.ShapeDtypeStruct(dims, F32)


FIELDS_SHAPE = shape(SLOTS, 2, W, W)


def call(kernel, steps, in_specs, out_specs, out_shape, scratch, products, mebibytes):
    return pl.pallas_call(
        kernel,
        grid=(steps,),
        in_specs=in_specs,
        out_specs=out_specs,
        out_shape=out_shape,
        scratch_shapes=scratch,
        compiler_params=pltpu.CompilerParams(
            vmem_limit_bytes=mebibytes * 2**20, dimension_semantics=("arbitrary",)
        ),
        cost_estimate=pl.CostEstimate(
            flops=SLOTS * products * 2 * W**3, bytes_accessed=products * 2**18, transcendentals=0
        ),
    )


def prepare_call(*args):
    return call(
        prepare_kernel,
        SLOTS // PREPARED,
        [SCALARS, WHOLE, pl.BlockSpec((PREPARED, W, W), lambda i: (i, 0, 0)), WHOLE],
        [
            pl.BlockSpec((PREPARED, W, W), lambda i: (i, 0, 0)),
            pl.BlockSpec((PREPARED, 2, W, W), lambda i: (i, 0, 0, 0)),
        ],
        [shape(SLOTS, W, W), FIELDS_SHAPE],
        [pltpu.VMEM((2, 2, 2 * W, HALF_W), F32)],
        0,
        16,
    )(*args)


def first_call(*args):
    return call(
        first_kernel,
        SLOTS // GROUP,
        [SCALARS] + [ANYWHERE] * 3 + [WHOLE, WHOLE, FIELDS, WHOLE],
        FIELDS,
        FIELDS_SHAPE,
        [
            pltpu.VMEM((2, 2, W, EXT), F32),
            pltpu.VMEM((GROUP, 2, W, W), F32),
            pltpu.SemaphoreType.DMA((5,)),
        ],
        24,
        52,
    )(*args)


def second_call(*args):
    return call(
        second_kernel,
        SLOTS // GROUP,
        [SCALARS] + [ANYWHERE] * 10 + [WHOLE] * 3,
        [WHOLE, pl.BlockSpec((GROUP, 4, W, W), lambda i: (i, 0, 0, 0))],
        [shape(2, W, W), shape(SLOTS, 4, W, W)],
        [
            pltpu.VMEM((2, 4, W, EXT), F32),
            pltpu.VMEM((2, 2, 2 * W, HALF_W), F32),
            pltpu.VMEM((SLOTS, 2, W, W), F32),
            pltpu.VMEM((12, W, W), BF16),
            pltpu.VMEM((SLOTS, 2, W, W), F32),
            pltpu.VMEM((SLOTS, W, W), F32),
            pltpu.SemaphoreType.DMA((3, 6)),
        ],
        48,
        54,
    )(*args)


def third_call(*args):
    return call(
        third_kernel,
        SLOTS // ADDED,
        [SCALARS, pl.BlockSpec((ADDED, 4, W, W), lambda i: (i, 0, 0, 0))],
        [ANYWHERE] * 5,
        [shape(4, W, TC)] + [shape(4, W, W)] * 4,
        [pltpu.VMEM((2, 4, W, EXT), F32), pltpu.SemaphoreType.DMA((5,))],
        24,
        40,
    )(*args)


def add_kernel(base, right, down0, down1, out):
    first, second = pl.ds(0, W), pl.ds(W, W)
    out[:, :, first] = base[:, :, first] + (right[...] + down0[...])
    out[:, :, second] = base[:, :, second] + down1[...]


def add_call(*args):
    whole = pl.BlockSpec((1, W, TC), lambda i: (i, 0, 0))
    part = pl.BlockSpec((1, W, W), lambda i: (i, 0, 0))
    return pl.pallas_call(
        add_kernel,
        grid=(4,),
        in_specs=[whole] + [part] * 3,
        out_specs=whole,
        out_shape=shape(4, W, TC),
        compiler_params=pltpu.CompilerParams(vmem_limit_bytes=8 * 2**20),
        cost_estimate=pl.CostEstimate(flops=2**20, bytes_accessed=7 * 2**20, transcendentals=0),
    )(*args)


def shift(value, axis, steps):
    count = lax.axis_size(axis)
    first, last = (max(0, -steps), min(count, count - steps))
    return lax.ppermute(value, axis, [(source, source + steps) for source in range(first, last)])


def add_shares(value, axis):
    count = lax.axis_size(axis)
    shares = value.reshape(count, -1, value.shape[-1])
    return lax.all_to_all(shares, axis, 0, 0, tiled=True).sum(axis=0)


def hand_out(value, axis):
    spread = jnp.broadcast_to(value[None], (lax.axis_size(axis), *value.shape))
    return lax.all_to_all(spread, axis, 0, 0, tiled=True)


def ring_sum(value, pairs):
    first = lax.ppermute(value, "row", pairs)
    second = lax.ppermute(first, "row", pairs)
    third = lax.ppermute(second, "row", pairs)
    return (value + second) + (first + third)


def ring_sum_after(value, pairs, arrived):
    first = lax.ppermute(value, "row", pairs)
    second = lax.ppermute(first, "row", pairs)
    second, arrived = lax.optimization_barrier((second, arrived))
    third = lax.ppermute(second, "row", pairs)
    return (value + second) + (first + third), arrived


def body(object_slab, probe_wave, scan_offsets, live_counts, amplitudes):
    rows_tile, cols_tile = object_slab.shape[1:]
    local_rows = scan_offsets[:, 0] - lax.axis_index("row") * rows_tile
    local_cols = scan_offsets[:, 1] - lax.axis_index("col") * cols_tile
    meta = jnp.concatenate([live_counts, local_rows, local_cols])
    hop, dft, fold = jnp.asarray(hop_tables()), jnp.asarray(dft_tables()), jnp.asarray(fold_tables())
    first_part, rest = lax.optimization_barrier((object_slab[:2, :, :W], object_slab))
    down0_one = shift(first_part, "row", -1)
    down1_one = shift(rest[:2, :, W:], "row", -1)
    right = shift(rest[:, :, :W], "col", -1)
    down0_two = shift(rest[2:, :, :W], "row", -1)
    amp, turned = prepare_call(meta, probe_wave, amplitudes, fold)
    down0_one, turned, last_part = lax.optimization_barrier((down0_one, turned, rest[2:, :, W:]))
    corner_one = shift(down0_one, "col", -1)
    down1_two = shift(last_part, "row", -1)
    prop = first_call(meta, object_slab, right, down0_one, down1_one, corner_one, turned, hop)
    down0_two, prop = lax.optimization_barrier((down0_two, prop))
    corner_two = shift(down0_two, "col", -1)
    gprobe, grads = second_call(
        meta, object_slab, right, down0_one, down0_two, down1_one, corner_one, turned, hop, prop, amp,
        down1_two, corner_two, dft,
    )
    share = add_shares(gprobe, "col")
    gown, gright, gdown0, gdown1, gcorner = third_call(meta, grads)
    side = lax.axis_size("row") // 4
    to_left_x = [(i, (i - side) % (4 * side)) for i in range(4 * side)]
    to_left_y = [(i, i - i % side + (i - 1) % side) for i in range(4 * side)]
    gcorner, gright, gdown0, gdown1, share = lax.optimization_barrier((gcorner, gright, gdown0, gdown1, share))
    corner_back = shift(gcorner, "col", 1)
    down1_back = shift(gdown1, "row", 1)
    gdown0 = gdown0 + corner_back
    down0_back = shift(gdown0, "row", 1)
    right_back = shift(gright, "col", 1)
    share, down1_back = ring_sum_after(ring_sum(share, to_left_x), to_left_y, down1_back)
    right_back, share = lax.optimization_barrier((right_back, share))
    probe_grad = hand_out(share, "col").reshape(probe_wave.shape)
    return add_call(gown, right_back, down0_back, down1_back), probe_grad


def solution(mesh):
    return jax.shard_map(
        body,
        mesh=mesh,
        in_specs=(
            P(None, "row", "col"),
            P(),
            P(("row", "col"), None),
            P(("row", "col")),
            P(("row", "col"), None, None),
        ),
        out_specs=(P(None, "row", "col"), P()),
        check_vma=False,
    )
```

```python
import math

import jax
import jax.numpy as jnp
import ml_dtypes
import numpy as np
from jax import lax
from jax.experimental import pallas as pl
from jax.experimental.pallas import tpu as pltpu
from jax.sharding import PartitionSpec as P

W = 256
HALF_W = 128
TC = 512
EXT = TC + W
SLOTS = 8
GROUP = 4
PREPARED = 2
ADDED = 2
CHUNK = 32
F32 = jnp.float32
BF16 = jnp.bfloat16

RE, IM, NEG_IM = 0, 1, 2


def split_host(table):
    high = table.astype(np.float32).astype(ml_dtypes.bfloat16)
    low = (table - high.astype(np.float64)).astype(np.float32).astype(ml_dtypes.bfloat16)
    return [high, low]


def hop_tables():
    index = np.arange(W)
    dft = np.exp(-2j * np.pi / W * (index[:, None] * index[None, :] % W)) / math.sqrt(W)
    freqs = np.where(index < W // 2, index, index - W) / W
    fresnel = np.exp(-1j * np.pi * (W / 4.0) * freqs**2)
    hop = np.conj(dft) @ (fresnel[:, None] * dft)
    hop = hop * np.exp(1j * np.pi * index / W)
    out = []
    for table in (hop, hop.T):
        for part in (table.real, table.imag, -table.imag):
            out.extend(split_host(part))
    return np.stack(out)


def dft_tables():
    index = np.arange(W)
    angles = 2.0 * np.pi / W * (index[:, None] + 0.5) * (index[None, :HALF_W] + 0.5)
    table = np.concatenate([np.cos(angles), np.sin(angles)], axis=1) / math.sqrt(W)
    return np.stack(split_host(table) + split_host(table.T))


def fold_tables():
    source = np.concatenate([np.arange(HALF_W), np.arange(W - 1, HALF_W - 1, -1)])
    table = np.zeros((W, W), np.float32)
    table[source, np.arange(W)] = 1.0
    return np.stack([table, table.T]).astype(ml_dtypes.bfloat16)


def split(x):
    high = x.astype(BF16)
    return high, (x - high.astype(F32)).astype(BF16)


def lanes(*parts):
    return jnp.concatenate(parts, axis=1)


def rows(*parts):
    return jnp.concatenate(parts, axis=0)


def dot(a, b):
    return jnp.dot(a, b, preferred_element_type=F32)


def half_right(field, tab, at):
    high, low = tab[2 * at], tab[2 * at + 1]
    rh, rl = split(field[0])
    ih, il = split(field[1])
    out = dot(rows(lanes(rh, rl, rh), lanes(ih, il, ih)), rows(high, high, low))
    return out[:W], out[W:]


def half_left(field, tab, at):
    high, low = tab[2 * at], tab[2 * at + 1]
    rh, rl = split(field[0])
    ih, il = split(field[1])
    out = dot(lanes(high, high, low), lanes(rows(rh, rl, rh), rows(ih, il, ih)))
    return out[:, :W], out[:, W:]


def hop_parts(tab, at, conj):
    im, neg = (IM, NEG_IM) if not conj else (NEG_IM, IM)

    def three(a, b):
        a, b = 2 * (3 * at + a), 2 * (3 * at + b)
        return [tab[a], tab[b], tab[a], tab[b], tab[a + 1], tab[b + 1]]

    return three(RE, neg), three(im, RE)


def hop_right(field, tab, at, conj):
    rh, rl = split(field[0])
    ih, il = split(field[1])
    to_re, to_im = hop_parts(tab, at, conj)
    out = dot(lanes(rh, ih, rl, il, rh, ih), lanes(rows(*to_re), rows(*to_im)))
    return out[:, :W], out[:, W:]


def hop_left(field, tab, at, conj):
    rh, rl = split(field[0])
    ih, il = split(field[1])
    to_re, to_im = hop_parts(tab, at, conj)
    out = dot(rows(lanes(*to_re), lanes(*to_im)), rows(rh, ih, rl, il, rh, ih))
    return out[:W], out[W:]


def spread_right(field):
    c, s = field[0][:, :HALF_W], field[0][:, HALF_W:]
    d, t = field[1][:, :HALF_W], field[1][:, HALF_W:]
    return lanes(c + t, t - c), lanes(d - s, -d - s)


def spread_left(field):
    c, s = field[0][:HALF_W], field[0][HALF_W:]
    d, t = field[1][:HALF_W], field[1][HALF_W:]
    return rows(c + t, t - c), rows(d - s, -d - s)


def gather_right(field):
    a, b = field[0][:, :HALF_W], field[0][:, HALF_W:]
    c, d = field[1][:, :HALF_W], field[1][:, HALF_W:]
    return lanes(a - b, -c - d), lanes(c - d, a + b)


def gather_left(field):
    a, b = field[0][:HALF_W], field[0][HALF_W:]
    c, d = field[1][:HALF_W], field[1][HALF_W:]
    return rows(a - b, -c - d), rows(c - d, a + b)


def times(a, b):
    return a[0] * b[0] - a[1] * b[1], a[0] * b[1] + a[1] * b[0]


def conj_times(a, b):
    return a[0] * b[0] + a[1] * b[1], a[0] * b[1] - a[1] * b[0]


def pair(ref, *at):
    return ref[(*at, 0)], ref[(*at, 1)]


def put(value, ref, *at):
    ref[(*at, 0)], ref[(*at, 1)] = value


def chunks(body):
    def step(i, carry):
        body(pl.multiple_of(i * CHUNK, CHUNK))
        return carry

    lax.fori_loop(0, W // CHUNK, step, 0)


def geometry(meta, slot):
    row, col = meta[1 + slot], meta[1 + SLOTS + slot]
    block = col // W
    first = pl.multiple_of(block * W, W)
    second = pl.multiple_of(block * W + W, W)
    return row, col - block * W, first, second


def masks(row, col, at):
    in_top = lax.broadcasted_iota(jnp.int32, (CHUNK, W), 0) + at >= row
    in_first = lax.broadcasted_iota(jnp.int32, (CHUNK, W), 1) >= col
    return in_top, in_first


def load_window(meta, slot, ext, planes, win, u):
    row, col, first, second = geometry(meta, slot)
    border = row // CHUNK

    def load(i, carry):
        here = pl.ds(pl.multiple_of(i * CHUNK, CHUNK), CHUNK)
        _, in_first = masks(row, col, 0)
        low = (i < border).astype(jnp.int32)
        for p in planes:
            win[u, p, here, :] = jnp.where(
                in_first, ext[low, p, here, pl.ds(first, W)], ext[low, p, here, pl.ds(second, W)]
            )
        return carry

    lax.fori_loop(0, W // CHUNK, load, 0, unroll=True)
    at = pl.multiple_of(border * CHUNK, CHUNK)
    here = pl.ds(at, CHUNK)
    in_top, in_first = masks(row, col, at)
    for p in planes:
        low = jnp.where(in_first, ext[1, p, here, pl.ds(first, W)], ext[1, p, here, pl.ds(second, W)])
        win[u, p, here, :] = jnp.where(in_top, win[u, p, here, :], low)


def add_window(meta, slot, win, u, planes, gext):
    row, col, first, second = geometry(meta, slot)
    border = row // CHUNK
    zero = jnp.zeros((CHUNK, W), F32)
    alive = slot < meta[0]

    def add(i, carry):
        at = pl.multiple_of(i * CHUNK, CHUNK)
        here = pl.ds(at, CHUNK)
        in_top, in_first = masks(row, col, at)
        low = (i < border).astype(jnp.int32)
        keep = jnp.logical_and(jnp.logical_or(in_top, i < border), alive)
        for p in planes:
            value = jnp.where(keep, win[u, p, here, :], zero)
            gext[low, p, here, pl.ds(first, W)] += jnp.where(in_first, value, zero)
            gext[low, p, here, pl.ds(second, W)] += jnp.where(in_first, zero, value)
        return carry

    lax.fori_loop(0, W // CHUNK, add, 0, unroll=True)
    at = pl.multiple_of(border * CHUNK, CHUNK)
    here = pl.ds(at, CHUNK)
    in_top, in_first = masks(row, col, at)
    for p in planes:
        value = jnp.where(jnp.logical_and(jnp.logical_not(in_top), alive), win[u, p, here, :], zero)
        gext[1, p, here, pl.ds(first, W)] += jnp.where(in_first, value, zero)
        gext[1, p, here, pl.ds(second, W)] += jnp.where(in_first, zero, value)


def turn_probe(meta, slot, twice, turned, u):
    row, col, _, _ = geometry(meta, slot)
    for p in range(2):
        here = pl.ds(W - row, W)
        turned[u, p] = pltpu.roll(lanes(twice[p, 0, here, :], twice[p, 1, here, :]), col, 1)


def add_probe(meta, slot, part, u, acc):
    row, col, _, _ = geometry(meta, slot)
    for p in range(2):
        here = pl.ds(W - row, W)
        value = jnp.where(slot < meta[0], pltpu.roll(part[u, p], W - col, 1), 0.0)
        acc[p, 0, here, :] += value[:, :HALF_W]
        acc[p, 1, here, :] += value[:, HALF_W:]


def tile_copies(refs, ext, sems):
    own, right, down0, down1, corner = refs
    return [
        (own, ext.at[0, :, :, pl.ds(0, TC)], sems.at[0]),
        (right, ext.at[0, :, :, pl.ds(TC, W)], sems.at[1]),
        (down0, ext.at[1, :, :, pl.ds(0, W)], sems.at[2]),
        (down1, ext.at[1, :, :, pl.ds(W, W)], sems.at[3]),
        (corner, ext.at[1, :, :, pl.ds(TC, W)], sems.at[4]),
    ]


def start_copies(copies):
    copies = [pltpu.make_async_copy(*copy) for copy in copies]
    for copy in copies:
        copy.start()
    return copies


def wait_copies(copies):
    for copy in copies:
        copy.wait()


def prepare_kernel(meta, probe, amp, fold, amp_out, turned, twice):
    step = pl.program_id(0)

    def fold_amplitudes(u):
        high = amp[u].astype(BF16)
        rest = amp[u] - high.astype(F32)
        mid = rest.astype(BF16)
        low = (rest - mid.astype(F32)).astype(BF16)
        right_way = dot(rows(high, mid, low), fold[0])
        out = dot(fold[1], lanes(*(right_way[i * W : (i + 1) * W].astype(BF16) for i in range(3))))
        amp_out[u] = out[:, :W] + out[:, W : 2 * W] + out[:, 2 * W :]

    @pl.when(step == 0)
    def double_probe():
        for p in range(2):
            for half in range(2):
                part = probe[p, :, half * HALF_W : (half + 1) * HALF_W]
                twice[p, half, :W, :] = part
                twice[p, half, W:, :] = part

    for u in range(PREPARED):
        fold_amplitudes(u)
        turn_probe(meta, step * PREPARED + u, twice, turned, u)


def first_kernel(meta, own, right, down0, down1, corner, turned, tab, prop, ext, win, sems):
    step = pl.program_id(0)

    @pl.when(step == 0)
    def begin():
        one = pl.ds(0, 2)
        refs = (own.at[one], right.at[one], down0, down1, corner)
        wait_copies(start_copies(tile_copies(refs, ext, sems)))

    @pl.when(step * GROUP < meta[0])
    def work():
        for u in range(GROUP):
            load_window(meta, step * GROUP + u, ext, (0, 1), win, u)
        fields = [times(pair(turned, u), pair(win, u)) for u in range(GROUP)]
        fields = [hop_right(f, tab, 0, False) for f in fields]
        fields = [hop_left(f, tab, 1, False) for f in fields]
        for u, f in enumerate(fields):
            put(f, prop, u)


def second_kernel(meta, own, right, down0_one, down0_two, down1_one, corner_one, turned_in, hop_in, prop_in, amp_in,
                  down1_two, corner_two, dft, gprobe, win,
                  ext, acc, turned, hop, prop, amp, sems):
    step = pl.program_id(0)
    group = range(GROUP)
    one, two = pl.ds(0, 2), pl.ds(2, 2)
    refs_one = (own.at[one], right.at[one], down0_one, down1_one, corner_one)
    refs_two = (own.at[two], right.at[two], down0_two, down1_two, corner_two)
    copies_one = tile_copies(refs_one, ext.at[:, one], sems.at[0])
    copies_two = tile_copies(refs_two, ext.at[:, two], sems.at[1])
    now, later = pl.ds(0, GROUP), pl.ds(GROUP, SLOTS - GROUP)
    copies_now = copies_two + [
        (prop_in.at[now], prop.at[now], sems.at[2, 0]),
        (amp_in.at[now], amp.at[now], sems.at[2, 1]),
    ]
    copies_later = [(hop_in, hop, sems.at[2, 2])] + copies_one + [
        (turned_in, turned, sems.at[2, 3]),
        (prop_in.at[later], prop.at[later], sems.at[2, 4]),
        (amp_in.at[later], amp.at[later], sems.at[2, 5]),
    ]

    @pl.when(step == 0)
    def begin():
        started = start_copies(copies_now)
        start_copies(copies_later)
        acc[...] = jnp.zeros_like(acc)
        wait_copies(started)

    live = step * GROUP < meta[0]

    @pl.when(live)
    def stage_one():
        for u in group:
            load_window(meta, step * GROUP + u, ext, (2, 3), win, u)
        fields = [times(pair(prop, step * GROUP + u), (win[u, 2], win[u, 3])) for u in group]
        fields = [spread_left(half_left(f, dft, 1)) for f in fields]
        fields = [spread_right(half_right(f, dft, 0)) for f in fields]
        chi = []
        for u, f in enumerate(fields):
            factor = 1.0 - amp[step * GROUP + u] * lax.rsqrt(f[0] * f[0] + f[1] * f[1] + 1.0)
            chi.append((factor * f[0], factor * f[1]))
        fields = [half_right(gather_right(f), dft, 1) for f in chi]
        fields = [half_left(gather_left(f), dft, 0) for f in fields]
        waves = [conj_times((win[u, 2], win[u, 3]), f) for u, f in enumerate(fields)]
        for u, f in enumerate(fields):
            win[u, 2], win[u, 3] = conj_times(pair(prop, step * GROUP + u), f)
        for u, f in enumerate(waves):
            put(f, prop, step * GROUP + u)

    @pl.when(step == 0)
    def arrive():
        wait_copies([pltpu.make_async_copy(*copy) for copy in copies_later])

    @pl.when(live)
    def stage_two():
        for u in group:
            load_window(meta, step * GROUP + u, ext, (0, 1), win, u)
        waves = [hop_left(pair(prop, step * GROUP + u), hop, 0, True) for u in group]
        waves = [hop_right(f, hop, 1, True) for f in waves]
        for u, wave in enumerate(waves):
            probe = pair(turned, step * GROUP + u)
            grad, part = conj_times(probe, wave), conj_times(pair(win, u), wave)
            put(grad, win, u)
            put(part, prop, step * GROUP + u)

        def finish(slot, u):
            add_probe(meta, slot, prop, slot, acc)

        for u in group:
            slot = step * GROUP + u
            finish(slot, u)

    @pl.when(step == SLOTS // GROUP - 1)
    def end():
        for p in range(2):
            gprobe[p] = lanes(acc[p, 0, :W, :] + acc[p, 0, W:, :], acc[p, 1, :W, :] + acc[p, 1, W:, :])


def third_kernel(meta, grads, gown, gright, gdown0, gdown1, gcorner, gext, sems):
    step = pl.program_id(0)

    @pl.when(step == 0)
    def begin():
        gext[...] = jnp.zeros_like(gext)

    for u in range(ADDED):
        slot = step * ADDED + u
        pl.when(slot < meta[0])(lambda: add_window(meta, slot, grads, u, range(4), gext))

    @pl.when(step == SLOTS // ADDED - 1)
    def end():
        wait_copies(start_copies([
            (gext.at[1, :, :, pl.ds(W, W)], gdown1, sems.at[0]),
            (gext.at[1, :, :, pl.ds(TC, W)], gcorner, sems.at[1]),
            (gext.at[1, :, :, pl.ds(0, W)], gdown0, sems.at[2]),
            (gext.at[0, :, :, pl.ds(TC, W)], gright, sems.at[3]),
            (gext.at[0, :, :, pl.ds(0, TC)], gown, sems.at[4]),
        ]))


ANYWHERE = pl.BlockSpec(memory_space=pl.ANY)
WHOLE = pl.BlockSpec(memory_space=pltpu.VMEM)
SCALARS = pl.BlockSpec(memory_space=pltpu.SMEM)
FIELDS = pl.BlockSpec((GROUP, 2, W, W), lambda i: (i, 0, 0, 0))
PLANES = pl.BlockSpec((GROUP, W, W), lambda i: (i, 0, 0))


def shape(*dims):
    return jax.ShapeDtypeStruct(dims, F32)


FIELDS_SHAPE = shape(SLOTS, 2, W, W)


def call(kernel, steps, in_specs, out_specs, out_shape, scratch, products, mebibytes):
    return pl.pallas_call(
        kernel,
        grid=(steps,),
        in_specs=in_specs,
        out_specs=out_specs,
        out_shape=out_shape,
        scratch_shapes=scratch,
        compiler_params=pltpu.CompilerParams(
            vmem_limit_bytes=mebibytes * 2**20, dimension_semantics=("arbitrary",)
        ),
        cost_estimate=pl.CostEstimate(
            flops=SLOTS * products * 2 * W**3, bytes_accessed=products * 2**18, transcendentals=0
        ),
    )


def prepare_call(*args):
    return call(
        prepare_kernel,
        SLOTS // PREPARED,
        [SCALARS, WHOLE, pl.BlockSpec((PREPARED, W, W), lambda i: (i, 0, 0)), WHOLE],
        [
            pl.BlockSpec((PREPARED, W, W), lambda i: (i, 0, 0)),
            pl.BlockSpec((PREPARED, 2, W, W), lambda i: (i, 0, 0, 0)),
        ],
        [shape(SLOTS, W, W), FIELDS_SHAPE],
        [pltpu.VMEM((2, 2, 2 * W, HALF_W), F32)],
        0,
        16,
    )(*args)


def first_call(*args):
    return call(
        first_kernel,
        SLOTS // GROUP,
        [SCALARS] + [ANYWHERE] * 3 + [WHOLE, WHOLE, FIELDS, WHOLE],
        FIELDS,
        FIELDS_SHAPE,
        [
            pltpu.VMEM((2, 2, W, EXT), F32),
            pltpu.VMEM((GROUP, 2, W, W), F32),
            pltpu.SemaphoreType.DMA((5,)),
        ],
        24,
        52,
    )(*args)


def second_call(*args):
    return call(
        second_kernel,
        SLOTS // GROUP,
        [SCALARS] + [ANYWHERE] * 10 + [WHOLE] * 3,
        [WHOLE, pl.BlockSpec((GROUP, 4, W, W), lambda i: (i, 0, 0, 0))],
        [shape(2, W, W), shape(SLOTS, 4, W, W)],
        [
            pltpu.VMEM((2, 4, W, EXT), F32),
            pltpu.VMEM((2, 2, 2 * W, HALF_W), F32),
            pltpu.VMEM((SLOTS, 2, W, W), F32),
            pltpu.VMEM((12, W, W), BF16),
            pltpu.VMEM((SLOTS, 2, W, W), F32),
            pltpu.VMEM((SLOTS, W, W), F32),
            pltpu.SemaphoreType.DMA((3, 6)),
        ],
        48,
        54,
    )(*args)


def third_call(*args):
    return call(
        third_kernel,
        SLOTS // ADDED,
        [SCALARS, pl.BlockSpec((ADDED, 4, W, W), lambda i: (i, 0, 0, 0))],
        [ANYWHERE] * 5,
        [shape(4, W, TC)] + [shape(4, W, W)] * 4,
        [pltpu.VMEM((2, 4, W, EXT), F32), pltpu.SemaphoreType.DMA((5,))],
        24,
        60,
    )(*args)


def add_kernel(base, right, down0, down1, out):
    first, second = pl.ds(0, W), pl.ds(W, W)
    out[:, :, first] = base[:, :, first] + (right[...] + down0[...])
    out[:, :, second] = base[:, :, second] + down1[...]


def add_call(*args):
    whole = pl.BlockSpec((1, W, TC), lambda i: (i, 0, 0))
    part = pl.BlockSpec((1, W, W), lambda i: (i, 0, 0))
    return pl.pallas_call(
        add_kernel,
        grid=(4,),
        in_specs=[whole] + [part] * 3,
        out_specs=whole,
        out_shape=shape(4, W, TC),
        compiler_params=pltpu.CompilerParams(vmem_limit_bytes=8 * 2**20),
        cost_estimate=pl.CostEstimate(flops=2**20, bytes_accessed=7 * 2**20, transcendentals=0),
    )(*args)


def shift(value, axis, steps):
    count = lax.axis_size(axis)
    first, last = (max(0, -steps), min(count, count - steps))
    return lax.ppermute(value, axis, [(source, source + steps) for source in range(first, last)])


def add_shares(value, axis):
    count = lax.axis_size(axis)
    shares = value.reshape(count, -1, value.shape[-1])
    return lax.all_to_all(shares, axis, 0, 0, tiled=True).sum(axis=0)


def hand_out(value, axis):
    spread = jnp.broadcast_to(value[None], (lax.axis_size(axis), *value.shape))
    return lax.all_to_all(spread, axis, 0, 0, tiled=True)


def ring_sum(value, pairs):
    first = lax.ppermute(value, "row", pairs)
    second = lax.ppermute(first, "row", pairs)
    third = lax.ppermute(second, "row", pairs)
    return (value + second) + (first + third)


def ring_sum_after(value, pairs, arrived):
    first = lax.ppermute(value, "row", pairs)
    second = lax.ppermute(first, "row", pairs)
    second, arrived = lax.optimization_barrier((second, arrived))
    third = lax.ppermute(second, "row", pairs)
    return (value + second) + (first + third), arrived


def body(object_slab, probe_wave, scan_offsets, live_counts, amplitudes):
    rows_tile, cols_tile = object_slab.shape[1:]
    local_rows = scan_offsets[:, 0] - lax.axis_index("row") * rows_tile
    local_cols = scan_offsets[:, 1] - lax.axis_index("col") * cols_tile
    meta = jnp.concatenate([live_counts, local_rows, local_cols])
    hop, dft, fold = jnp.asarray(hop_tables()), jnp.asarray(dft_tables()), jnp.asarray(fold_tables())
    first_part, rest = lax.optimization_barrier((object_slab[:2, :, :W], object_slab))
    down0_one = shift(first_part, "row", -1)
    down1_one = shift(rest[:2, :, W:], "row", -1)
    right = shift(rest[:, :, :W], "col", -1)
    down0_two = shift(rest[2:, :, :W], "row", -1)
    amp, turned = prepare_call(meta, probe_wave, amplitudes, fold)
    down0_one, turned, last_part = lax.optimization_barrier((down0_one, turned, rest[2:, :, W:]))
    corner_one = shift(down0_one, "col", -1)
    down1_two = shift(last_part, "row", -1)
    prop = first_call(meta, object_slab, right, down0_one, down1_one, corner_one, turned, hop)
    down0_two, prop = lax.optimization_barrier((down0_two, prop))
    corner_two = shift(down0_two, "col", -1)
    gprobe, grads = second_call(
        meta, object_slab, right, down0_one, down0_two, down1_one, corner_one, turned, hop, prop, amp,
        down1_two, corner_two, dft,
    )
    share = add_shares(gprobe, "col")
    gown, gright, gdown0, gdown1, gcorner = third_call(meta, grads)
    side = lax.axis_size("row") // 4
    to_left_x = [(i, (i - side) % (4 * side)) for i in range(4 * side)]
    to_left_y = [(i, i - i % side + (i - 1) % side) for i in range(4 * side)]
    gcorner, gright, gdown0, gdown1, share = lax.optimization_barrier((gcorner, gright, gdown0, gdown1, share))
    corner_back = shift(gcorner, "col", 1)
    down1_back = shift(gdown1, "row", 1)
    gdown0 = gdown0 + corner_back
    down0_back = shift(gdown0, "row", 1)
    right_back = shift(gright, "col", 1)
    share, down1_back = ring_sum_after(ring_sum(share, to_left_x), to_left_y, down1_back)
    right_back, share = lax.optimization_barrier((right_back, share))
    probe_grad = hand_out(share, "col").reshape(probe_wave.shape)
    return add_call(gown, right_back, down0_back, down1_back), probe_grad


def solution(mesh):
    return jax.shard_map(
        body,
        mesh=mesh,
        in_specs=(
            P(None, "row", "col"),
            P(),
            P(("row", "col"), None),
            P(("row", "col")),
            P(("row", "col"), None, None),
        ),
        out_specs=(P(None, "row", "col"), P()),
        check_vma=False,
    )
```

```python
import functools
import math

import jax
import jax.numpy as jnp
import ml_dtypes
import numpy as np
from jax import lax
from jax.experimental import pallas as pl
from jax.experimental.pallas import tpu as pltpu
from jax.sharding import PartitionSpec as P

W = 256
HALF_W = 128
TC = 512
EXT = TC + W
SLOTS = 8
GROUP = 4
PREPARED = 2
ADDED = 2
CHUNK = 32
F32 = jnp.float32
BF16 = jnp.bfloat16

RE, IM, NEG_IM = 0, 1, 2


def split_host(table):
    high = table.astype(np.float32).astype(ml_dtypes.bfloat16)
    low = (table - high.astype(np.float64)).astype(np.float32).astype(ml_dtypes.bfloat16)
    return [high, low]


def hop_tables():
    index = np.arange(W)
    dft = np.exp(-2j * np.pi / W * (index[:, None] * index[None, :] % W)) / math.sqrt(W)
    freqs = np.where(index < W // 2, index, index - W) / W
    fresnel = np.exp(-1j * np.pi * (W / 4.0) * freqs**2)
    hop = np.conj(dft) @ (fresnel[:, None] * dft)
    hop = hop * np.exp(1j * np.pi * index / W)
    out = []
    for table in (hop, hop.T):
        for part in (table.real, table.imag, -table.imag):
            out.extend(split_host(part))
    return np.stack(out)


def dft_tables():
    index = np.arange(W)
    angles = 2.0 * np.pi / W * (index[:, None] + 0.5) * (index[None, :HALF_W] + 0.5)
    table = np.concatenate([np.cos(angles), np.sin(angles)], axis=1) / math.sqrt(W)
    return np.stack(split_host(table) + split_host(table.T))


def fold_tables():
    source = np.concatenate([np.arange(HALF_W), np.arange(W - 1, HALF_W - 1, -1)])
    table = np.zeros((W, W), np.float32)
    table[source, np.arange(W)] = 1.0
    return np.stack([table, table.T]).astype(ml_dtypes.bfloat16)


def split(x):
    high = x.astype(BF16)
    return high, (x - high.astype(F32)).astype(BF16)


def lanes(*parts):
    return jnp.concatenate(parts, axis=1)


def rows(*parts):
    return jnp.concatenate(parts, axis=0)


def dot(a, b):
    return jnp.dot(a, b, preferred_element_type=F32)


def half_right(field, tab, at):
    high, low = tab[2 * at], tab[2 * at + 1]
    rh, rl = split(field[0])
    ih, il = split(field[1])
    out = dot(rows(lanes(rh, rl, rh), lanes(ih, il, ih)), rows(high, high, low))
    return out[:W], out[W:]


def half_left(field, tab, at):
    high, low = tab[2 * at], tab[2 * at + 1]
    rh, rl = split(field[0])
    ih, il = split(field[1])
    out = dot(lanes(high, high, low), lanes(rows(rh, rl, rh), rows(ih, il, ih)))
    return out[:, :W], out[:, W:]


def hop_parts(tab, at, conj):
    im, neg = (IM, NEG_IM) if not conj else (NEG_IM, IM)

    def three(a, b):
        a, b = 2 * (3 * at + a), 2 * (3 * at + b)
        return [tab[a], tab[b], tab[a], tab[b], tab[a + 1], tab[b + 1]]

    return three(RE, neg), three(im, RE)


def hop_right(field, tab, at, conj):
    rh, rl = split(field[0])
    ih, il = split(field[1])
    to_re, to_im = hop_parts(tab, at, conj)
    out = dot(lanes(rh, ih, rl, il, rh, ih), lanes(rows(*to_re), rows(*to_im)))
    return out[:, :W], out[:, W:]


def hop_left(field, tab, at, conj):
    rh, rl = split(field[0])
    ih, il = split(field[1])
    to_re, to_im = hop_parts(tab, at, conj)
    out = dot(rows(lanes(*to_re), lanes(*to_im)), rows(rh, ih, rl, il, rh, ih))
    return out[:W], out[W:]


def spread_right(field):
    c, s = field[0][:, :HALF_W], field[0][:, HALF_W:]
    d, t = field[1][:, :HALF_W], field[1][:, HALF_W:]
    return lanes(c + t, t - c), lanes(d - s, -d - s)


def spread_left(field):
    c, s = field[0][:HALF_W], field[0][HALF_W:]
    d, t = field[1][:HALF_W], field[1][HALF_W:]
    return rows(c + t, t - c), rows(d - s, -d - s)


def gather_right(field):
    a, b = field[0][:, :HALF_W], field[0][:, HALF_W:]
    c, d = field[1][:, :HALF_W], field[1][:, HALF_W:]
    return lanes(a - b, -c - d), lanes(c - d, a + b)


def gather_left(field):
    a, b = field[0][:HALF_W], field[0][HALF_W:]
    c, d = field[1][:HALF_W], field[1][HALF_W:]
    return rows(a - b, -c - d), rows(c - d, a + b)


def times(a, b):
    return a[0] * b[0] - a[1] * b[1], a[0] * b[1] + a[1] * b[0]


def conj_times(a, b):
    return a[0] * b[0] + a[1] * b[1], a[0] * b[1] - a[1] * b[0]


def pair(ref, *at):
    return ref[(*at, 0)], ref[(*at, 1)]


def put(value, ref, *at):
    ref[(*at, 0)], ref[(*at, 1)] = value


def chunks(body):
    def step(i, carry):
        body(pl.multiple_of(i * CHUNK, CHUNK))
        return carry

    lax.fori_loop(0, W // CHUNK, step, 0)


def geometry(meta, slot):
    row, col = meta[1 + slot], meta[1 + SLOTS + slot]
    block = col // W
    first = pl.multiple_of(block * W, W)
    second = pl.multiple_of(block * W + W, W)
    return row, col - block * W, first, second


def masks(row, col, at):
    in_top = lax.broadcasted_iota(jnp.int32, (CHUNK, W), 0) + at >= row
    in_first = lax.broadcasted_iota(jnp.int32, (CHUNK, W), 1) >= col
    return in_top, in_first


def load_window(meta, slot, ext, planes, win, u):
    row, col, first, second = geometry(meta, slot)
    border = row // CHUNK

    def load(i, carry):
        here = pl.ds(pl.multiple_of(i * CHUNK, CHUNK), CHUNK)
        _, in_first = masks(row, col, 0)
        low = (i < border).astype(jnp.int32)
        for p in planes:
            win[u, p, here, :] = jnp.where(
                in_first, ext[low, p, here, pl.ds(first, W)], ext[low, p, here, pl.ds(second, W)]
            )
        return carry

    lax.fori_loop(0, W // CHUNK, load, 0, unroll=True)
    at = pl.multiple_of(border * CHUNK, CHUNK)
    here = pl.ds(at, CHUNK)
    in_top, in_first = masks(row, col, at)
    for p in planes:
        low = jnp.where(in_first, ext[1, p, here, pl.ds(first, W)], ext[1, p, here, pl.ds(second, W)])
        win[u, p, here, :] = jnp.where(in_top, win[u, p, here, :], low)


def add_window(meta, slot, win, u, planes, gext):
    row, col, first, second = geometry(meta, slot)
    border = row // CHUNK
    zero = jnp.zeros((CHUNK, W), F32)
    alive = slot < meta[0]

    def add(i, carry):
        at = pl.multiple_of(i * CHUNK, CHUNK)
        here = pl.ds(at, CHUNK)
        in_top, in_first = masks(row, col, at)
        low = (i < border).astype(jnp.int32)
        keep = jnp.logical_and(jnp.logical_or(in_top, i < border), alive)
        for p in planes:
            value = jnp.where(keep, win[u, p, here, :], zero)
            gext[low, p, here, pl.ds(first, W)] += jnp.where(in_first, value, zero)
            gext[low, p, here, pl.ds(second, W)] += jnp.where(in_first, zero, value)
        return carry

    lax.fori_loop(0, W // CHUNK, add, 0, unroll=True)
    at = pl.multiple_of(border * CHUNK, CHUNK)
    here = pl.ds(at, CHUNK)
    in_top, in_first = masks(row, col, at)
    for p in planes:
        value = jnp.where(jnp.logical_and(jnp.logical_not(in_top), alive), win[u, p, here, :], zero)
        gext[1, p, here, pl.ds(first, W)] += jnp.where(in_first, value, zero)
        gext[1, p, here, pl.ds(second, W)] += jnp.where(in_first, zero, value)


def turn_probe(meta, slot, twice, turned, u):
    row, col, _, _ = geometry(meta, slot)
    for p in range(2):
        here = pl.ds(W - row, W)
        turned[u, p] = pltpu.roll(lanes(twice[p, 0, here, :], twice[p, 1, here, :]), col, 1)


def add_probe(meta, slot, part, u, acc):
    row, col, _, _ = geometry(meta, slot)
    for p in range(2):
        here = pl.ds(W - row, W)
        value = jnp.where(slot < meta[0], pltpu.roll(part[u, p], W - col, 1), 0.0)
        acc[p, 0, here, :] += value[:, :HALF_W]
        acc[p, 1, here, :] += value[:, HALF_W:]


def tile_copies(refs, ext, sems):
    own, right, down0, down1, corner = refs
    return [
        (own, ext.at[0, :, :, pl.ds(0, TC)], sems.at[0]),
        (right, ext.at[0, :, :, pl.ds(TC, W)], sems.at[1]),
        (down0, ext.at[1, :, :, pl.ds(0, W)], sems.at[2]),
        (down1, ext.at[1, :, :, pl.ds(W, W)], sems.at[3]),
        (corner, ext.at[1, :, :, pl.ds(TC, W)], sems.at[4]),
    ]


def start_copies(copies):
    copies = [pltpu.make_async_copy(*copy) for copy in copies]
    for copy in copies:
        copy.start()
    return copies


def wait_copies(copies):
    for copy in copies:
        copy.wait()


def prepare_kernel(meta, probe, amp, fold, amp_out, turned, twice):
    step = pl.program_id(0)

    def fold_amplitudes(u):
        high = amp[u].astype(BF16)
        rest = amp[u] - high.astype(F32)
        mid = rest.astype(BF16)
        low = (rest - mid.astype(F32)).astype(BF16)
        right_way = dot(rows(high, mid, low), fold[0])
        out = dot(fold[1], lanes(*(right_way[i * W : (i + 1) * W].astype(BF16) for i in range(3))))
        amp_out[u] = out[:, :W] + out[:, W : 2 * W] + out[:, 2 * W :]

    @pl.when(step == 0)
    def double_probe():
        for p in range(2):
            for half in range(2):
                part = probe[p, :, half * HALF_W : (half + 1) * HALF_W]
                twice[p, half, :W, :] = part
                twice[p, half, W:, :] = part

    for u in range(PREPARED):
        fold_amplitudes(u)
        turn_probe(meta, step * PREPARED + u, twice, turned, u)


def first_kernel(start, meta, own, right, down0, down1, corner, turned_in, hop_in, prop, ext, turned, hop, win, sems):
    @pl.when(start < meta[0])
    def work():
        one, group = pl.ds(0, 2), pl.ds(start, GROUP)
        refs = (own.at[one], right.at[one], down0, down1, corner)
        started = start_copies(tile_copies(refs, ext, sems))
        rest = start_copies([(turned_in.at[group], turned, sems.at[5]), (hop_in, hop, sems.at[6])])
        wait_copies(started)
        for u in range(GROUP):
            load_window(meta, start + u, ext, (0, 1), win, u)
        wait_copies(rest)
        fields = [times(pair(turned, u), pair(win, u)) for u in range(GROUP)]
        fields = [hop_right(f, hop, 0, False) for f in fields]
        fields = [hop_left(f, hop, 1, False) for f in fields]
        for u, f in enumerate(fields):
            put(f, prop, u)


def second_kernel(meta, own, right, down0_one, down0_two, down1_one, corner_one, turned_in, hop_in, prop_now, prop_later, amp_in,
                  down1_two, corner_two, dft, gprobe, win,
                  ext, acc, turned, hop, prop, amp, sems):
    step = pl.program_id(0)
    group = range(GROUP)
    one, two = pl.ds(0, 2), pl.ds(2, 2)
    refs_one = (own.at[one], right.at[one], down0_one, down1_one, corner_one)
    refs_two = (own.at[two], right.at[two], down0_two, down1_two, corner_two)
    copies_one = tile_copies(refs_one, ext.at[:, one], sems.at[0])
    copies_two = tile_copies(refs_two, ext.at[:, two], sems.at[1])
    now, later = pl.ds(0, GROUP), pl.ds(GROUP, SLOTS - GROUP)
    copies_now = copies_two + [
        (prop_now, prop.at[now], sems.at[2, 0]),
        (amp_in.at[now], amp.at[now], sems.at[2, 1]),
    ]
    copies_later = [(hop_in, hop, sems.at[2, 2])] + copies_one + [
        (turned_in, turned, sems.at[2, 3]),
        (prop_later, prop.at[later], sems.at[2, 4]),
        (amp_in.at[later], amp.at[later], sems.at[2, 5]),
    ]

    @pl.when(step == 0)
    def begin():
        started = start_copies(copies_now)
        start_copies(copies_later)
        acc[...] = jnp.zeros_like(acc)
        wait_copies(started)

    live = step * GROUP < meta[0]

    @pl.when(live)
    def stage_one():
        for u in group:
            load_window(meta, step * GROUP + u, ext, (2, 3), win, u)
        fields = [times(pair(prop, step * GROUP + u), (win[u, 2], win[u, 3])) for u in group]
        fields = [spread_left(half_left(f, dft, 1)) for f in fields]
        fields = [spread_right(half_right(f, dft, 0)) for f in fields]
        chi = []
        for u, f in enumerate(fields):
            factor = 1.0 - amp[step * GROUP + u] * lax.rsqrt(f[0] * f[0] + f[1] * f[1] + 1.0)
            chi.append((factor * f[0], factor * f[1]))
        fields = [half_right(gather_right(f), dft, 1) for f in chi]
        fields = [half_left(gather_left(f), dft, 0) for f in fields]
        waves = [conj_times((win[u, 2], win[u, 3]), f) for u, f in enumerate(fields)]
        for u, f in enumerate(fields):
            win[u, 2], win[u, 3] = conj_times(pair(prop, step * GROUP + u), f)
        for u, f in enumerate(waves):
            put(f, prop, step * GROUP + u)

    @pl.when(step == 0)
    def arrive():
        wait_copies([pltpu.make_async_copy(*copy) for copy in copies_later])

    @pl.when(live)
    def stage_two():
        for u in group:
            load_window(meta, step * GROUP + u, ext, (0, 1), win, u)
        waves = [hop_left(pair(prop, step * GROUP + u), hop, 0, True) for u in group]
        waves = [hop_right(f, hop, 1, True) for f in waves]
        for u, wave in enumerate(waves):
            probe = pair(turned, step * GROUP + u)
            grad, part = conj_times(probe, wave), conj_times(pair(win, u), wave)
            put(grad, win, u)
            put(part, prop, step * GROUP + u)

        def finish(slot, u):
            add_probe(meta, slot, prop, slot, acc)

        for u in group:
            slot = step * GROUP + u
            finish(slot, u)

    @pl.when(step == SLOTS // GROUP - 1)
    def end():
        for p in range(2):
            gprobe[p] = lanes(acc[p, 0, :W, :] + acc[p, 0, W:, :], acc[p, 1, :W, :] + acc[p, 1, W:, :])


def third_kernel(meta, grads, gown, gright, gdown0, gdown1, gcorner, gext, sems):
    step = pl.program_id(0)

    @pl.when(step == 0)
    def begin():
        gext[...] = jnp.zeros_like(gext)

    for u in range(ADDED):
        slot = step * ADDED + u
        pl.when(slot < meta[0])(lambda: add_window(meta, slot, grads, u, range(4), gext))

    @pl.when(step == SLOTS // ADDED - 1)
    def end():
        wait_copies(start_copies([
            (gext.at[1, :, :, pl.ds(W, W)], gdown1, sems.at[0]),
            (gext.at[1, :, :, pl.ds(TC, W)], gcorner, sems.at[1]),
            (gext.at[1, :, :, pl.ds(0, W)], gdown0, sems.at[2]),
            (gext.at[0, :, :, pl.ds(TC, W)], gright, sems.at[3]),
            (gext.at[0, :, :, pl.ds(0, TC)], gown, sems.at[4]),
        ]))


ANYWHERE = pl.BlockSpec(memory_space=pl.ANY)
WHOLE = pl.BlockSpec(memory_space=pltpu.VMEM)
SCALARS = pl.BlockSpec(memory_space=pltpu.SMEM)
FIELDS = pl.BlockSpec((GROUP, 2, W, W), lambda i: (i, 0, 0, 0))
PLANES = pl.BlockSpec((GROUP, W, W), lambda i: (i, 0, 0))


def shape(*dims):
    return jax.ShapeDtypeStruct(dims, F32)


FIELDS_SHAPE = shape(SLOTS, 2, W, W)


def call(kernel, steps, in_specs, out_specs, out_shape, scratch, products, mebibytes):
    return pl.pallas_call(
        kernel,
        grid=(steps,),
        in_specs=in_specs,
        out_specs=out_specs,
        out_shape=out_shape,
        scratch_shapes=scratch,
        compiler_params=pltpu.CompilerParams(
            vmem_limit_bytes=mebibytes * 2**20, dimension_semantics=("arbitrary",)
        ),
        cost_estimate=pl.CostEstimate(
            flops=SLOTS * products * 2 * W**3, bytes_accessed=products * 2**18, transcendentals=0
        ),
    )


def prepare_call(*args):
    return call(
        prepare_kernel,
        SLOTS // PREPARED,
        [SCALARS, WHOLE, pl.BlockSpec((PREPARED, W, W), lambda i: (i, 0, 0)), WHOLE],
        [
            pl.BlockSpec((PREPARED, W, W), lambda i: (i, 0, 0)),
            pl.BlockSpec((PREPARED, 2, W, W), lambda i: (i, 0, 0, 0)),
        ],
        [shape(SLOTS, W, W), FIELDS_SHAPE],
        [pltpu.VMEM((2, 2, 2 * W, HALF_W), F32)],
        0,
        16,
    )(*args)


def first_call(start, products, *args):
    return call(
        functools.partial(first_kernel, start),
        1,
        [SCALARS] + [ANYWHERE] * 3 + [WHOLE, WHOLE] + [ANYWHERE] * 2,
        pl.BlockSpec((GROUP, 2, W, W), lambda i: (0, 0, 0, 0)),
        shape(GROUP, 2, W, W),
        [
            pltpu.VMEM((2, 2, W, EXT), F32),
            pltpu.VMEM((GROUP, 2, W, W), F32),
            pltpu.VMEM((12, W, W), BF16),
            pltpu.VMEM((GROUP, 2, W, W), F32),
            pltpu.SemaphoreType.DMA((7,)),
        ],
        products,
        52,
    )(*args)


def second_call(*args):
    return call(
        second_kernel,
        SLOTS // GROUP,
        [SCALARS] + [ANYWHERE] * 11 + [WHOLE] * 3,
        [WHOLE, pl.BlockSpec((GROUP, 4, W, W), lambda i: (i, 0, 0, 0))],
        [shape(2, W, W), shape(SLOTS, 4, W, W)],
        [
            pltpu.VMEM((2, 4, W, EXT), F32),
            pltpu.VMEM((2, 2, 2 * W, HALF_W), F32),
            pltpu.VMEM((SLOTS, 2, W, W), F32),
            pltpu.VMEM((12, W, W), BF16),
            pltpu.VMEM((SLOTS, 2, W, W), F32),
            pltpu.VMEM((SLOTS, W, W), F32),
            pltpu.SemaphoreType.DMA((3, 6)),
        ],
        48,
        54,
    )(*args)


def third_call(*args):
    return call(
        third_kernel,
        SLOTS // ADDED,
        [SCALARS, pl.BlockSpec((ADDED, 4, W, W), lambda i: (i, 0, 0, 0))],
        [ANYWHERE] * 5,
        [shape(4, W, TC)] + [shape(4, W, W)] * 4,
        [pltpu.VMEM((2, 4, W, EXT), F32), pltpu.SemaphoreType.DMA((5,))],
        24,
        40,
    )(*args)


def add_kernel(base, right, down0, down1, out):
    first, second = pl.ds(0, W), pl.ds(W, W)
    out[:, :, first] = base[:, :, first] + (right[...] + down0[...])
    out[:, :, second] = base[:, :, second] + down1[...]


def add_call(*args):
    whole = pl.BlockSpec((1, W, TC), lambda i: (i, 0, 0))
    part = pl.BlockSpec((1, W, W), lambda i: (i, 0, 0))
    return pl.pallas_call(
        add_kernel,
        grid=(4,),
        in_specs=[whole] + [part] * 3,
        out_specs=whole,
        out_shape=shape(4, W, TC),
        compiler_params=pltpu.CompilerParams(vmem_limit_bytes=8 * 2**20),
        cost_estimate=pl.CostEstimate(flops=2**20, bytes_accessed=7 * 2**20, transcendentals=0),
    )(*args)


def shift(value, axis, steps):
    count = lax.axis_size(axis)
    first, last = (max(0, -steps), min(count, count - steps))
    return lax.ppermute(value, axis, [(source, source + steps) for source in range(first, last)])


def add_shares(value, axis):
    count = lax.axis_size(axis)
    shares = value.reshape(count, -1, value.shape[-1])
    return lax.all_to_all(shares, axis, 0, 0, tiled=True).sum(axis=0)


def hand_out(value, axis):
    spread = jnp.broadcast_to(value[None], (lax.axis_size(axis), *value.shape))
    return lax.all_to_all(spread, axis, 0, 0, tiled=True)


def ring_sum(value, pairs):
    first = lax.ppermute(value, "row", pairs)
    second = lax.ppermute(first, "row", pairs)
    third = lax.ppermute(second, "row", pairs)
    return (value + second) + (first + third)


def ring_sum_after(value, pairs, arrived):
    first = lax.ppermute(value, "row", pairs)
    second = lax.ppermute(first, "row", pairs)
    second, arrived = lax.optimization_barrier((second, arrived))
    third = lax.ppermute(second, "row", pairs)
    return (value + second) + (first + third), arrived


def body(object_slab, probe_wave, scan_offsets, live_counts, amplitudes):
    rows_tile, cols_tile = object_slab.shape[1:]
    local_rows = scan_offsets[:, 0] - lax.axis_index("row") * rows_tile
    local_cols = scan_offsets[:, 1] - lax.axis_index("col") * cols_tile
    meta = jnp.concatenate([live_counts, local_rows, local_cols])
    hop, dft, fold = jnp.asarray(hop_tables()), jnp.asarray(dft_tables()), jnp.asarray(fold_tables())
    first_part, rest = lax.optimization_barrier((object_slab[:2, :, :W], object_slab))
    down0_one = shift(first_part, "row", -1)
    down1_one = shift(rest[:2, :, W:], "row", -1)
    right = shift(rest[:, :, :W], "col", -1)
    down0_two = shift(rest[2:, :, :W], "row", -1)
    amp, turned = prepare_call(meta, probe_wave, amplitudes, fold)
    down0_one, turned, last_part = lax.optimization_barrier((down0_one, turned, rest[2:, :, W:]))
    corner_one = shift(down0_one, "col", -1)
    down1_two = shift(last_part, "row", -1)
    near = (meta, object_slab, right, down0_one, down1_one, corner_one, turned, hop)
    prop_now = first_call(0, 12, *near)
    down0_two, prop_now, near = lax.optimization_barrier((down0_two, prop_now, near))
    corner_two = shift(down0_two, "col", -1)
    prop_later = first_call(GROUP, 0, *near)
    gprobe, grads = second_call(
        meta, object_slab, right, down0_one, down0_two, down1_one, corner_one, turned, hop, prop_now, prop_later, amp,
        down1_two, corner_two, dft,
    )
    share = add_shares(gprobe, "col")
    gown, gright, gdown0, gdown1, gcorner = third_call(meta, grads)
    side = lax.axis_size("row") // 4
    to_left_x = [(i, (i - side) % (4 * side)) for i in range(4 * side)]
    to_left_y = [(i, i - i % side + (i - 1) % side) for i in range(4 * side)]
    gcorner, gright, gdown0, gdown1, share = lax.optimization_barrier((gcorner, gright, gdown0, gdown1, share))
    corner_back = shift(gcorner, "col", 1)
    down1_back = shift(gdown1, "row", 1)
    gdown0 = gdown0 + corner_back
    down0_back = shift(gdown0, "row", 1)
    right_back = shift(gright, "col", 1)
    share, down1_back = ring_sum_after(ring_sum(share, to_left_x), to_left_y, down1_back)
    right_back, share = lax.optimization_barrier((right_back, share))
    probe_grad = hand_out(share, "col").reshape(probe_wave.shape)
    return add_call(gown, right_back, down0_back, down1_back), probe_grad


def solution(mesh):
    return jax.shard_map(
        body,
        mesh=mesh,
        in_specs=(
            P(None, "row", "col"),
            P(),
            P(("row", "col"), None),
            P(("row", "col")),
            P(("row", "col"), None, None),
        ),
        out_specs=(P(None, "row", "col"), P()),
        check_vma=False,
    )
```
